32 devices in a mesh: dp: 8 (over y, x, core), tensor: 4 (over z).
Axes of the slice: x: 2, y: 2, z: 4, core: 2. Of those that a mesh axis runs over, the one named last changes fastest.
Arguments:
- tokens: bfloat16 [16384, 2048], P('dp'), may hold values from -6 to 6
- segments: int32 [16384], P('dp'), may hold values from 0 to 10, as said below
- positions: int32 [16384], P('dp'), may hold values from 0 to 4046, as said below
- ln1_gain: float32 [2048], replicated, may hold values from 0.25 to 1.75
- ln1_bias: float32 [2048], replicated, may hold values from -2 to 2
- ln2_gain: float32 [2048], replicated, may hold values from 0.25 to 1.75
- ln2_bias: float32 [2048], replicated, may hold values from -2 to 2
- qkv_weight: bfloat16 [2048, 6144], P(None, 'tensor'), may hold values from -0.125 to 0.125
- dense_weight: bfloat16 [2048, 2048], P('tensor'), may hold values from -1 to 1
- fc1_weight: bfloat16 [2048, 8192], P(None, 'tensor'), may hold values from -0.125 to 0.125
- fc2_weight: bfloat16 [8192, 2048], P('tensor'), may hold values from -0.0625 to 0.0625
- upstream: bfloat16 [16384, 2048], P('dp', 'tensor'), may hold values from -6 to 6
Outputs:
- output: bfloat16 [16384, 2048], P('dp', 'tensor')
- input_grad: float32 [16384, 2048], P('dp')
- qkv_grad: float32 [2048, 6144], P('dp', 'tensor')
- dense_grad: float32 [2048, 2048], P('tensor', 'dp')
- fc1_grad: float32 [2048, 8192], P('dp', 'tensor')
- fc2_grad: float32 [8192, 2048], P('tensor', 'dp')
- ln1_gain_grad: float32 [2048], P('dp')
- ln1_bias_grad: float32 [2048], P('dp')
- ln2_gain_grad: float32 [2048], P('dp')
- ln2_bias_grad: float32 [2048], P('dp')
The draws below stay inside these ranges and needn't reach their ends.
Inputs may be any that keep to these rules, and one draw needn't show every extreme that they name: `segments`: within each sequence of 2048 tokens the numbers start at 0 and rise by one at each document's start; a document holds 200 to 2000 tokens, the last one of a sequence may be cut shorter. `positions`: A token's place in its document plus an offset below 2048 drawn for that document.
All inputs are finite; a program needn't handle non-finite values.
Results may differ from the reference program's by a relative error of at most 0.012.
Values may be sent and summed in bfloat16 or wider, within the bound.
A program may use at most 384 MiB of HBM per device.

```python
import jax
import jax.numpy as jnp
from jax import lax

D = 2048
HEADS = 8
HEAD_DIM = 256
ROT_DIM = 64
FF = 8192
SEQ_LEN = 2048
SEQUENCES = 8
TOKENS = 16384


def document_layout(key):
    short_len = SEQ_LEN * 100 // 1024
    long_len = SEQ_LEN * 1000 // 1024
    doc_count = SEQ_LEN // short_len + 1
    length_key = jax.random.fold_in(key, 5)
    pick_key = jax.random.fold_in(key, 7)
    lengths = jax.random.randint(length_key, (SEQUENCES, doc_count), short_len, long_len + 1, dtype=jnp.int32)
    chosen = jax.random.randint(pick_key, (), 0, SEQUENCES, dtype=jnp.int32)
    second = (chosen + 1) % SEQUENCES
    rows = jnp.arange(SEQUENCES, dtype=jnp.int32)
    columns = jnp.arange(doc_count, dtype=jnp.int32)
    lengths = jnp.where((rows == chosen)[:, None], short_len, lengths)
    first_long = (rows == second)[:, None] & (columns == 0)[None, :]
    lengths = jnp.where(first_long, long_len, lengths)
    ends = jnp.cumsum(lengths, axis=1)
    starts = ends - lengths
    places = jnp.arange(SEQ_LEN, dtype=jnp.int32)
    doc_ids = jnp.sum((places[None, :, None] >= ends[:, None, :]).astype(jnp.int32), axis=2)
    picked = doc_ids[:, :, None] == columns[None, None, :]
    return (doc_ids, places, starts, picked, first_long)


def draw_segments(key, part):
    doc_ids, places, starts, picked, first_long = document_layout(key)
    return doc_ids.reshape(-1)


def draw_positions(key, part):
    doc_ids, places, starts, picked, first_long = document_layout(key)
    key = jax.random.fold_in(key, 11)
    offsets = jax.random.randint(key, starts.shape, 0, SEQ_LEN, dtype=jnp.int32)
    offsets = jnp.where(first_long, SEQ_LEN - 1, offsets)
    shifted = offsets - starts
    moved = jnp.sum(jnp.where(picked, shifted[:, None, :], 0), axis=2)
    return (places[None, :] + moved).reshape(-1)


def spiked(array, own_key, source, target, shards_of, factor):
    def block_of(axis_at):
        return (jnp.arange(array.shape[axis_at]) // (array.shape[axis_at] // shards_of)).reshape((-1,) + (1,) * (array.ndim - 1 - axis_at))

    first = jax.random.permutation(own_key, shards_of)[block_of(target)]
    other_side = (block_of(target) + shards_of // 2) % shards_of
    return jnp.where((block_of(source) == first) | (block_of(source) == other_side), factor * array, array)


def shard_levels(rng, dims, pieces, low, largest):
    def one(position, blocks):
        heights = jax.random.uniform(jax.random.fold_in(jax.random.fold_in(rng, 6), position), (blocks,), jnp.float32, low / len(pieces), largest / len(pieces))
        return jnp.repeat(jnp.exp(heights), dims[position] // blocks).reshape((-1,) + (1,) * (len(dims) - position - 1))

    level = one(*pieces[0])
    for cut in pieces[1:]:
        level = level * one(*cut)
    return level


def bell_draw(rng, extent, scale, reach, shards=(), kind=jnp.bfloat16):
    array = jax.random.normal(rng, extent, jnp.float32) * scale
    if len(shards) > 0:
        array = shard_levels(rng, extent, shards, -0.22, 0.18) * array
    return jnp.clip(array, min=-reach, max=reach).astype(kind)


def heavy_noise(key, shape, width, limit, pieces, heavy, kind=jnp.bfloat16):
    entries = width * jax.random.normal(key, shape, jnp.float32)
    if pieces:
        entries = entries * shard_levels(key, shape, pieces, -0.22, 0.18)
    return jnp.clip(spiked(entries, jax.random.fold_in(key, 3), *heavy), -limit, limit).astype(kind)


def setup_inputs(seed: int = 0) -> dict:
    keys = jax.random.split(jax.random.key(seed), 13)
    return {
        "tokens": heavy_noise(keys[0], (TOKENS, D), 1.0, 6.0, ((0, 8),), (0, 1, 8, 2.0)),
        "segments": draw_segments(jax.random.fold_in(keys[12], 71), 0),
        "positions": draw_positions(jax.random.fold_in(keys[12], 71), 0),
        "ln1_gain": jnp.clip(1.0 + 0.15 * jax.random.normal(keys[3], (D,), jnp.float32), 0.25, 1.75),
        "ln1_bias": bell_draw(keys[4], (D,), 0.3, 2.0, (), jnp.float32),
        "ln2_gain": jnp.clip(1.0 + 0.15 * jax.random.normal(keys[5], (D,), jnp.float32), 0.25, 1.75),
        "ln2_bias": bell_draw(keys[6], (D,), 0.3, 2.0, (), jnp.float32),
        "qkv_weight": bell_draw(keys[7], (D, 3 * D), D ** -0.5, 0.125, ((1, 4),)),
        "dense_weight": bell_draw(keys[8], (D, D), (D // 64) ** -0.5, 1.0, ((0, 4),)),
        "fc1_weight": bell_draw(keys[9], (D, FF), D ** -0.5, 0.125, ((1, 4),)),
        "fc2_weight": bell_draw(keys[10], (FF, D), FF ** -0.5, 0.0625, ((0, 4),)),
        "upstream": heavy_noise(keys[11], (TOKENS, D), 1.0, 6.0, ((0, 8), (1, 4)), (0, 1, 8, 2.0)),
    }


@jax.custom_vjp
def low(v):
    return lax.optimization_barrier(v.astype(jnp.bfloat16)).astype(jnp.float32)

@jax.custom_vjp
def low_back(v):
    return v

def low_keep(v):
    return (low(v), None)

def low_pass(kept, grad):
    return (grad,)

def back_keep(v):
    return (v, None)

def back_low(kept, grad):
    return (low(grad),)
low.defvjp(low_keep, low_pass)
low_back.defvjp(back_keep, back_low)

def layer_norm(values, gain, bias):
    center = values - lax.optimization_barrier(jnp.mean(values, axis=-1, keepdims=True))
    spread = lax.optimization_barrier(jnp.mean(center * center, axis=-1, keepdims=True))
    return center * lax.rsqrt(spread + 1e-05) * gain + bias

def tables(positions):
    half = ROT_DIM // 2
    steps_up = jnp.arange(half).astype(jnp.float32) * 2.0 / ROT_DIM
    inverse = jnp.power(jnp.float32(10000.0), -steps_up)
    angle = positions.astype(jnp.float32)[:, None] * inverse[None, :]
    return (jnp.concatenate([jnp.cos(angle), jnp.cos(angle)], -1), jnp.concatenate([jnp.sin(angle), jnp.sin(angle)], -1))

def rotate(values, cos_rows, sin_rows):
    half = ROT_DIM // 2
    front = values[..., :ROT_DIM]
    turned = jnp.concatenate([-front[..., half:], front[..., :half]], -1)
    return jnp.concatenate([front * cos_rows + turned * sin_rows, values[..., ROT_DIM:]], -1)

def exact_gelu(values):
    return jax.nn.gelu(values, approximate=False)

def reference(tokens, segments, positions, ln1_gain, ln1_bias, ln2_gain, ln2_bias, qkv_weight, dense_weight, fc1_weight, fc2_weight, upstream):
    highest = lax.Precision.HIGHEST
    score_scale = HEAD_DIM ** (-0.5)
    doc_rows = segments.reshape(SEQUENCES, SEQ_LEN)
    cos_all, sin_all = tables(positions)
    cos_rows = cos_all.reshape(SEQUENCES, SEQ_LEN, 1, ROT_DIM)
    sin_rows = sin_all.reshape(SEQUENCES, SEQ_LEN, 1, ROT_DIM)
    places = jnp.arange(SEQ_LEN, dtype=jnp.int32)

    def attend(packed):
        query, key_rows, value_rows, docs = packed
        scores = jnp.einsum('qhd,khd->hqk', query, key_rows, precision=highest)
        scores = low_back(scores) * score_scale
        allowed = (docs[:, None] == docs[None, :]) & (places[:, None] >= places[None, :])
        scores = jnp.where(allowed[None], scores, -1e+30)
        weights = low(jax.nn.softmax(scores, axis=-1))
        attended = jnp.einsum('hqk,khd->qhd', weights, value_rows, precision=highest)
        return low(low_back(attended))

    def forward(inputs, gain_one, bias_one, gain_two, bias_two, w_qkv, w_dense, w_first, w_second):
        h_one = low(layer_norm(inputs, gain_one, bias_one))
        h_two = low(layer_norm(inputs, gain_two, bias_two))
        qkv = low_back(jnp.dot(h_one, w_qkv, precision=highest))
        parts = qkv.reshape(SEQUENCES, SEQ_LEN, HEADS, 3, HEAD_DIM)
        query = low(rotate(parts[:, :, :, 0], cos_rows, sin_rows))
        key_rows = low(rotate(parts[:, :, :, 1], cos_rows, sin_rows))
        value_rows = low(parts[:, :, :, 2])
        attended = lax.map(jax.checkpoint(attend), (query, key_rows, value_rows, doc_rows))
        attended = attended.reshape(TOKENS, D)
        pre_act = low_back(jnp.dot(h_two, w_first, precision=highest))
        hidden = low(exact_gelu(pre_act))
        total = jnp.dot(attended, w_dense, precision=highest) + jnp.dot(hidden, w_second, precision=highest)
        return inputs + total
    floats = (tokens.astype(jnp.float32), ln1_gain.astype(jnp.float32), ln1_bias.astype(jnp.float32), ln2_gain.astype(jnp.float32), ln2_bias.astype(jnp.float32), qkv_weight.astype(jnp.float32), dense_weight.astype(jnp.float32), fc1_weight.astype(jnp.float32), fc2_weight.astype(jnp.float32))
    result, pull = jax.vjp(forward, *floats)
    grads = pull(upstream.astype(jnp.float32))
    return (result.astype(jnp.bfloat16), grads[0], grads[5], grads[6], grads[7], grads[8], grads[1], grads[2], grads[3], grads[4])
```

```python
import functools

import jax
import jax.numpy as jnp
from jax import lax
from jax.experimental import pallas as pl
from jax.experimental.pallas import tpu as pltpu
from jax.sharding import PartitionSpec as P

AX = "tensor"
HEAD_DIM = 256
ROT_DIM = 64
SEQ_LEN = 2048
LANES = 128
VMEM_CAP = 60 * 2**20
NT = (((1,), (1,)), ((), ()))
TN = (((0,), (0,)), ((), ()))


def rot_tables(positions):
    half = ROT_DIM // 2
    steps_up = jnp.arange(half).astype(jnp.float32) * 2.0 / ROT_DIM
    inverse = jnp.power(jnp.float32(10000.0), -steps_up)
    angle = positions.astype(jnp.float32)[:, None] * inverse[None, :]
    cos, sin = jnp.cos(angle), jnp.sin(angle)
    zero = jnp.zeros_like(sin)
    rest = jnp.zeros((positions.shape[0], LANES - ROT_DIM), jnp.float32)
    cos_t = jnp.concatenate([cos, cos, rest + 1.0], -1)
    sin_up = jnp.concatenate([-sin, zero, rest], -1)
    sin_down = jnp.concatenate([zero, sin, rest], -1)
    return cos_t, sin_up, sin_down


def rotate_tile(u, cos_t, sin_up, sin_down):
    half = ROT_DIM // 2
    return u * cos_t + pltpu.roll(u, LANES - half, 1) * sin_up + pltpu.roll(u, half, 1) * sin_down


def rotate_back_tile(g, cos_t, sin_up, sin_down):
    half = ROT_DIM // 2
    return g * cos_t + pltpu.roll(g * sin_down, LANES - half, 1) + pltpu.roll(g * sin_up, half, 1)


def pre_kernel(x_ref, g1_ref, b1_ref, g2_ref, b2_ref, cos_ref, su_ref, sd_ref, w_ref, h1_ref, h2_ref, qkv_ref):
    x = x_ref[...].astype(jnp.float32)
    center = x - jnp.mean(x, axis=-1, keepdims=True)
    inv = lax.rsqrt(jnp.mean(center * center, axis=-1, keepdims=True) + 1e-05)
    normed = center * inv
    h1 = (normed * g1_ref[...] + b1_ref[...]).astype(jnp.bfloat16)
    h1_ref[...] = h1
    h2_ref[...] = (normed * g2_ref[...] + b2_ref[...]).astype(jnp.bfloat16)
    cos_t, su, sd = cos_ref[...], su_ref[...], sd_ref[...]
    for b in range(w_ref.shape[1] // HEAD_DIM):
        cols = slice(b * HEAD_DIM, (b + 1) * HEAD_DIM)
        y = jnp.dot(h1, w_ref[:, cols], preferred_element_type=jnp.float32)
        if b % 3 < 2:
            qkv_ref[:, b * HEAD_DIM : b * HEAD_DIM + LANES] = rotate_tile(y[:, :LANES], cos_t, su, sd).astype(jnp.bfloat16)
            qkv_ref[:, b * HEAD_DIM + LANES : (b + 1) * HEAD_DIM] = y[:, LANES:].astype(jnp.bfloat16)
        else:
            qkv_ref[:, cols] = y.astype(jnp.bfloat16)


def project(tokens, g1, b1, g2, b2, rot, w, rows=256):
    total, width = tokens.shape
    rows = min(rows, total)
    row_blk = lambda cols: pl.BlockSpec((rows, cols), lambda i: (i, 0))
    vec = pl.BlockSpec((1, width), lambda i: (0, 0))
    cols = w.shape[1]
    return pl.pallas_call(
        pre_kernel,
        grid=(total // rows,),
        in_specs=[row_blk(width), vec, vec, vec, vec, row_blk(LANES), row_blk(LANES), row_blk(LANES),
                  pl.BlockSpec((width, cols), lambda i: (0, 0), pipeline_mode=pl.Buffered(1))],
        out_specs=[row_blk(width), row_blk(width), row_blk(cols)],
        out_shape=[jax.ShapeDtypeStruct((total, width), jnp.bfloat16)] * 2 + [jax.ShapeDtypeStruct((total, cols), jnp.bfloat16)],
        compiler_params=pltpu.CompilerParams(vmem_limit_bytes=VMEM_CAP),
        cost_estimate=pl.CostEstimate(flops=2 * total * width * cols, bytes_accessed=6 * total * width + 2 * cols * (width + total), transcendentals=0),
        name="norm_project",
    )(tokens, g1[None], b1[None], g2[None], b2[None], *rot, w)


def attend_kernel(block, heads, qkv_ref, drow_ref, dcol_ref, o_ref, lse_ref, v_turned):
    i = pl.program_id(1)
    scale = HEAD_DIM ** (-0.5)
    part = lambda h, c: slice((3 * h + c) * HEAD_DIM, (3 * h + c + 1) * HEAD_DIM)

    @pl.when(i == 0)
    def _():
        for h in range(heads):
            v_turned[h] = qkv_ref[:, part(h, 2)].T

    here = pl.ds(pl.multiple_of(i * block, block), block)
    queries = [qkv_ref[here, part(h, 0)] for h in range(heads)]
    docs_q = drow_ref[...]
    gap = lax.broadcasted_iota(jnp.int32, (block, block), 1) - lax.broadcasted_iota(jnp.int32, (block, block), 0)

    def body(j, carry):
        rows = pl.ds(pl.multiple_of(j * block, block), block)
        allowed = (docs_q == dcol_ref[rows, :]) & (gap >= (j - i) * block)
        new = []
        for h in range(heads):
            m, l, acc = carry[h]
            s = lax.dot_general(qkv_ref[rows, part(h, 1)], queries[h], NT, preferred_element_type=jnp.float32) * scale
            s = jnp.where(allowed, s, -1e30)
            m_new = jnp.maximum(m, jnp.max(s, axis=0, keepdims=True))
            p = jnp.exp(s - m_new)
            alpha = jnp.exp(m - m_new)
            l = l * alpha + jnp.sum(p, axis=0, keepdims=True)
            acc = acc * alpha + jnp.dot(v_turned[h, :, rows], p.astype(jnp.bfloat16), preferred_element_type=jnp.float32)
            new.append((m_new, l, acc))
        return tuple(new)

    start = (jnp.full((1, block), -1e30, jnp.float32), jnp.zeros((1, block), jnp.float32), jnp.zeros((HEAD_DIM, block), jnp.float32))
    carry = lax.fori_loop(0, i + 1, body, (start,) * heads)
    for h in range(heads):
        m, l, acc = carry[h]
        o_ref[:, h * HEAD_DIM : (h + 1) * HEAD_DIM] = (acc * (1.0 / l)).T.astype(jnp.bfloat16)
        lse_ref[h] = m + jnp.log(l)


def attend(qkv, docs, block=512):
    total, cols = qkv.shape
    heads = cols // (3 * HEAD_DIM)
    seqs = total // SEQ_LEN
    n = SEQ_LEN // block
    return pl.pallas_call(
        functools.partial(attend_kernel, block, heads),
        grid=(seqs, n),
        in_specs=[
            pl.BlockSpec((SEQ_LEN, cols), lambda s, i: (s, 0)),
            pl.BlockSpec((1, block), lambda s, i: (0, s * n + i)),
            pl.BlockSpec((SEQ_LEN, 1), lambda s, i: (s, 0)),
        ],
        out_specs=[pl.BlockSpec((block, heads * HEAD_DIM), lambda s, i: (s * n + i, 0)),
                   pl.BlockSpec((heads, 1, block), lambda s, i: (0, 0, s * n + i))],
        out_shape=[jax.ShapeDtypeStruct((total, heads * HEAD_DIM), jnp.bfloat16), jax.ShapeDtypeStruct((heads, 1, total), jnp.float32)],
        scratch_shapes=[pltpu.VMEM((heads, HEAD_DIM, SEQ_LEN), jnp.bfloat16)],
        compiler_params=pltpu.CompilerParams(vmem_limit_bytes=VMEM_CAP),
        cost_estimate=pl.CostEstimate(flops=2 * total * SEQ_LEN * heads * HEAD_DIM, bytes_accessed=4 * total * cols, transcendentals=total * SEQ_LEN),
        name="attend",
    )(qkv, docs[None, :], docs[:, None])


def attend_back_kernel(block, n, heads, qkv_ref, g_ref, o_ref, dcol_ref, drow_ref, lse_ref, cos_ref, su_ref, sd_ref, out_ref, dk, dv):
    i = pl.program_id(1)
    scale = HEAD_DIM ** (-0.5)
    part = lambda h, c: slice((3 * h + c) * HEAD_DIM, (3 * h + c + 1) * HEAD_DIM)
    cols = lambda h: slice(h * HEAD_DIM, (h + 1) * HEAD_DIM)

    @pl.when(i == 0)
    def _():
        dk[...] = jnp.zeros_like(dk)
        dv[...] = jnp.zeros_like(dv)

    here = pl.ds(pl.multiple_of(i * block, block), block)
    docs_q = drow_ref[...]
    ones = jnp.ones((8, HEAD_DIM), jnp.float32)
    queries = [qkv_ref[here, part(h, 0)] for h in range(heads)]
    grads = [g_ref[:, cols(h)] for h in range(heads)]
    deltas = [
        lax.dot_general(ones, grads[h].astype(jnp.float32) * o_ref[:, cols(h)].astype(jnp.float32), NT,
                        precision=lax.Precision.HIGHEST, preferred_element_type=jnp.float32)[:1]
        for h in range(heads)
    ]
    gap = lax.broadcasted_iota(jnp.int32, (block, block), 1) - lax.broadcasted_iota(jnp.int32, (block, block), 0)

    def body(j, carry):
        rows = pl.ds(pl.multiple_of(j * block, block), block)
        allowed = (docs_q == dcol_ref[rows, :]) & (gap >= (j - i) * block)
        new = []
        for h in range(heads):
            q, g = queries[h], grads[h]
            k = qkv_ref[rows, part(h, 1)]
            s = lax.dot_general(k, q, NT, preferred_element_type=jnp.float32) * scale
            p = jnp.exp(jnp.where(allowed, s - lse_ref[h], -1e30))
            dp = lax.dot_general(qkv_ref[rows, part(h, 2)], g, NT, preferred_element_type=jnp.float32)
            ds = (p * (dp - deltas[h]) * scale).astype(jnp.bfloat16)
            dv[rows, cols(h)] += jnp.dot(p.astype(jnp.bfloat16), g, preferred_element_type=jnp.float32)
            dk[rows, cols(h)] += jnp.dot(ds, q, preferred_element_type=jnp.float32)
            new.append(carry[h] + lax.dot_general(ds, k, TN, preferred_element_type=jnp.float32))
        return tuple(new)

    dq = lax.fori_loop(0, i + 1, body, (jnp.zeros((block, HEAD_DIM), jnp.float32),) * heads)

    def put(rows, first, val):
        rot = (cos_ref[rows, :], su_ref[rows, :], sd_ref[rows, :])
        out_ref[rows, first : first + LANES] = rotate_back_tile(val[:, :LANES], *rot).astype(jnp.bfloat16)
        out_ref[rows, first + LANES : first + HEAD_DIM] = val[:, LANES:].astype(jnp.bfloat16)

    for h in range(heads):
        put(here, 3 * h * HEAD_DIM, dq[h])

    @pl.when(i == n - 1)
    def _():
        for h in range(heads):
            for b in range(n):
                rows = slice(b * block, (b + 1) * block)
                put(rows, (3 * h + 1) * HEAD_DIM, dk[rows, cols(h)])
                out_ref[rows, part(h, 2)] = dv[rows, cols(h)].astype(jnp.bfloat16)


def attend_back(qkv, grad_att, attended, docs, lse, rot, block=512):
    total, cols = qkv.shape
    heads = cols // (3 * HEAD_DIM)
    seqs = total // SEQ_LEN
    n = SEQ_LEN // block
    whole = pl.BlockSpec((SEQ_LEN, cols), lambda s, i: (s, 0))
    mine = pl.BlockSpec((block, heads * HEAD_DIM), lambda s, i: (s * n + i, 0))
    table = pl.BlockSpec((SEQ_LEN, LANES), lambda s, i: (s, 0))
    return pl.pallas_call(
        functools.partial(attend_back_kernel, block, n, heads),
        grid=(seqs, n),
        in_specs=[
            whole, mine, mine,
            pl.BlockSpec((SEQ_LEN, 1), lambda s, i: (s, 0)),
            pl.BlockSpec((1, block), lambda s, i: (0, s * n + i)),
            pl.BlockSpec((heads, 1, block), lambda s, i: (0, 0, s * n + i)),
            table, table, table,
        ],
        out_specs=whole,
        out_shape=jax.ShapeDtypeStruct((total, cols), jnp.bfloat16),
        scratch_shapes=[pltpu.VMEM((SEQ_LEN, heads * HEAD_DIM), jnp.float32)] * 2,
        compiler_params=pltpu.CompilerParams(vmem_limit_bytes=VMEM_CAP),
        cost_estimate=pl.CostEstimate(flops=5 * total * SEQ_LEN * heads * HEAD_DIM, bytes_accessed=8 * total * cols, transcendentals=total * SEQ_LEN),
        name="attend_back",
    )(qkv, grad_att, attended, docs[:, None], docs[None, :], lse, *rot)


def ar_kernel(n, C, s_ref, full_ref, own, recv, ld_sem, rs_send, rs_recv, agr_send, agl_send, ag_recv, st_sem):
    k = lax.axis_index(AX)
    R, W = own.shape[2], own.shape[3]
    bar = pltpu.get_barrier_semaphore()
    @pl.when(k > 0)
    def _():
        pl.semaphore_signal(bar, inc=1, device_id={AX: k-1}, device_id_type=pl.DeviceIdType.MESH)
    @pl.when(k < n-1)
    def _():
        pl.semaphore_signal(bar, inc=1, device_id={AX: k+1}, device_id_type=pl.DeviceIdType.MESH)
    pl.semaphore_wait(bar, (k > 0).astype(jnp.int32) + (k < n-1).astype(jnp.int32))

    def rows(c): return pl.ds(pl.multiple_of(c*R, R), R)
    def ld(c, j):
        return pltpu.make_async_copy(s_ref.at[rows(c), pl.ds(j*W, W)], own.at[c, j], ld_sem.at[c, j])
    def rs_copy(c, j, right):
        dst = jnp.where(k-1 == j, n, j) if not right else j
        return pltpu.make_async_remote_copy(own.at[c, j], recv.at[c, dst], rs_send.at[c, j], rs_recv.at[c, dst],
            device_id={AX: k+1 if right else k-1}, device_id_type=pl.DeviceIdType.MESH)
    def ag_copy(c, j, right):
        blk = full_ref.at[rows(c), pl.ds(j*W, W)]
        return pltpu.make_async_remote_copy(blk, blk, (agr_send if right else agl_send).at[c, j], ag_recv.at[c, j],
            device_id={AX: k+1 if right else k-1}, device_id_type=pl.DeviceIdType.MESH)
    def own_ag_copy(c, j, right):
        blk = full_ref.at[rows(c), pl.ds(j*W, W)]
        return pltpu.make_async_remote_copy(own.at[c, j], blk, (agr_send if right else agl_send).at[c, j], ag_recv.at[c, j],
            device_id={AX: k+1 if right else k-1}, device_id_type=pl.DeviceIdType.MESH)
    def store(c, j):
        return pltpu.make_async_copy(own.at[c, j], full_ref.at[rows(c), pl.ds(j*W, W)], st_sem.at[c])

    for c in range(C):
        for j in range(n): ld(c, j).start()

    def when(cond):
        return pl.when(cond)
    def ok(c): return jnp.logical_and(c >= 0, c < C)

    def step(i, _):
        @pl.when(i < C)
        def _():
            for j in range(n): ld(i, j).wait()
        for p in range(n):
            for right in (True, False):
                j = p if right else n-1-p
                dist = (k - j) if right else (j - k)
                c_ag = i - (n-1) - dist
                c_rs = i - (k if right else n-1-k)
                @pl.when((dist > 0) & ok(c_ag))
                def _(j=j, right=right, c=c_ag):
                    ag_copy(c, j, right).wait_recv()
                    @pl.when((k < n-1) if right else (k > 0))
                    def _(): ag_copy(c, j, right).start()
                @pl.when((dist < 0) & ok(c_rs))
                def _(j=j, right=right, c=c_rs):
                    @pl.when((k > 0) if right else (k < n-1))
                    def _():
                        pltpu.make_async_remote_copy(own.at[c, j], recv.at[c, j], rs_send.at[c, j], rs_recv.at[c, j],
                            device_id={AX: k}, device_id_type=pl.DeviceIdType.MESH).wait_recv()
                        own[c, j] = own[c, j] + recv[c, j]
                    rs_copy(c, j, right).start()
        c = i - (n-1)
        for j in range(n):
            @pl.when((k == j) & ok(c))
            def _(j=j):
                acc = own[c, j].astype(jnp.float32)
                if j > 0:
                    rs_copy_w = pltpu.make_async_remote_copy(own.at[c, j], recv.at[c, j], rs_send.at[c, j], rs_recv.at[c, j], device_id={AX: k}, device_id_type=pl.DeviceIdType.MESH)
                    rs_copy_w.wait_recv()
                    acc = acc + recv[c, j].astype(jnp.float32)
                if j < n-1:
                    w = pltpu.make_async_remote_copy(own.at[c, j], recv.at[c, n], rs_send.at[c, j], rs_recv.at[c, n], device_id={AX: k}, device_id_type=pl.DeviceIdType.MESH)
                    w.wait_recv()
                    acc = acc + recv[c, n].astype(jnp.float32)
                own[c, j] = acc.astype(own.dtype)
                store(c, j).start()
                if j < n-1: own_ag_copy(c, j, True).start()
                if j > 0: own_ag_copy(c, j, False).start()
        return 0
    lax.fori_loop(0, C + 2*(n-1), step, 0)
    def drain(c, _):
        for j in range(n):
            @pl.when(k < j)
            def _():
                rs_copy(c, j, True).wait_send()
                @pl.when(k > 0)
                def _(): ag_copy(c, j, False).wait_send()
            @pl.when(k > j)
            def _():
                rs_copy(c, j, False).wait_send()
                @pl.when(k < n-1)
                def _(): ag_copy(c, j, True).wait_send()
            @pl.when(k == j)
            def _():
                store(c, j).wait()
                if j < n-1: own_ag_copy(c, j, True).wait_send()
                if j > 0: own_ag_copy(c, j, False).wait_send()
        return 0
    lax.fori_loop(0, C, drain, 0)


def sum_over_tensor(s, chunks=16):
    n = lax.axis_size(AX)
    total, width = s.shape
    rows, cols = total // chunks, width // n
    dma = pltpu.SemaphoreType.DMA
    return pl.pallas_call(
        functools.partial(ar_kernel, n, chunks),
        out_shape=jax.ShapeDtypeStruct(s.shape, s.dtype),
        in_specs=[pl.BlockSpec(memory_space=pl.ANY)],
        out_specs=pl.BlockSpec(memory_space=pl.ANY),
        scratch_shapes=[
            pltpu.VMEM((chunks, n, rows, cols), s.dtype),
            pltpu.VMEM((chunks, n + 1, rows, cols), s.dtype),
            dma((chunks, n)), dma((chunks, n)), dma((chunks, n + 1)), dma((chunks, n)), dma((chunks, n)), dma((chunks, n)), dma((chunks,)),
        ],
        compiler_params=pltpu.CompilerParams(collective_id=0, has_side_effects=True, vmem_limit_bytes=VMEM_CAP),
        name="sum_over_tensor",
    )(s)


def exact_gelu(values):
    return jax.nn.gelu(values, approximate=False)


def mul(a, b):
    return jnp.dot(a, b, preferred_element_type=jnp.float32)


def on_device(tokens, segments, positions, ln1_gain, ln1_bias, ln2_gain, ln2_bias, qkv_weight, dense_weight, fc1_weight, fc2_weight, upstream):
    low = jnp.bfloat16
    total_rows, width = tokens.shape
    up = lax.all_gather(upstream, AX, axis=1, tiled=True)
    rot = rot_tables(positions)
    h_one, h_two, qkv = project(tokens, ln1_gain, ln1_bias, ln2_gain, ln2_bias, rot, qkv_weight)
    attended, lse = attend(qkv, segments, 1024)
    pre_act = mul(h_two, fc1_weight)
    hidden_wide, pull = jax.vjp(exact_gelu, pre_act)
    hidden = hidden_wide.astype(low)
    slope = pull(jnp.ones_like(pre_act))[0].astype(low)
    partial_out = (mul(attended, dense_weight) + mul(hidden, fc2_weight)).astype(low)
    own_sum = lax.psum_scatter(partial_out, AX, scatter_dimension=1, tiled=True)
    share = width // lax.axis_size(AX)
    own_x = lax.dynamic_slice_in_dim(tokens, lax.axis_index(AX) * share, share, 1)
    output = (own_x.astype(jnp.float32) + own_sum.astype(jnp.float32)).astype(low)

    grad_att = mul(up, dense_weight.T).astype(low)
    grad_qkv = attend_back(qkv, grad_att, attended, segments, lse, rot)
    grad_pre = (mul(up, fc2_weight.T) * slope.astype(jnp.float32)).astype(low)
    grad_h_two = mul(grad_pre, fc1_weight.T)
    grad_h_one = mul(grad_qkv, qkv_weight.T)
    partial_s = (grad_h_one * ln1_gain + grad_h_two * ln2_gain).astype(low)
    x = tokens.astype(jnp.float32)
    center = x - jnp.mean(x, axis=-1, keepdims=True)
    inv_scale = lax.rsqrt(jnp.mean(center * center, axis=-1, keepdims=True) + 1e-05)
    normed = center * inv_scale
    norm_part = jnp.stack([
        jnp.sum(grad_h_one * normed, axis=0),
        jnp.sum(grad_h_one, axis=0),
        jnp.sum(grad_h_two * normed, axis=0),
        jnp.sum(grad_h_two, axis=0),
    ])
    fc2_term = mul(hidden.T, up).astype(low)
    fc1_term = mul(h_two.T, grad_pre).astype(low)
    dense_term = mul(attended.T, up).astype(low)
    qkv_term = mul(h_one.T, grad_qkv).astype(low)
    partial_s, fc2_term, fc1_term, dense_term, qkv_term, norm_part = lax.optimization_barrier(
        (partial_s, fc2_term, fc1_term, dense_term, qkv_term, norm_part))
    s = sum_over_tensor(partial_s).astype(jnp.float32)
    input_grad = up.astype(jnp.float32) + inv_scale * (
        s - jnp.mean(s, axis=-1, keepdims=True) - normed * jnp.mean(s * normed, axis=-1, keepdims=True))
    scatter = lambda g, d: lax.psum_scatter(g, "dp", scatter_dimension=d, tiled=True).astype(jnp.float32)
    norm_grads = lax.psum_scatter(lax.psum(norm_part, AX), "dp", scatter_dimension=1, tiled=True)
    return (
        output, input_grad,
        scatter(qkv_term, 0), scatter(dense_term, 1), scatter(fc1_term, 0), scatter(fc2_term, 1),
        norm_grads[0], norm_grads[1], norm_grads[2], norm_grads[3],
    )


def solution(mesh):
    in_specs = (
        P("dp", None),
        P("dp"),
        P("dp"),
        P(),
        P(),
        P(),
        P(),
        P(None, "tensor"),
        P("tensor", None),
        P(None, "tensor"),
        P("tensor", None),
        P("dp", "tensor"),
    )
    out_specs = (
        P("dp", "tensor"),
        P("dp", None),
        P("dp", "tensor"),
        P("tensor", "dp"),
        P("dp", "tensor"),
        P("tensor", "dp"),
        P("dp"),
        P("dp"),
        P("dp"),
        P("dp"),
    )
    return jax.shard_map(
        on_device, mesh=mesh, in_specs=in_specs, out_specs=out_specs, check_vma=False
    )
```

```python
import functools
import itertools

import jax
import jax.numpy as jnp
from jax import lax
from jax.experimental import pallas as pl
from jax.experimental.pallas import tpu as pltpu
from jax.sharding import PartitionSpec as P

HEAD_DIM = 256
ROT_DIM = 64
SEQ_LEN = 2048
LANES = 128
VMEM_CAP = 60 * 2**20
NT = (((1,), (1,)), ((), ()))
TN = (((0,), (0,)), ((), ()))


def rot_tables(positions):
    half = ROT_DIM // 2
    steps_up = jnp.arange(half).astype(jnp.float32) * 2.0 / ROT_DIM
    inverse = jnp.power(jnp.float32(10000.0), -steps_up)
    angle = positions.astype(jnp.float32)[:, None] * inverse[None, :]
    cos, sin = jnp.cos(angle), jnp.sin(angle)
    zero = jnp.zeros_like(sin)
    rest = jnp.zeros((positions.shape[0], LANES - ROT_DIM), jnp.float32)
    cos_t = jnp.concatenate([cos, cos, rest + 1.0], -1)
    sin_up = jnp.concatenate([-sin, zero, rest], -1)
    sin_down = jnp.concatenate([zero, sin, rest], -1)
    return cos_t, sin_up, sin_down


def rotate_tile(u, cos_t, sin_up, sin_down):
    half = ROT_DIM // 2
    return u * cos_t + pltpu.roll(u, LANES - half, 1) * sin_up + pltpu.roll(u, half, 1) * sin_down


def rotate_back_tile(g, cos_t, sin_up, sin_down):
    half = ROT_DIM // 2
    return g * cos_t + pltpu.roll(g * sin_down, LANES - half, 1) + pltpu.roll(g * sin_up, half, 1)


def pre_kernel(x_ref, g1_ref, b1_ref, g2_ref, b2_ref, cos_ref, su_ref, sd_ref, w_ref, h1_ref, h2_ref, qkv_ref):
    x = x_ref[...].astype(jnp.float32)
    center = x - jnp.mean(x, axis=-1, keepdims=True)
    inv = lax.rsqrt(jnp.mean(center * center, axis=-1, keepdims=True) + 1e-05)
    normed = center * inv
    h1 = (normed * g1_ref[...] + b1_ref[...]).astype(jnp.bfloat16)
    h1_ref[...] = h1
    h2_ref[...] = (normed * g2_ref[...] + b2_ref[...]).astype(jnp.bfloat16)
    cos_t, su, sd = cos_ref[...], su_ref[...], sd_ref[...]
    for b in range(w_ref.shape[1] // HEAD_DIM):
        cols = slice(b * HEAD_DIM, (b + 1) * HEAD_DIM)
        y = jnp.dot(h1, w_ref[:, cols], preferred_element_type=jnp.float32)
        if b % 3 < 2:
            qkv_ref[:, b * HEAD_DIM : b * HEAD_DIM + LANES] = rotate_tile(y[:, :LANES], cos_t, su, sd).astype(jnp.bfloat16)
            qkv_ref[:, b * HEAD_DIM + LANES : (b + 1) * HEAD_DIM] = y[:, LANES:].astype(jnp.bfloat16)
        else:
            qkv_ref[:, cols] = y.astype(jnp.bfloat16)


def project(tokens, g1, b1, g2, b2, rot, w, rows=256):
    total, width = tokens.shape
    rows = min(rows, total)
    row_blk = lambda cols: pl.BlockSpec((rows, cols), lambda i: (i, 0))
    vec = pl.BlockSpec((1, width), lambda i: (0, 0))
    cols = w.shape[1]
    return pl.pallas_call(
        pre_kernel,
        grid=(total // rows,),
        in_specs=[row_blk(width), vec, vec, vec, vec, row_blk(LANES), row_blk(LANES), row_blk(LANES),
                  pl.BlockSpec((width, cols), lambda i: (0, 0), pipeline_mode=pl.Buffered(1))],
        out_specs=[row_blk(width), row_blk(width), row_blk(cols)],
        out_shape=[jax.ShapeDtypeStruct((total, width), jnp.bfloat16)] * 2 + [jax.ShapeDtypeStruct((total, cols), jnp.bfloat16)],
        compiler_params=pltpu.CompilerParams(vmem_limit_bytes=VMEM_CAP),
        cost_estimate=pl.CostEstimate(flops=2 * total * width * cols, bytes_accessed=6 * total * width + 2 * cols * (width + total), transcendentals=0),
        name="norm_project",
    )(tokens, g1[None], b1[None], g2[None], b2[None], *rot, w)


def attend_kernel(block, heads, qkv_ref, drow_ref, dcol_ref, o_ref, lse_ref, v_turned):
    i = pl.program_id(1)
    scale = HEAD_DIM ** (-0.5)
    part = lambda h, c: slice((3 * h + c) * HEAD_DIM, (3 * h + c + 1) * HEAD_DIM)

    @pl.when(i == 0)
    def _():
        for h in range(heads):
            v_turned[h] = qkv_ref[:, part(h, 2)].T

    here = pl.ds(pl.multiple_of(i * block, block), block)
    queries = [qkv_ref[here, part(h, 0)] for h in range(heads)]
    docs_q = drow_ref[...]
    gap = lax.broadcasted_iota(jnp.int32, (block, block), 1) - lax.broadcasted_iota(jnp.int32, (block, block), 0)

    def body(j, carry):
        rows = pl.ds(pl.multiple_of(j * block, block), block)
        allowed = (docs_q == dcol_ref[rows, :]) & (gap >= (j - i) * block)
        new = []
        for h in range(heads):
            m, l, acc = carry[h]
            s = lax.dot_general(qkv_ref[rows, part(h, 1)], queries[h], NT, preferred_element_type=jnp.float32) * scale
            s = jnp.where(allowed, s, -1e30)
            m_new = jnp.maximum(m, jnp.max(s, axis=0, keepdims=True))
            p = jnp.exp(s - m_new)
            alpha = jnp.exp(m - m_new)
            l = l * alpha + jnp.sum(p, axis=0, keepdims=True)
            acc = acc * alpha + jnp.dot(v_turned[h, :, rows], p.astype(jnp.bfloat16), preferred_element_type=jnp.float32)
            new.append((m_new, l, acc))
        return tuple(new)

    start = (jnp.full((1, block), -1e30, jnp.float32), jnp.zeros((1, block), jnp.float32), jnp.zeros((HEAD_DIM, block), jnp.float32))
    carry = lax.fori_loop(0, i + 1, body, (start,) * heads)
    for h in range(heads):
        m, l, acc = carry[h]
        o_ref[:, h * HEAD_DIM : (h + 1) * HEAD_DIM] = (acc * (1.0 / l)).T.astype(jnp.bfloat16)
        lse_ref[h] = m + jnp.log(l)


def attend(qkv, docs, block=512):
    total, cols = qkv.shape
    heads = cols // (3 * HEAD_DIM)
    seqs = total // SEQ_LEN
    n = SEQ_LEN // block
    return pl.pallas_call(
        functools.partial(attend_kernel, block, heads),
        grid=(seqs, n),
        in_specs=[
            pl.BlockSpec((SEQ_LEN, cols), lambda s, i: (s, 0)),
            pl.BlockSpec((1, block), lambda s, i: (0, s * n + i)),
            pl.BlockSpec((SEQ_LEN, 1), lambda s, i: (s, 0)),
        ],
        out_specs=[pl.BlockSpec((block, heads * HEAD_DIM), lambda s, i: (s * n + i, 0)),
                   pl.BlockSpec((heads, 1, block), lambda s, i: (0, 0, s * n + i))],
        out_shape=[jax.ShapeDtypeStruct((total, heads * HEAD_DIM), jnp.bfloat16), jax.ShapeDtypeStruct((heads, 1, total), jnp.float32)],
        scratch_shapes=[pltpu.VMEM((heads, HEAD_DIM, SEQ_LEN), jnp.bfloat16)],
        compiler_params=pltpu.CompilerParams(vmem_limit_bytes=VMEM_CAP),
        cost_estimate=pl.CostEstimate(flops=2 * total * SEQ_LEN * heads * HEAD_DIM, bytes_accessed=4 * total * cols, transcendentals=total * SEQ_LEN),
        name="attend",
    )(qkv, docs[None, :], docs[:, None])


def attend_back_kernel(block, n, heads, qkv_ref, g_ref, o_ref, dcol_ref, drow_ref, lse_ref, cos_ref, su_ref, sd_ref, out_ref, dk, dv):
    i = pl.program_id(1)
    scale = HEAD_DIM ** (-0.5)
    part = lambda h, c: slice((3 * h + c) * HEAD_DIM, (3 * h + c + 1) * HEAD_DIM)
    cols = lambda h: slice(h * HEAD_DIM, (h + 1) * HEAD_DIM)

    @pl.when(i == 0)
    def _():
        dk[...] = jnp.zeros_like(dk)
        dv[...] = jnp.zeros_like(dv)

    here = pl.ds(pl.multiple_of(i * block, block), block)
    docs_q = drow_ref[...]
    ones = jnp.ones((8, HEAD_DIM), jnp.float32)
    queries = [qkv_ref[here, part(h, 0)] for h in range(heads)]
    grads = [g_ref[:, cols(h)] for h in range(heads)]
    deltas = [
        lax.dot_general(ones, grads[h].astype(jnp.float32) * o_ref[:, cols(h)].astype(jnp.float32), NT,
                        precision=lax.Precision.HIGHEST, preferred_element_type=jnp.float32)[:1]
        for h in range(heads)
    ]
    gap = lax.broadcasted_iota(jnp.int32, (block, block), 1) - lax.broadcasted_iota(jnp.int32, (block, block), 0)

    def body(j, carry):
        rows = pl.ds(pl.multiple_of(j * block, block), block)
        allowed = (docs_q == dcol_ref[rows, :]) & (gap >= (j - i) * block)
        new = []
        for h in range(heads):
            q, g = queries[h], grads[h]
            k = qkv_ref[rows, part(h, 1)]
            s = lax.dot_general(k, q, NT, preferred_element_type=jnp.float32) * scale
            p = jnp.exp(jnp.where(allowed, s - lse_ref[h], -1e30))
            dp = lax.dot_general(qkv_ref[rows, part(h, 2)], g, NT, preferred_element_type=jnp.float32)
            ds = (p * (dp - deltas[h]) * scale).astype(jnp.bfloat16)
            dv[rows, cols(h)] += jnp.dot(p.astype(jnp.bfloat16), g, preferred_element_type=jnp.float32)
            dk[rows, cols(h)] += jnp.dot(ds, q, preferred_element_type=jnp.float32)
            new.append(carry[h] + lax.dot_general(ds, k, TN, preferred_element_type=jnp.float32))
        return tuple(new)

    dq = lax.fori_loop(0, i + 1, body, (jnp.zeros((block, HEAD_DIM), jnp.float32),) * heads)

    def put(rows, first, val):
        rot = (cos_ref[rows, :], su_ref[rows, :], sd_ref[rows, :])
        out_ref[rows, first : first + LANES] = rotate_back_tile(val[:, :LANES], *rot).astype(jnp.bfloat16)
        out_ref[rows, first + LANES : first + HEAD_DIM] = val[:, LANES:].astype(jnp.bfloat16)

    for h in range(heads):
        put(here, 3 * h * HEAD_DIM, dq[h])

    @pl.when(i == n - 1)
    def _():
        for h in range(heads):
            for b in range(n):
                rows = slice(b * block, (b + 1) * block)
                put(rows, (3 * h + 1) * HEAD_DIM, dk[rows, cols(h)])
                out_ref[rows, part(h, 2)] = dv[rows, cols(h)].astype(jnp.bfloat16)


def attend_back(qkv, grad_att, attended, docs, lse, rot, block=512):
    total, cols = qkv.shape
    heads = cols // (3 * HEAD_DIM)
    seqs = total // SEQ_LEN
    n = SEQ_LEN // block
    whole = pl.BlockSpec((SEQ_LEN, cols), lambda s, i: (s, 0))
    mine = pl.BlockSpec((block, heads * HEAD_DIM), lambda s, i: (s * n + i, 0))
    table = pl.BlockSpec((SEQ_LEN, LANES), lambda s, i: (s, 0))
    return pl.pallas_call(
        functools.partial(attend_back_kernel, block, n, heads),
        grid=(seqs, n),
        in_specs=[
            whole, mine, mine,
            pl.BlockSpec((SEQ_LEN, 1), lambda s, i: (s, 0)),
            pl.BlockSpec((1, block), lambda s, i: (0, s * n + i)),
            pl.BlockSpec((heads, 1, block), lambda s, i: (0, 0, s * n + i)),
            table, table, table,
        ],
        out_specs=whole,
        out_shape=jax.ShapeDtypeStruct((total, cols), jnp.bfloat16),
        scratch_shapes=[pltpu.VMEM((SEQ_LEN, heads * HEAD_DIM), jnp.float32)] * 2,
        compiler_params=pltpu.CompilerParams(vmem_limit_bytes=VMEM_CAP),
        cost_estimate=pl.CostEstimate(flops=5 * total * SEQ_LEN * heads * HEAD_DIM, bytes_accessed=8 * total * cols, transcendentals=total * SEQ_LEN),
        name="attend_back",
    )(qkv, grad_att, attended, docs[:, None], docs[None, :], lse, *rot)


AX = "tensor"
DP = "dp"
MESH = pl.DeviceIdType.MESH
STRIP = 256


def greet(peers):
    barrier = pltpu.get_barrier_semaphore()
    count = 0
    for cond, device in peers:
        @pl.when(cond)
        def _(device=device):
            pl.semaphore_signal(barrier, inc=1, device_id=device, device_id_type=MESH)
        count = count + jnp.asarray(cond).astype(jnp.int32)
    pl.semaphore_wait(barrier, count)


def within(c, count):
    return (c >= 0) & (c < count)


class LineSum:
    def __init__(self, n, chunks, full_ref, own, recv, rs_send, rs_recv, ag_right, ag_left, ag_recv, store_sem):
        self.n, self.chunks, self.full_ref, self.own, self.recv = n, chunks, full_ref, own, recv
        self.rs_send, self.rs_recv, self.ag_send, self.ag_recv, self.store_sem = rs_send, rs_recv, (ag_right, ag_left), ag_recv, store_sem
        self.k = lax.axis_index(AX)
        self.rows, self.cols = own.shape[2], own.shape[3]

    def block(self, c, j):
        return self.full_ref.at[pl.ds(pl.multiple_of(c * self.rows, self.rows), self.rows), pl.ds(j * self.cols, self.cols)]

    def copy(self, src, dst, send, recv, right):
        return pltpu.make_async_remote_copy(src, dst, send, recv, device_id={AX: self.k + 1 if right else self.k - 1}, device_id_type=MESH)

    def scatter_copy(self, c, j, right):
        slot = j if right else jnp.where(self.k - 1 == j, self.n, j)
        return self.copy(self.own.at[c, j], self.recv.at[c, slot], self.rs_send.at[c, j], self.rs_recv.at[c, slot], right)

    def scatter_arrived(self, c, slot):
        dst = self.recv.at[c, slot]
        pltpu.make_async_copy(dst, dst, self.rs_recv.at[c, slot]).wait()

    def gather_copy(self, c, j, right, src=None):
        block = self.block(c, j)
        return self.copy(block if src is None else src, block, self.ag_send[0 if right else 1].at[c, j], self.ag_recv.at[c, j], right)

    def gather_arrived(self, c, j):
        block = self.block(c, j)
        pltpu.make_async_copy(block, block, self.ag_recv.at[c, j]).wait()

    def store(self, c, j):
        return pltpu.make_async_copy(self.own.at[c, j], self.block(c, j), self.store_sem.at[c])

    def step(self, i):
        n, k, chunks = self.n, self.k, self.chunks
        for p in range(n):
            for right in (True, False):
                j = p if right else n - 1 - p
                dist = (k - j) if right else (j - k)
                onward = (k < n - 1) if right else (k > 0)
                behind = (k > 0) if right else (k < n - 1)
                c_gather = i - (n - 1) - dist
                c_scatter = i - (k if right else n - 1 - k)

                @pl.when((dist > 0) & within(c_gather, chunks))
                def _(j=j, right=right, c=c_gather, onward=onward):
                    self.gather_arrived(c, j)

                    @pl.when(onward)
                    def _():
                        self.gather_copy(c, j, right).start()

                @pl.when((dist < 0) & within(c_scatter, chunks))
                def _(j=j, right=right, c=c_scatter, behind=behind):
                    @pl.when(behind)
                    def _():
                        self.scatter_arrived(c, j)
                        self.own[c, j] = self.own[c, j] + self.recv[c, j]

                    self.scatter_copy(c, j, right).start()

        c = i - (n - 1)
        for j in range(n):
            @pl.when((k == j) & within(c, chunks))
            def _(j=j):
                total = self.own[c, j].astype(jnp.float32)
                if j > 0:
                    self.scatter_arrived(c, j)
                    total = total + self.recv[c, j].astype(jnp.float32)
                if j < n - 1:
                    self.scatter_arrived(c, n)
                    total = total + self.recv[c, n].astype(jnp.float32)
                self.own[c, j] = total.astype(self.own.dtype)
                self.store(c, j).start()
                if j < n - 1:
                    self.gather_copy(c, j, True, self.own.at[c, j]).start()
                if j > 0:
                    self.gather_copy(c, j, False, self.own.at[c, j]).start()

    def drain(self):
        n, k = self.n, self.k

        def one(c, _):
            for j in range(n):
                @pl.when(k < j)
                def _(j=j):
                    self.scatter_copy(c, j, True).wait_send()

                    @pl.when(k > 0)
                    def _():
                        self.gather_copy(c, j, False).wait_send()

                @pl.when(k > j)
                def _(j=j):
                    self.scatter_copy(c, j, False).wait_send()

                    @pl.when(k < n - 1)
                    def _():
                        self.gather_copy(c, j, True).wait_send()

                @pl.when(k == j)
                def _(j=j):
                    self.store(c, j).wait()
                    if j < n - 1:
                        self.gather_copy(c, j, True, self.own.at[c, j]).wait_send()
                    if j > 0:
                        self.gather_copy(c, j, False, self.own.at[c, j]).wait_send()
            return 0

        lax.fori_loop(0, self.chunks, one, 0)


class HalvingSum:
    def __init__(self, dp, groups, xs, ys, outs, xbuf, ybuf, tiles, recvs, stage, stage_turned, x_sem, y_sem, send_sem, recv_sem, out_sem):
        self.dp, self.bits = dp, dp.bit_length() - 1
        self.groups, self.xs, self.ys, self.outs = groups, xs, ys, outs
        self.xbuf, self.ybuf, self.tiles, self.recvs = xbuf, ybuf, tiles, recvs
        self.stage, self.stage_turned = stage, stage_turned
        self.x_sem, self.y_sem, self.send_sem, self.recv_sem, self.out_sem = x_sem, y_sem, send_sem, recv_sem, out_sem
        self.me = lax.axis_index(DP)
        self.slots = tiles.shape[0]
        self.width = tiles.shape[-1]
        self.first = [sum(g["count"] for g in groups[:i]) for i in range(len(groups) + 1)]
        self.total = self.first[-1]

    def bit(self, b):
        return lax.rem(lax.div(self.me, 2**b), 2)

    def partner(self, b):
        return self.me + (1 - 2 * self.bit(b)) * 2**b

    def order(self, odd):
        rest = list(range(1, self.bits))
        return [0] + (rest[1:] + rest[:1] if odd else rest)

    def pick(self, odd, level, value):
        done = self.order(odd)[:level]
        now = self.order(odd)[level]
        return tuple(0 if b in done else value if b == now else slice(None) for b in range(self.bits))

    def in_group(self, t, g):
        return (t >= self.first[g]) & (t < self.first[g + 1])

    def x_copies(self, t):
        for g, group in enumerate(self.groups):
            at = pl.ds(pl.multiple_of((t - self.first[g]) * STRIP, STRIP), STRIP)
            slot = lax.rem(t, 2)
            yield self.in_group(t, g), pltpu.make_async_copy(self.xs[group["x"]].at[:, at], self.xbuf.at[slot], self.x_sem.at[slot])

    def x_start(self, t):
        for cond, copy in self.x_copies(t):
            @pl.when(cond)
            def _(copy=copy):
                copy.start()

    def x_wait(self, t):
        slot = lax.rem(t, 2)
        pltpu.make_async_copy(self.xbuf.at[slot], self.xbuf.at[slot], self.x_sem.at[slot]).wait()

    def y_copy(self, g):
        y = self.groups[g]["y"]
        return pltpu.make_async_copy(self.ys[y], self.ybuf.at[y % 2], self.y_sem.at[y % 2])

    def send(self, u, odd, level):
        slot = lax.rem(u, self.slots)
        return pltpu.make_async_remote_copy(
            self.tiles.at[(slot, *self.pick(odd, level, 1))], self.recvs[level].at[slot],
            self.send_sem.at[level, slot], self.recv_sem.at[level, slot],
            device_id={DP: self.partner(self.order(odd)[level])}, device_id_type=MESH)

    def out_copies(self, u):
        slot = lax.rem(u, 2)
        for g, group in enumerate(self.groups):
            at = pl.ds(pl.multiple_of((u - self.first[g]) * STRIP, STRIP), STRIP)
            out = self.outs[group["out"]]
            if group["turned"]:
                yield self.in_group(u, g), pltpu.make_async_copy(self.stage_turned.at[slot], out.at[:, at], self.out_sem.at[slot])
            else:
                yield self.in_group(u, g), pltpu.make_async_copy(self.stage.at[slot], out.at[at, :], self.out_sem.at[slot])

    def out_wait(self, u):
        for cond, copy in self.out_copies(u):
            @pl.when(cond)
            def _(copy=copy):
                copy.wait()

    def prologue(self):
        self.x_start(jnp.int32(0))
        self.y_copy(0).start()
        for g in range(1, len(self.groups)):
            if self.groups[g]["y"] == 1:
                self.y_copy(g).start()
                break

    def tick(self, t, place, period):
        odd = place % 2
        for level in range(self.bits - 1, -1, -1):
            u = t - level - 1
            u_odd = (place - level - 1) % period % 2

            @pl.when(within(u, self.total))
            def _(u=u, u_odd=u_odd, level=level):
                slot = lax.rem(u, self.slots)
                got = self.recvs[level]
                pltpu.make_async_copy(got.at[slot], got.at[slot], self.recv_sem.at[level, slot]).wait()
                keep = (slot, *self.pick(u_odd, level, 0))
                if level < self.bits - 1:
                    left = [range(2) if isinstance(p, slice) else (p,) for p in keep[1:]]
                    for flat, idx in enumerate(itertools.product(*left)):
                        pos = tuple(int(b) for b in format(flat, "b").zfill(self.bits - 1 - level))
                        self.tiles[(slot, *idx)] = self.tiles[(slot, *idx)] + got[(slot, *pos)]
                    self.send(u, u_odd, level + 1).start()
                else:
                    @pl.when(u >= 2)
                    def _():
                        self.out_wait(u - 2)

                    value = self.tiles[keep].astype(jnp.float32) + got[slot].astype(jnp.float32)
                    for g, group in enumerate(self.groups):
                        @pl.when(self.in_group(u, g))
                        def _(group=group):
                            if group["turned"]:
                                self.stage_turned[lax.rem(u, 2)] = value.T
                            else:
                                self.stage[lax.rem(u, 2)] = value
                    for cond, copy in self.out_copies(u):
                        @pl.when(cond)
                        def _(copy=copy):
                            copy.start()

        @pl.when(within(t, self.total))
        def _():
            slot = lax.rem(t, self.slots)

            @pl.when(t >= self.slots)
            def _():
                for level in range(self.bits):
                    self.send(t - self.slots, (place - self.slots) % period % 2, level).wait_send()

            seen = []
            for g, group in enumerate(self.groups):
                if group["y"] in seen:
                    continue
                seen.append(group["y"])

                @pl.when(t == self.first[g])
                def _(g=g, group=group):
                    self.y_copy(g).wait()
                    if group["y"] == 1:
                        for later in range(len(self.groups)):
                            if self.groups[later]["y"] == 2:
                                self.y_copy(later).start()
                                break

            @pl.when(t + 1 < self.total)
            def _():
                self.x_start(t + 1)

            self.x_wait(t)
            y_slot = jnp.int32(0)
            for g, group in enumerate(self.groups):
                y_slot = jnp.where(t >= self.first[g], group["y"] % 2, y_slot)
            x = self.xbuf[lax.rem(t, 2)]
            for flat in range(self.dp):
                idx = tuple((flat >> b) & 1 for b in range(self.bits))
                shard = sum((self.bit(b) + idx[b] * (1 - 2 * self.bit(b))) * 2**b for b in range(self.bits))
                at = pl.ds(pl.multiple_of(shard * self.width, self.width), self.width)
                self.tiles[(slot, *idx)] = lax.dot_general(x, self.ybuf[y_slot, :, at], TN, preferred_element_type=jnp.float32).astype(jnp.bfloat16)
            self.send(t, odd, 0).start()

    def drain(self, period):
        for u in range(self.total - self.slots, self.total):
            for level in range(self.bits):
                self.send(jnp.int32(u), u % period % 2, level).wait_send()
        for u in range(self.total - 2, self.total):
            self.out_wait(jnp.int32(u))


def sums_kernel(n, dp, chunks, steps, ticks, groups, n_x, n_y, n_out, *refs):
    refs = list(refs)
    take = lambda count: [refs.pop(0) for _ in range(count)]
    (s_ref,) = take(1)
    xs, ys = take(n_x), take(n_y)
    (full_ref,) = take(1)
    outs = take(n_out)
    own, recv, load_sem, *line_sems = take(9)
    bits = dp.bit_length() - 1
    xbuf, ybuf, tiles = take(3)
    recvs = take(bits)
    rest = take(7)
    k, me = lax.axis_index(AX), lax.axis_index(DP)
    line = LineSum(n, chunks, full_ref, own, recv, *line_sems)
    halving = HalvingSum(dp, groups, xs, ys, outs, xbuf, ybuf, tiles, recvs, *rest)

    def load(c, j):
        return pltpu.make_async_copy(s_ref.at[pl.ds(pl.multiple_of(c * line.rows, line.rows), line.rows), pl.ds(j * line.cols, line.cols)], own.at[c, j], load_sem.at[c, j])

    for c in range(chunks):
        for j in range(n):
            load(c, j).start()
    halving.prologue()
    greet([(k > 0, {AX: k - 1}), (k < n - 1, {AX: k + 1})] + [(me >= 0, {DP: halving.partner(b)}) for b in range(bits)])

    def body(i, _):
        for e in range(steps + ticks):
            before = e * steps // (steps + ticks)
            if (e + 1) * steps // (steps + ticks) > before:
                c = steps * i + before

                @pl.when(c < chunks)
                def _(c=c):
                    for j in range(n):
                        load(c, j).wait()

                line.step(c)
            else:
                place = e - before
                halving.tick(ticks * i + place, place, ticks)
        return 0

    lax.fori_loop(0, max(-(-(chunks + 2 * (n - 1)) // steps), -(-(halving.total + bits) // ticks)), body, 0)
    line.drain()
    halving.drain(ticks)


def back_sums(s, xs, ys, groups, chunks=16, slots=6, steps=4, ticks=5):
    n, dp = lax.axis_size(AX), lax.axis_size(DP)
    bits = dp.bit_length() - 1
    total, width = s.shape
    rows, cols = total // chunks, width // n
    w = width // dp
    dma = pltpu.SemaphoreType.DMA
    out_shapes = [None] * len(groups)
    for g in groups:
        size = xs[g["x"]].shape[1]
        out_shapes[g["out"]] = jax.ShapeDtypeStruct((w, size) if g["turned"] else (size, w), jnp.float32)
    anywhere = pl.BlockSpec(memory_space=pl.ANY)
    vmem = pltpu.VMEM
    low = jnp.bfloat16
    return pl.pallas_call(
        functools.partial(sums_kernel, n, dp, chunks, steps, ticks, groups, len(xs), len(ys), len(out_shapes)),
        out_shape=[jax.ShapeDtypeStruct(s.shape, s.dtype)] + out_shapes,
        in_specs=[anywhere] * (1 + len(xs) + len(ys)),
        out_specs=[anywhere] * (1 + len(out_shapes)),
        scratch_shapes=[
            vmem((chunks, n, rows, cols), low), vmem((chunks, n + 1, rows, cols), low),
            dma((chunks, n)), dma((chunks, n)), dma((chunks, n + 1)), dma((chunks, n)), dma((chunks, n)), dma((chunks, n)), dma((chunks,)),
            vmem((2, total, STRIP), low), vmem((2, total, width), low), vmem((slots, *(2,) * bits, STRIP, w), low),
            *[vmem((slots, *(2,) * (bits - 1 - level), STRIP, w), low) for level in range(bits)],
            vmem((2, STRIP, w), jnp.float32), vmem((2, w, STRIP), jnp.float32),
            dma((2,)), dma((2,)), dma((bits, slots)), dma((bits, slots)), dma((2,)),
        ],
        compiler_params=pltpu.CompilerParams(collective_id=0, has_side_effects=True, vmem_limit_bytes=VMEM_CAP),
        name="back_sums",
    )(s, *xs, *ys)


def exact_gelu(values):
    return jax.nn.gelu(values, approximate=False)


def mul(a, b):
    return jnp.dot(a, b, preferred_element_type=jnp.float32)


def on_device(tokens, segments, positions, ln1_gain, ln1_bias, ln2_gain, ln2_bias, qkv_weight, dense_weight, fc1_weight, fc2_weight, upstream):
    low = jnp.bfloat16
    total_rows, width = tokens.shape
    up = lax.all_gather(upstream, AX, axis=1, tiled=True)
    rot = rot_tables(positions)
    h_one, h_two, qkv = project(tokens, ln1_gain, ln1_bias, ln2_gain, ln2_bias, rot, qkv_weight)
    attended, lse = attend(qkv, segments, 1024)
    pre_act = mul(h_two, fc1_weight)
    hidden_wide, pull = jax.vjp(exact_gelu, pre_act)
    hidden = hidden_wide.astype(low)
    slope = pull(jnp.ones_like(pre_act))[0].astype(low)
    partial_out = (mul(attended, dense_weight) + mul(hidden, fc2_weight)).astype(low)
    own_sum = lax.psum_scatter(partial_out, AX, scatter_dimension=1, tiled=True)
    share = width // lax.axis_size(AX)
    own_x = lax.dynamic_slice_in_dim(tokens, lax.axis_index(AX) * share, share, 1)
    output = (own_x.astype(jnp.float32) + own_sum.astype(jnp.float32)).astype(low)

    grad_att = mul(up, dense_weight.T).astype(low)
    grad_qkv = attend_back(qkv, grad_att, attended, segments, lse, rot)
    grad_pre = (mul(up, fc2_weight.T) * slope.astype(jnp.float32)).astype(low)
    grad_h_two = mul(grad_pre, fc1_weight.T)
    grad_h_one = mul(grad_qkv, qkv_weight.T)
    partial_s = (grad_h_one * ln1_gain + grad_h_two * ln2_gain).astype(low)
    x = tokens.astype(jnp.float32)
    center = x - jnp.mean(x, axis=-1, keepdims=True)
    inv_scale = lax.rsqrt(jnp.mean(center * center, axis=-1, keepdims=True) + 1e-05)
    normed = center * inv_scale
    norm_part = jnp.stack([
        jnp.sum(grad_h_one * normed, axis=0),
        jnp.sum(grad_h_one, axis=0),
        jnp.sum(grad_h_two * normed, axis=0),
        jnp.sum(grad_h_two, axis=0),
    ])
    groups = [
        dict(x=0, y=0, count=grad_pre.shape[1] // STRIP, turned=True, out=2),
        dict(x=1, y=1, count=hidden.shape[1] // STRIP, turned=False, out=3),
        dict(x=2, y=1, count=attended.shape[1] // STRIP, turned=False, out=1),
        dict(x=3, y=2, count=grad_qkv.shape[1] // STRIP, turned=True, out=0),
    ]
    s, qkv_grad, dense_grad, fc1_grad, fc2_grad = back_sums(
        partial_s, [grad_pre, hidden, attended, grad_qkv], [h_two, up, h_one], groups)
    s = s.astype(jnp.float32)
    input_grad = up.astype(jnp.float32) + inv_scale * (
        s - jnp.mean(s, axis=-1, keepdims=True) - normed * jnp.mean(s * normed, axis=-1, keepdims=True))
    norm_grads = lax.psum_scatter(lax.psum(norm_part, AX), DP, scatter_dimension=1, tiled=True)
    return (
        output, input_grad, qkv_grad, dense_grad, fc1_grad, fc2_grad,
        norm_grads[0], norm_grads[1], norm_grads[2], norm_grads[3],
    )


def solution(mesh):
    in_specs = (
        P("dp", None),
        P("dp"),
        P("dp"),
        P(),
        P(),
        P(),
        P(),
        P(None, "tensor"),
        P("tensor", None),
        P(None, "tensor"),
        P("tensor", None),
        P("dp", "tensor"),
    )
    out_specs = (
        P("dp", "tensor"),
        P("dp", None),
        P("dp", "tensor"),
        P("tensor", "dp"),
        P("dp", "tensor"),
        P("tensor", "dp"),
        P("dp"),
        P("dp"),
        P("dp"),
        P("dp"),
    )
    return jax.shard_map(
        on_device, mesh=mesh, in_specs=in_specs, out_specs=out_specs, check_vma=False
    )
```

```python
import functools
import itertools

import jax
import jax.numpy as jnp
from jax import lax
from jax.experimental import pallas as pl
from jax.experimental.pallas import tpu as pltpu
from jax.sharding import PartitionSpec as P

HEAD_DIM = 256
ROT_DIM = 64
SEQ_LEN = 2048
LANES = 128
VMEM_CAP = 60 * 2**20
NT = (((1,), (1,)), ((), ()))
TN = (((0,), (0,)), ((), ()))


def rot_tables(positions):
    half = ROT_DIM // 2
    steps_up = jnp.arange(half).astype(jnp.float32) * 2.0 / ROT_DIM
    inverse = jnp.power(jnp.float32(10000.0), -steps_up)
    angle = positions.astype(jnp.float32)[:, None] * inverse[None, :]
    cos, sin = jnp.cos(angle), jnp.sin(angle)
    zero = jnp.zeros_like(sin)
    rest = jnp.zeros((positions.shape[0], LANES - ROT_DIM), jnp.float32)
    cos_t = jnp.concatenate([cos, cos, rest + 1.0], -1)
    sin_up = jnp.concatenate([-sin, zero, rest], -1)
    sin_down = jnp.concatenate([zero, sin, rest], -1)
    return cos_t, sin_up, sin_down


def rotate_tile(u, cos_t, sin_up, sin_down):
    half = ROT_DIM // 2
    return u * cos_t + pltpu.roll(u, LANES - half, 1) * sin_up + pltpu.roll(u, half, 1) * sin_down


def rotate_back_tile(g, cos_t, sin_up, sin_down):
    half = ROT_DIM // 2
    return g * cos_t + pltpu.roll(g * sin_down, LANES - half, 1) + pltpu.roll(g * sin_up, half, 1)


def pre_kernel(x_ref, g1_ref, b1_ref, g2_ref, b2_ref, cos_ref, su_ref, sd_ref, w_ref, h1_ref, h2_ref, qkv_ref):
    x = x_ref[...].astype(jnp.float32)
    center = x - jnp.mean(x, axis=-1, keepdims=True)
    inv = lax.rsqrt(jnp.mean(center * center, axis=-1, keepdims=True) + 1e-05)
    normed = center * inv
    h1 = (normed * g1_ref[...] + b1_ref[...]).astype(jnp.bfloat16)
    h1_ref[...] = h1
    h2_ref[...] = (normed * g2_ref[...] + b2_ref[...]).astype(jnp.bfloat16)
    cos_t, su, sd = cos_ref[...], su_ref[...], sd_ref[...]
    for b in range(w_ref.shape[1] // HEAD_DIM):
        cols = slice(b * HEAD_DIM, (b + 1) * HEAD_DIM)
        y = jnp.dot(h1, w_ref[:, cols], preferred_element_type=jnp.float32)
        if b % 3 < 2:
            qkv_ref[:, b * HEAD_DIM : b * HEAD_DIM + LANES] = rotate_tile(y[:, :LANES], cos_t, su, sd).astype(jnp.bfloat16)
            qkv_ref[:, b * HEAD_DIM + LANES : (b + 1) * HEAD_DIM] = y[:, LANES:].astype(jnp.bfloat16)
        else:
            qkv_ref[:, cols] = y.astype(jnp.bfloat16)


def project(tokens, g1, b1, g2, b2, rot, w, rows=256):
    total, width = tokens.shape
    rows = min(rows, total)
    row_blk = lambda cols: pl.BlockSpec((rows, cols), lambda i: (i, 0))
    vec = pl.BlockSpec((1, width), lambda i: (0, 0))
    cols = w.shape[1]
    return pl.pallas_call(
        pre_kernel,
        grid=(total // rows,),
        in_specs=[row_blk(width), vec, vec, vec, vec, row_blk(LANES), row_blk(LANES), row_blk(LANES),
                  pl.BlockSpec((width, cols), lambda i: (0, 0), pipeline_mode=pl.Buffered(1))],
        out_specs=[row_blk(width), row_blk(width), row_blk(cols)],
        out_shape=[jax.ShapeDtypeStruct((total, width), jnp.bfloat16)] * 2 + [jax.ShapeDtypeStruct((total, cols), jnp.bfloat16)],
        compiler_params=pltpu.CompilerParams(vmem_limit_bytes=VMEM_CAP),
        cost_estimate=pl.CostEstimate(flops=2 * total * width * cols, bytes_accessed=6 * total * width + 2 * cols * (width + total), transcendentals=0),
        name="norm_project",
    )(tokens, g1[None], b1[None], g2[None], b2[None], *rot, w)


def attend_kernel(block, heads, qkv_ref, drow_ref, dcol_ref, o_ref, lse_ref, v_turned):
    i = pl.program_id(1)
    scale = HEAD_DIM ** (-0.5)
    part = lambda h, c: slice((3 * h + c) * HEAD_DIM, (3 * h + c + 1) * HEAD_DIM)

    @pl.when(i == 0)
    def _():
        for h in range(heads):
            v_turned[h] = qkv_ref[:, part(h, 2)].T

    here = pl.ds(pl.multiple_of(i * block, block), block)
    queries = [qkv_ref[here, part(h, 0)] for h in range(heads)]
    docs_q = drow_ref[...]
    gap = lax.broadcasted_iota(jnp.int32, (block, block), 1) - lax.broadcasted_iota(jnp.int32, (block, block), 0)

    def body(j, carry):
        rows = pl.ds(pl.multiple_of(j * block, block), block)
        allowed = (docs_q == dcol_ref[rows, :]) & (gap >= (j - i) * block)
        new = []
        for h in range(heads):
            m, l, acc = carry[h]
            s = lax.dot_general(qkv_ref[rows, part(h, 1)], queries[h], NT, preferred_element_type=jnp.float32) * scale
            s = jnp.where(allowed, s, -1e30)
            m_new = jnp.maximum(m, jnp.max(s, axis=0, keepdims=True))
            p = jnp.exp(s - m_new)
            alpha = jnp.exp(m - m_new)
            l = l * alpha + jnp.sum(p, axis=0, keepdims=True)
            acc = acc * alpha + jnp.dot(v_turned[h, :, rows], p.astype(jnp.bfloat16), preferred_element_type=jnp.float32)
            new.append((m_new, l, acc))
        return tuple(new)

    start = (jnp.full((1, block), -1e30, jnp.float32), jnp.zeros((1, block), jnp.float32), jnp.zeros((HEAD_DIM, block), jnp.float32))
    carry = lax.fori_loop(0, i + 1, body, (start,) * heads)
    for h in range(heads):
        m, l, acc = carry[h]
        o_ref[:, h * HEAD_DIM : (h + 1) * HEAD_DIM] = (acc * (1.0 / l)).T.astype(jnp.bfloat16)
        lse_ref[h] = m + jnp.log(l)


def attend(qkv, docs, block=512):
    total, cols = qkv.shape
    heads = cols // (3 * HEAD_DIM)
    seqs = total // SEQ_LEN
    n = SEQ_LEN // block
    return pl.pallas_call(
        functools.partial(attend_kernel, block, heads),
        grid=(seqs, n),
        in_specs=[
            pl.BlockSpec((SEQ_LEN, cols), lambda s, i: (s, 0)),
            pl.BlockSpec((1, block), lambda s, i: (0, s * n + i)),
            pl.BlockSpec((SEQ_LEN, 1), lambda s, i: (s, 0)),
        ],
        out_specs=[pl.BlockSpec((block, heads * HEAD_DIM), lambda s, i: (s * n + i, 0)),
                   pl.BlockSpec((heads, 1, block), lambda s, i: (0, 0, s * n + i))],
        out_shape=[jax.ShapeDtypeStruct((total, heads * HEAD_DIM), jnp.bfloat16), jax.ShapeDtypeStruct((heads, 1, total), jnp.float32)],
        scratch_shapes=[pltpu.VMEM((heads, HEAD_DIM, SEQ_LEN), jnp.bfloat16)],
        compiler_params=pltpu.CompilerParams(vmem_limit_bytes=VMEM_CAP),
        cost_estimate=pl.CostEstimate(flops=2 * total * SEQ_LEN * heads * HEAD_DIM, bytes_accessed=4 * total * cols, transcendentals=total * SEQ_LEN),
        name="attend",
    )(qkv, docs[None, :], docs[:, None])


def attend_back_kernel(block, n, heads, qkv_ref, g_ref, o_ref, dcol_ref, drow_ref, lse_ref, cos_ref, su_ref, sd_ref, out_ref, dk, dv):
    i = pl.program_id(1)
    scale = HEAD_DIM ** (-0.5)
    part = lambda h, c: slice((3 * h + c) * HEAD_DIM, (3 * h + c + 1) * HEAD_DIM)
    cols = lambda h: slice(h * HEAD_DIM, (h + 1) * HEAD_DIM)

    @pl.when(i == 0)
    def _():
        dk[...] = jnp.zeros_like(dk)
        dv[...] = jnp.zeros_like(dv)

    here = pl.ds(pl.multiple_of(i * block, block), block)
    docs_q = drow_ref[...]
    ones = jnp.ones((8, HEAD_DIM), jnp.float32)
    queries = [qkv_ref[here, part(h, 0)] for h in range(heads)]
    grads = [g_ref[:, cols(h)] for h in range(heads)]
    deltas = [
        lax.dot_general(ones, grads[h].astype(jnp.float32) * o_ref[:, cols(h)].astype(jnp.float32), NT,
                        precision=lax.Precision.HIGHEST, preferred_element_type=jnp.float32)[:1]
        for h in range(heads)
    ]
    gap = lax.broadcasted_iota(jnp.int32, (block, block), 1) - lax.broadcasted_iota(jnp.int32, (block, block), 0)

    def body(j, carry):
        rows = pl.ds(pl.multiple_of(j * block, block), block)
        allowed = (docs_q == dcol_ref[rows, :]) & (gap >= (j - i) * block)
        new = []
        for h in range(heads):
            q, g = queries[h], grads[h]
            k = qkv_ref[rows, part(h, 1)]
            s = lax.dot_general(k, q, NT, preferred_element_type=jnp.float32) * scale
            p = jnp.exp(jnp.where(allowed, s - lse_ref[h], -1e30))
            dp = lax.dot_general(qkv_ref[rows, part(h, 2)], g, NT, preferred_element_type=jnp.float32)
            ds = (p * (dp - deltas[h]) * scale).astype(jnp.bfloat16)
            dv[rows, cols(h)] += jnp.dot(p.astype(jnp.bfloat16), g, preferred_element_type=jnp.float32)
            dk[rows, cols(h)] += jnp.dot(ds, q, preferred_element_type=jnp.float32)
            new.append(carry[h] + lax.dot_general(ds, k, TN, preferred_element_type=jnp.float32))
        return tuple(new)

    dq = lax.fori_loop(0, i + 1, body, (jnp.zeros((block, HEAD_DIM), jnp.float32),) * heads)

    def put(rows, first, val):
        rot = (cos_ref[rows, :], su_ref[rows, :], sd_ref[rows, :])
        out_ref[rows, first : first + LANES] = rotate_back_tile(val[:, :LANES], *rot).astype(jnp.bfloat16)
        out_ref[rows, first + LANES : first + HEAD_DIM] = val[:, LANES:].astype(jnp.bfloat16)

    for h in range(heads):
        put(here, 3 * h * HEAD_DIM, dq[h])

    @pl.when(i == n - 1)
    def _():
        for h in range(heads):
            for b in range(n):
                rows = slice(b * block, (b + 1) * block)
                put(rows, (3 * h + 1) * HEAD_DIM, dk[rows, cols(h)])
                out_ref[rows, part(h, 2)] = dv[rows, cols(h)].astype(jnp.bfloat16)


def attend_back(qkv, grad_att, attended, docs, lse, rot, block=512):
    total, cols = qkv.shape
    heads = cols // (3 * HEAD_DIM)
    seqs = total // SEQ_LEN
    n = SEQ_LEN // block
    whole = pl.BlockSpec((SEQ_LEN, cols), lambda s, i: (s, 0))
    mine = pl.BlockSpec((block, heads * HEAD_DIM), lambda s, i: (s * n + i, 0))
    table = pl.BlockSpec((SEQ_LEN, LANES), lambda s, i: (s, 0))
    return pl.pallas_call(
        functools.partial(attend_back_kernel, block, n, heads),
        grid=(seqs, n),
        in_specs=[
            whole, mine, mine,
            pl.BlockSpec((SEQ_LEN, 1), lambda s, i: (s, 0)),
            pl.BlockSpec((1, block), lambda s, i: (0, s * n + i)),
            pl.BlockSpec((heads, 1, block), lambda s, i: (0, 0, s * n + i)),
            table, table, table,
        ],
        out_specs=whole,
        out_shape=jax.ShapeDtypeStruct((total, cols), jnp.bfloat16),
        scratch_shapes=[pltpu.VMEM((SEQ_LEN, heads * HEAD_DIM), jnp.float32)] * 2,
        compiler_params=pltpu.CompilerParams(vmem_limit_bytes=VMEM_CAP),
        cost_estimate=pl.CostEstimate(flops=5 * total * SEQ_LEN * heads * HEAD_DIM, bytes_accessed=8 * total * cols, transcendentals=total * SEQ_LEN),
        name="attend_back",
    )(qkv, grad_att, attended, docs[:, None], docs[None, :], lse, *rot)


def terms_kernel(x_ref, gq_ref, gh2_ref, g1_ref, g2_ref, w_ref, s_ref, sums_ref):
    @pl.when(pl.program_id(0) == 0)
    def _():
        sums_ref[...] = jnp.zeros_like(sums_ref)

    x = x_ref[...].astype(jnp.float32)
    center = x - jnp.mean(x, axis=-1, keepdims=True)
    inv = lax.rsqrt(jnp.mean(center * center, axis=-1, keepdims=True) + 1e-05)
    gq = gq_ref[...]
    tile = 512
    for t in range(0, x.shape[1], tile):
        at = slice(t, t + tile)
        gh1 = lax.dot_general(gq, w_ref[at, :], NT, preferred_element_type=jnp.float32)
        gh2 = gh2_ref[:, at].astype(jnp.float32)
        normed = center[:, at] * inv
        s_ref[:, at] = (gh1 * g1_ref[:, at] + gh2 * g2_ref[:, at]).astype(jnp.bfloat16)
        for row, value in enumerate((gh1 * normed, gh1, gh2 * normed, gh2)):
            sums_ref[row : row + 1, at] += jnp.sum(value, axis=0, keepdims=True)


def input_terms(tokens, grad_qkv, grad_h2, g1, g2, w, rows=256):
    total, width = tokens.shape
    rows = min(rows, total)
    cols = w.shape[1]
    row_blk = lambda c: pl.BlockSpec((rows, c), lambda i: (i, 0))
    vec = pl.BlockSpec((1, width), lambda i: (0, 0))
    return pl.pallas_call(
        terms_kernel,
        grid=(total // rows,),
        in_specs=[row_blk(width), row_blk(cols), row_blk(width), vec, vec, pl.BlockSpec(w.shape, lambda i: (0, 0), pipeline_mode=pl.Buffered(1))],
        out_specs=[row_blk(width), pl.BlockSpec((8, width), lambda i: (0, 0))],
        out_shape=[jax.ShapeDtypeStruct((total, width), jnp.bfloat16), jax.ShapeDtypeStruct((8, width), jnp.float32)],
        compiler_params=pltpu.CompilerParams(vmem_limit_bytes=VMEM_CAP),
        cost_estimate=pl.CostEstimate(flops=2 * total * width * cols, bytes_accessed=6 * total * width + 2 * cols * (width + total), transcendentals=0),
        name="input_terms",
    )(tokens, grad_qkv, grad_h2, g1[None], g2[None], w)


def finish_kernel(x_ref, s_ref, up_ref, out_ref):
    x = x_ref[...].astype(jnp.float32)
    center = x - jnp.mean(x, axis=-1, keepdims=True)
    inv = lax.rsqrt(jnp.mean(center * center, axis=-1, keepdims=True) + 1e-05)
    s = s_ref[...].astype(jnp.float32)
    slope = jnp.mean(s * center, axis=-1, keepdims=True) * (inv * inv)
    out_ref[...] = up_ref[...].astype(jnp.float32) + inv * (s - jnp.mean(s, axis=-1, keepdims=True) - center * slope)


def finish(tokens, s, up, rows=256):
    total, width = tokens.shape
    block = pl.BlockSpec((min(rows, total), width), lambda i: (i, 0))
    return pl.pallas_call(
        finish_kernel,
        grid=(total // min(rows, total),),
        in_specs=[block] * 3,
        out_specs=block,
        out_shape=jax.ShapeDtypeStruct((total, width), jnp.float32),
        compiler_params=pltpu.CompilerParams(vmem_limit_bytes=VMEM_CAP),
        cost_estimate=pl.CostEstimate(flops=10 * total * width, bytes_accessed=10 * total * width, transcendentals=0),
        name="finish",
    )(tokens, s, up)


AX = "tensor"
DP = "dp"
MESH = pl.DeviceIdType.MESH
STRIP = 256


def greet(peers):
    barrier = pltpu.get_barrier_semaphore()
    count = 0
    for cond, device in peers:
        @pl.when(cond)
        def _(device=device):
            pl.semaphore_signal(barrier, inc=1, device_id=device, device_id_type=MESH)
        count = count + jnp.asarray(cond).astype(jnp.int32)
    pl.semaphore_wait(barrier, count)


def within(c, count):
    return (c >= 0) & (c < count)


def blend(first, second):
    both = [(place / len(one), which, entry) for which, one in enumerate((first, second)) for place, entry in enumerate(one)]
    return [entry for _, _, entry in sorted(both, key=lambda e: e[:2])]


class LineSum:
    def __init__(self, n, chunks, full_ref, own, recv, rs_send, rs_recv, ag_right, ag_left, ag_recv, store_sem):
        self.n, self.chunks, self.full_ref, self.own, self.recv = n, chunks, full_ref, own, recv
        self.rs_send, self.rs_recv, self.ag_send, self.ag_recv, self.store_sem = rs_send, rs_recv, (ag_right, ag_left), ag_recv, store_sem
        self.k = lax.axis_index(AX)
        self.rows, self.cols = own.shape[2], own.shape[3]

    def block(self, c, j):
        return self.full_ref.at[pl.ds(pl.multiple_of(c * self.rows, self.rows), self.rows), pl.ds(j * self.cols, self.cols)]

    def copy(self, src, dst, send, recv, right):
        return pltpu.make_async_remote_copy(src, dst, send, recv, device_id={AX: self.k + 1 if right else self.k - 1}, device_id_type=MESH)

    def scatter_copy(self, c, j, right):
        slot = j if right else jnp.where(self.k - 1 == j, self.n, j)
        return self.copy(self.own.at[c, j], self.recv.at[c, slot], self.rs_send.at[c, j], self.rs_recv.at[c, slot], right)

    def scatter_arrived(self, c, slot):
        dst = self.recv.at[c, slot]
        pltpu.make_async_copy(dst, dst, self.rs_recv.at[c, slot]).wait()

    def gather_copy(self, c, j, right, src=None):
        block = self.block(c, j)
        return self.copy(block if src is None else src, block, self.ag_send[0 if right else 1].at[c, j], self.ag_recv.at[c, j], right)

    def gather_arrived(self, c, j):
        block = self.block(c, j)
        pltpu.make_async_copy(block, block, self.ag_recv.at[c, j]).wait()

    def store(self, c, j):
        return pltpu.make_async_copy(self.own.at[c, j], self.block(c, j), self.store_sem.at[c])

    def pieces(self, i):
        return [functools.partial(self.pass_on, i, p) for p in range(self.n)] + [functools.partial(self.close, i)]

    def pass_on(self, i, p):
        n, k, chunks = self.n, self.k, self.chunks
        for right in (True, False):
            j = p if right else n - 1 - p
            dist = (k - j) if right else (j - k)
            onward = (k < n - 1) if right else (k > 0)
            behind = (k > 0) if right else (k < n - 1)
            c_gather = i - (n - 1) - dist
            c_scatter = i - (k if right else n - 1 - k)

            @pl.when((dist > 0) & within(c_gather, chunks))
            def _(j=j, right=right, c=c_gather, onward=onward):
                self.gather_arrived(c, j)

                @pl.when(onward)
                def _():
                    self.gather_copy(c, j, right).start()

            @pl.when((dist < 0) & within(c_scatter, chunks))
            def _(j=j, right=right, c=c_scatter, behind=behind):
                @pl.when(behind)
                def _():
                    self.scatter_arrived(c, j)
                    self.own[c, j] = self.own[c, j] + self.recv[c, j]

                self.scatter_copy(c, j, right).start()

    def close(self, i):
        n, k, chunks = self.n, self.k, self.chunks
        c = i - (n - 1)
        for j in range(n):
            @pl.when((k == j) & within(c, chunks))
            def _(j=j):
                total = self.own[c, j].astype(jnp.float32)
                if j > 0:
                    self.scatter_arrived(c, j)
                    total = total + self.recv[c, j].astype(jnp.float32)
                if j < n - 1:
                    self.scatter_arrived(c, n)
                    total = total + self.recv[c, n].astype(jnp.float32)
                self.own[c, j] = total.astype(self.own.dtype)
                self.store(c, j).start()
                if j < n - 1:
                    self.gather_copy(c, j, True, self.own.at[c, j]).start()
                if j > 0:
                    self.gather_copy(c, j, False, self.own.at[c, j]).start()

    def drain(self):
        n, k = self.n, self.k

        def one(c, _):
            for j in range(n):
                @pl.when(k < j)
                def _(j=j):
                    self.scatter_copy(c, j, True).wait_send()

                    @pl.when(k > 0)
                    def _():
                        self.gather_copy(c, j, False).wait_send()

                @pl.when(k > j)
                def _(j=j):
                    self.scatter_copy(c, j, False).wait_send()

                    @pl.when(k < n - 1)
                    def _():
                        self.gather_copy(c, j, True).wait_send()

                @pl.when(k == j)
                def _(j=j):
                    self.store(c, j).wait()
                    if j < n - 1:
                        self.gather_copy(c, j, True, self.own.at[c, j]).wait_send()
                    if j > 0:
                        self.gather_copy(c, j, False, self.own.at[c, j]).wait_send()
            return 0

        lax.fori_loop(0, self.chunks, one, 0)


class HalvingSum:
    def __init__(self, dp, groups, xs, ys, outs, xbuf, ybuf, tiles, recvs, stage, stage_turned, x_sem, y_sem, send_sem, recv_sem, out_sem):
        self.dp, self.bits = dp, dp.bit_length() - 1
        self.groups, self.xs, self.ys, self.outs = groups, xs, ys, outs
        self.xbuf, self.ybuf, self.tiles, self.recvs = xbuf, ybuf, tiles, recvs
        self.stage, self.stage_turned = stage, stage_turned
        self.x_sem, self.y_sem, self.send_sem, self.recv_sem, self.out_sem = x_sem, y_sem, send_sem, recv_sem, out_sem
        self.me = lax.axis_index(DP)
        self.slots = tiles.shape[0]
        self.width = tiles.shape[-1]
        self.first = [sum(g["count"] for g in groups[:i]) for i in range(len(groups) + 1)]
        self.total = self.first[-1]
        self.lags = [1 + 2 * level for level in range(self.bits)]

    def bit(self, b):
        return lax.rem(lax.div(self.me, 2**b), 2)

    def partner(self, b):
        return self.me + (1 - 2 * self.bit(b)) * 2**b

    def order(self, odd):
        rest = list(range(1, self.bits))
        return [0] + (rest[1:] + rest[:1] if odd else rest)

    def pick(self, odd, level, value):
        done = self.order(odd)[:level]
        now = self.order(odd)[level]
        return tuple(0 if b in done else value if b == now else slice(None) for b in range(self.bits))

    def in_group(self, t, g):
        return (t >= self.first[g]) & (t < self.first[g + 1])

    def x_copies(self, t):
        for g, group in enumerate(self.groups):
            at = pl.ds(pl.multiple_of((t - self.first[g]) * STRIP, STRIP), STRIP)
            slot = lax.rem(t, 2)
            yield self.in_group(t, g), pltpu.make_async_copy(self.xs[group["x"]].at[:, at], self.xbuf.at[slot], self.x_sem.at[slot])

    def x_start(self, t):
        for cond, copy in self.x_copies(t):
            @pl.when(cond)
            def _(copy=copy):
                copy.start()

    def x_wait(self, t):
        slot = lax.rem(t, 2)
        pltpu.make_async_copy(self.xbuf.at[slot], self.xbuf.at[slot], self.x_sem.at[slot]).wait()

    def y_copy(self, g):
        y = self.groups[g]["y"]
        return pltpu.make_async_copy(self.ys[y], self.ybuf.at[y % 2], self.y_sem.at[y % 2])

    def send(self, u, odd, level):
        slot = lax.rem(u, self.slots)
        return pltpu.make_async_remote_copy(
            self.tiles.at[(slot, *self.pick(odd, level, 1))], self.recvs[level].at[slot],
            self.send_sem.at[level, slot], self.recv_sem.at[level, slot],
            device_id={DP: self.partner(self.order(odd)[level])}, device_id_type=MESH)

    def out_copies(self, u):
        slot = lax.rem(u, 2)
        for g, group in enumerate(self.groups):
            at = pl.ds(pl.multiple_of((u - self.first[g]) * STRIP, STRIP), STRIP)
            out = self.outs[group["out"]]
            if group["turned"]:
                yield self.in_group(u, g), pltpu.make_async_copy(self.stage_turned.at[slot], out.at[:, at], self.out_sem.at[slot])
            else:
                yield self.in_group(u, g), pltpu.make_async_copy(self.stage.at[slot], out.at[at, :], self.out_sem.at[slot])

    def out_wait(self, u):
        for cond, copy in self.out_copies(u):
            @pl.when(cond)
            def _(copy=copy):
                copy.wait()

    def prologue(self):
        self.x_start(jnp.int32(0))
        self.y_copy(0).start()
        for g in range(1, len(self.groups)):
            if self.groups[g]["y"] == 1:
                self.y_copy(g).start()
                break

    def pieces(self, t, place, period, parts=4):
        odd = place % 2
        share = max(self.dp // parts, 1)
        spans = [range(first, first + share) for first in range(0, self.dp, share)]
        return [functools.partial(self.halve, t, place, period)] + [
            functools.partial(self.multiply, t, place, period, span, span[0] == 0, span[-1] == self.dp - 1) for span in spans]

    def halve(self, t, place, period):
        for level in range(self.bits - 1, -1, -1):
            u = t - self.lags[level]
            u_odd = (place - self.lags[level]) % period % 2

            @pl.when(within(u, self.total))
            def _(u=u, u_odd=u_odd, level=level):
                slot = lax.rem(u, self.slots)
                got = self.recvs[level]
                pltpu.make_async_copy(got.at[slot], got.at[slot], self.recv_sem.at[level, slot]).wait()
                keep = (slot, *self.pick(u_odd, level, 0))
                if level < self.bits - 1:
                    left = [range(2) if isinstance(p, slice) else (p,) for p in keep[1:]]
                    for flat, idx in enumerate(itertools.product(*left)):
                        pos = tuple(int(b) for b in format(flat, "b").zfill(self.bits - 1 - level))
                        self.tiles[(slot, *idx)] = self.tiles[(slot, *idx)] + got[(slot, *pos)]
                    self.send(u, u_odd, level + 1).start()
                else:
                    @pl.when(u >= 2)
                    def _():
                        self.out_wait(u - 2)

                    value = self.tiles[keep].astype(jnp.float32) + got[slot].astype(jnp.float32)
                    for g, group in enumerate(self.groups):
                        @pl.when(self.in_group(u, g))
                        def _(group=group):
                            if group["turned"]:
                                self.stage_turned[lax.rem(u, 2)] = value.T
                            else:
                                self.stage[lax.rem(u, 2)] = value
                    for cond, copy in self.out_copies(u):
                        @pl.when(cond)
                        def _(copy=copy):
                            copy.start()

    def ready(self, t, place, period):
        @pl.when(t >= self.slots)
        def _():
            for level in range(self.bits):
                self.send(t - self.slots, (place - self.slots) % period % 2, level).wait_send()

        seen = []
        for g, group in enumerate(self.groups):
            if group["y"] in seen:
                continue
            seen.append(group["y"])

            @pl.when(t == self.first[g])
            def _(g=g, group=group):
                self.y_copy(g).wait()
                if group["y"] == 1:
                    for later in range(len(self.groups)):
                        if self.groups[later]["y"] == 2:
                            self.y_copy(later).start()
                            break

        @pl.when(t + 1 < self.total)
        def _():
            self.x_start(t + 1)

        self.x_wait(t)

    def multiply(self, t, place, period, span, opens, closes):
        @pl.when(within(t, self.total))
        def _():
            if opens:
                self.ready(t, place, period)
            slot = lax.rem(t, self.slots)
            y_slot = jnp.int32(0)
            for g, group in enumerate(self.groups):
                y_slot = jnp.where(t >= self.first[g], group["y"] % 2, y_slot)
            x = self.xbuf[lax.rem(t, 2)]
            for flat in span:
                idx = tuple((flat >> b) & 1 for b in range(self.bits))
                shard = sum((self.bit(b) + idx[b] * (1 - 2 * self.bit(b))) * 2**b for b in range(self.bits))
                at = pl.ds(pl.multiple_of(shard * self.width, self.width), self.width)
                self.tiles[(slot, *idx)] = lax.dot_general(x, self.ybuf[y_slot, :, at], TN, preferred_element_type=jnp.float32).astype(jnp.bfloat16)
            if closes:
                self.send(t, place % 2, 0).start()

    def drain(self, period):
        for u in range(self.total - self.slots, self.total):
            for level in range(self.bits):
                self.send(jnp.int32(u), u % period % 2, level).wait_send()
        for u in range(self.total - 2, self.total):
            self.out_wait(jnp.int32(u))


class SmallSum:
    def __init__(self, n, bits, partner, part_ref, out_ref, acc, dp_recv, line_send, line_recv, sems):
        self.n, self.bits, self.partner = n, bits, partner
        self.part_ref, self.out_ref, self.acc, self.dp_recv, self.line_send, self.line_recv = part_ref, out_ref, acc, dp_recv, line_send, line_recv
        self.dp_send_sem, self.dp_recv_sem, self.line_send_sem, self.line_recv_sem, self.own_sem = sems
        self.k, self.me = lax.axis_index(AX), lax.axis_index(DP)

    def first(self):
        return pltpu.make_async_copy(self.part_ref, self.acc, self.own_sem.at[0])

    def last(self):
        return pltpu.make_async_copy(self.dp_recv.at[0, :, pl.ds(0, self.out_ref.shape[1])], self.out_ref, self.own_sem.at[1])

    def swap(self, b):
        return pltpu.make_async_remote_copy(
            self.acc, self.dp_recv.at[b], self.dp_send_sem.at[b], self.dp_recv_sem.at[b], device_id={DP: self.partner(b)}, device_id_type=MESH)

    def onward(self, way):
        return pltpu.make_async_remote_copy(
            self.line_send.at[way], self.line_recv.at[way], self.line_send_sem.at[way], self.line_recv_sem.at[way],
            device_id={AX: self.k + 1 - 2 * way}, device_id_type=MESH)

    def step(self, i):
        n, k = self.n, self.k
        for b in range(self.bits + 1):
            @pl.when(i == b)
            def _(b=b):
                if b == 0:
                    self.first().wait()
                else:
                    self.swap(b - 1).wait()
                    self.acc[...] = self.acc[...] + self.dp_recv[b - 1]
                if b < self.bits:
                    self.swap(b).start()
        for way in range(2):
            place = k if way == 0 else n - 1 - k

            @pl.when(i == self.bits + 1 + place)
            def _(way=way, place=place):
                self.line_send[way] = self.acc[...]

                @pl.when(place > 0)
                def _():
                    got = self.line_recv.at[way]
                    pltpu.make_async_copy(got, got, self.line_recv_sem.at[way]).wait()
                    self.line_send[way] = self.acc[...] + self.line_recv[way]

                @pl.when(place < n - 1)
                def _():
                    self.onward(way).start()

        @pl.when(i == self.bits + 1 + n)
        def _():
            self.acc[...] = self.line_send[0] + self.line_send[1] - self.acc[...]
            part = self.out_ref.shape[1]
            self.dp_recv[0, :, :part] = self.acc[:, pl.ds(pl.multiple_of(self.me * part, part), part)]
            self.last().start()

    def drain(self):
        @pl.when(self.k < self.n - 1)
        def _():
            self.onward(0).wait_send()

        @pl.when(self.k > 0)
        def _():
            self.onward(1).wait_send()

        self.last().wait()


def sums_kernel(n, dp, chunks, steps, ticks, groups, n_x, n_y, n_out, *refs):
    refs = list(refs)
    take = lambda count: [refs.pop(0) for _ in range(count)]
    s_ref, part_ref = take(2)
    xs, ys = take(n_x), take(n_y)
    full_ref, sum_ref = take(2)
    outs = take(n_out)
    own, recv, load_sem, *line_sems = take(9)
    bits = dp.bit_length() - 1
    xbuf, ybuf, tiles = take(3)
    recvs = take(bits)
    rest = take(7)
    small_bufs, small_sems = take(4), take(5)
    k, me = lax.axis_index(AX), lax.axis_index(DP)
    line = LineSum(n, chunks, full_ref, own, recv, *line_sems)
    halving = HalvingSum(dp, groups, xs, ys, outs, xbuf, ybuf, tiles, recvs, *rest)
    small = SmallSum(n, bits, halving.partner, part_ref, sum_ref, *small_bufs, small_sems)
    small.first().start()

    def load(c, j):
        return pltpu.make_async_copy(s_ref.at[pl.ds(pl.multiple_of(c * line.rows, line.rows), line.rows), pl.ds(j * line.cols, line.cols)], own.at[c, j], load_sem.at[c, j])

    for c in range(chunks):
        for j in range(n):
            load(c, j).start()
    halving.prologue()
    greet([(k > 0, {AX: k - 1}), (k < n - 1, {AX: k + 1})] + [(me >= 0, {DP: halving.partner(b)}) for b in range(bits)])

    def loaded(c):
        @pl.when(c < chunks)
        def _():
            for j in range(n):
                load(c, j).wait()

    def body(i, _):
        lines, strips = [], []
        for e in range(steps):
            c = steps * i + e
            lines.append(functools.partial(loaded, c))
            lines += line.pieces(c)
            lines.append(functools.partial(small.step, c))
        for place in range(ticks):
            strips += halving.pieces(ticks * i + place, place, ticks)
        for piece in blend(lines, strips):
            piece()
        return 0

    lax.fori_loop(0, max(-(-(chunks + 2 * (n - 1)) // steps), -(-(halving.total + halving.lags[-1]) // ticks)), body, 0)
    line.drain()
    halving.drain(ticks)
    small.drain()


def back_sums(s, part, xs, ys, groups, chunks=16, slots=6, steps=2, ticks=3):
    n, dp = lax.axis_size(AX), lax.axis_size(DP)
    bits = dp.bit_length() - 1
    total, width = s.shape
    rows, cols = total // chunks, width // n
    w = width // dp
    dma = pltpu.SemaphoreType.DMA
    out_shapes = [None] * len(groups)
    for g in groups:
        size = xs[g["x"]].shape[1]
        out_shapes[g["out"]] = jax.ShapeDtypeStruct((w, size) if g["turned"] else (size, w), jnp.float32)
    anywhere = pl.BlockSpec(memory_space=pl.ANY)
    vmem = pltpu.VMEM
    low = jnp.bfloat16
    return pl.pallas_call(
        functools.partial(sums_kernel, n, dp, chunks, steps, ticks, groups, len(xs), len(ys), len(out_shapes)),
        out_shape=[jax.ShapeDtypeStruct(s.shape, s.dtype), jax.ShapeDtypeStruct((part.shape[0], w), jnp.float32)] + out_shapes,
        in_specs=[anywhere] * (2 + len(xs) + len(ys)),
        out_specs=[anywhere] * (2 + len(out_shapes)),
        scratch_shapes=[
            vmem((chunks, n, rows, cols), low), vmem((chunks, n + 1, rows, cols), low),
            dma((chunks, n)), dma((chunks, n)), dma((chunks, n + 1)), dma((chunks, n)), dma((chunks, n)), dma((chunks, n)), dma((chunks,)),
            vmem((2, total, STRIP), low), vmem((2, total, width), low), vmem((slots, *(2,) * bits, STRIP, w), low),
            *[vmem((slots, *(2,) * (bits - 1 - level), STRIP, w), low) for level in range(bits)],
            vmem((2, STRIP, w), jnp.float32), vmem((2, w, STRIP), jnp.float32),
            dma((2,)), dma((2,)), dma((bits, slots)), dma((bits, slots)), dma((2,)),
            vmem(part.shape, jnp.float32), vmem((bits, *part.shape), jnp.float32), vmem((2, *part.shape), jnp.float32), vmem((2, *part.shape), jnp.float32),
            dma((bits,)), dma((bits,)), dma((2,)), dma((2,)), dma((2,)),
        ],
        compiler_params=pltpu.CompilerParams(collective_id=0, has_side_effects=True, vmem_limit_bytes=VMEM_CAP),
        name="back_sums",
    )(s, part, *xs, *ys)


class LineFeed:
    def __init__(self, n, chunks, near_left, near_right, up_ref, own, recv, rs_send, rs_recv, ag_right, ag_left, ag_recv, finish):
        self.n, self.chunks = n, chunks
        self.near, self.up_ref, self.own, self.recv = (near_left, near_right), up_ref, own, recv
        self.rs_send, self.rs_recv, self.ag_send, self.ag_recv, self.finish = rs_send, rs_recv, (ag_right, ag_left), ag_recv, finish
        self.k = lax.axis_index(AX)
        self.rows, self.cols = own.shape[2], own.shape[3]

    def span(self, c):
        return pl.ds(pl.multiple_of(c * self.rows, self.rows), self.rows)

    def block(self, c, j):
        return self.up_ref.at[self.span(c), pl.ds(j * self.cols, self.cols)]

    def copy(self, src, dst, send, recv, right):
        return pltpu.make_async_remote_copy(src, dst, send, recv, device_id={AX: self.k + 1 if right else self.k - 1}, device_id_type=MESH)

    def scatter_copy(self, c, j, right):
        slot = j if right else jnp.where(self.k - 1 == j, self.n, j)
        return self.copy(self.own.at[c, j], self.recv.at[c, slot], self.rs_send.at[c, j], self.rs_recv.at[c, slot], right)

    def scatter_arrived(self, c, slot):
        dst = self.recv.at[c, slot]
        pltpu.make_async_copy(dst, dst, self.rs_recv.at[c, slot]).wait()

    def gather_copy(self, c, j, right, near):
        src = self.near[0 if right else 1].at[self.span(c), :] if near else self.block(c, j)
        return self.copy(src, self.block(c, j), self.ag_send[0 if right else 1].at[c, j], self.ag_recv.at[c, j], right)

    def gather_arrived(self, c, j):
        block = self.block(c, j)
        pltpu.make_async_copy(block, block, self.ag_recv.at[c, j]).wait()

    def step(self, i):
        n, k, chunks = self.n, self.k, self.chunks
        for p in range(n):
            for right in (True, False):
                j = p if right else n - 1 - p
                dist = (k - j) if right else (j - k)
                onward = (k < n - 1) if right else (k > 0)
                behind = (k > 0) if right else (k < n - 1)
                c_gather = i - (dist - 1)
                c_scatter = i - (k if right else n - 1 - k)

                @pl.when((dist == 1) & onward & within(i, chunks))
                def _(j=j, right=right):
                    self.gather_copy(i, j, right, True).start()

                @pl.when((dist > 1) & within(c_gather, chunks))
                def _(j=j, right=right, c=c_gather, onward=onward):
                    self.gather_arrived(c, j)

                    @pl.when(onward)
                    def _():
                        self.gather_copy(c, j, right, False).start()

                @pl.when((dist < 0) & within(c_scatter, chunks))
                def _(j=j, right=right, c=c_scatter, behind=behind):
                    @pl.when(behind)
                    def _():
                        self.scatter_arrived(c, j)
                        self.own[c, j] = self.own[c, j] + self.recv[c, j]

                    self.scatter_copy(c, j, right).start()

        c = i - (n - 1)
        for j in range(n):
            @pl.when((k == j) & within(c, chunks))
            def _(j=j):
                total = self.own[c, j].astype(jnp.float32)
                if j > 0:
                    self.scatter_arrived(c, j)
                    total = total + self.recv[c, j].astype(jnp.float32)
                if j < n - 1:
                    self.scatter_arrived(c, n)
                    total = total + self.recv[c, n].astype(jnp.float32)
                self.finish(c, j, total)

    def drain(self):
        n, k = self.n, self.k

        def one(c, _):
            for j in range(n):
                @pl.when(k < j)
                def _(j=j):
                    self.scatter_copy(c, j, True).wait_send()

                    @pl.when(k > 0)
                    def _():
                        self.gather_copy(c, j, False, False).wait_send()

                @pl.when(k > j)
                def _(j=j):
                    self.scatter_copy(c, j, False).wait_send()

                    @pl.when(k < n - 1)
                    def _():
                        self.gather_copy(c, j, True, False).wait_send()
            return 0

        lax.fori_loop(0, self.chunks, one, 0)


def gelu_and_slope(x):
    share = 0.5 * (1.0 + lax.erf(x * (0.5**0.5)))
    return x * share, share + x * (jnp.exp(-0.5 * x * x) * (2.0 * jnp.pi) ** -0.5)


class Stream:
    def __init__(self, hbm, slots, sem, inward):
        self.hbm, self.slots, self.sem, self.inward = hbm, slots, sem, inward
        self.rows = slots.shape[1]

    def copy(self, p):
        at = self.hbm.at[pl.ds(pl.multiple_of(p * self.rows, self.rows), self.rows), :]
        slot = lax.rem(p, 2)
        pair = (at, self.slots.at[slot]) if self.inward else (self.slots.at[slot], at)
        return pltpu.make_async_copy(*pair, self.sem.at[slot])


def feed_kernel(
    n, chunks, tile,
    h2_ref, att_ref, fc1_ref, fc2_ref, dense_ref, up_own_ref, left_ref, right_ref, x_ref,
    up_ref, hidden_ref, grad_pre_ref, grad_h2_ref, grad_att_ref, out_ref,
    own, recv, fc1, fc2, dense, x_own, h2_buf, att_buf, up_buf, hid_buf, gp_buf, gh_buf, ga_buf, slope,
    weight_sem, near_sem, h2_sem, att_sem, up_sem, hid_sem, gp_sem, gh_sem, ga_sem, out_sem, *line_sems,
):
    k = lax.axis_index(AX)
    low = jnp.bfloat16
    rows = h2_buf.shape[1]
    blocks = h2_ref.shape[0] // rows
    per_block = rows // own.shape[2]
    lag = (n + 1) // 2
    cols = own.shape[3]

    def finish(c, j, total):
        at = pl.ds(pl.multiple_of(c * own.shape[2], own.shape[2]), own.shape[2])
        own[c, j] = (x_own[at, :].astype(jnp.float32) + total).astype(low)
        store(c, j).start()

    def store(c, j):
        at = pl.ds(pl.multiple_of(c * own.shape[2], own.shape[2]), own.shape[2])
        return pltpu.make_async_copy(own.at[c, j], out_ref.at[at, :], out_sem.at[c])

    line = LineFeed(n, chunks, left_ref, right_ref, up_ref, own, recv, *line_sems, finish)
    h2_in, att_in = Stream(h2_ref, h2_buf, h2_sem, True), Stream(att_ref, att_buf, att_sem, True)
    hid_out, gp_out = Stream(hidden_ref, hid_buf, hid_sem, False), Stream(grad_pre_ref, gp_buf, gp_sem, False)
    gh_out, ga_out = Stream(grad_h2_ref, gh_buf, gh_sem, False), Stream(grad_att_ref, ga_buf, ga_sem, False)

    h2_in.copy(jnp.int32(0)).start()
    att_in.copy(jnp.int32(0)).start()
    weights = [pltpu.make_async_copy(a, b, weight_sem.at[w]) for w, (a, b) in enumerate(((fc1_ref, fc1), (dense_ref, dense), (fc2_ref, fc2), (x_ref, x_own)))]
    for copy in weights:
        copy.start()

    def up_pieces(q):
        at, two = pl.ds(pl.multiple_of(q * rows, rows), rows), lax.rem(q, 2)
        for j in range(n):
            span = pl.ds(j * cols, cols)
            dst = up_buf.at[two, :, span]
            for cond, src in ((k == j, up_own_ref), (k - 1 == j, left_ref), (k + 1 == j, right_ref)):
                yield cond, True, pltpu.make_async_copy(src.at[at, :], dst, up_sem.at[two, j]), pltpu.make_async_copy(dst, up_ref.at[at, span], near_sem.at[two, j])
            far = (k - j > 1) | (j - k > 1)
            yield far, False, pltpu.make_async_copy(up_ref.at[at, span], dst, up_sem.at[two, j]), None

    def up_start(q):
        for cond, _, load, _ in up_pieces(q):
            @pl.when(cond)
            def _(load=load):
                load.start()

    def up_wait(q):
        for cond, near, load, put in up_pieces(q):
            @pl.when(cond)
            def _(near=near, load=load, put=put):
                load.wait()
                if near:
                    put.start()

    def up_put_wait(q):
        for cond, near, _, put in up_pieces(q):
            if near:
                @pl.when(cond)
                def _(put=put):
                    put.wait()

    greet([(k > 0, {AX: k - 1}), (k < n - 1, {AX: k + 1})])

    def forward(p):
        @pl.when(p + 1 < blocks)
        def _():
            h2_in.copy(p + 1).start()
            att_in.copy(p + 1).start()

        @pl.when(p == 0)
        def _():
            weights[0].wait()

        @pl.when(p >= 2)
        def _():
            hid_out.copy(p - 2).wait()

        h2_in.copy(p).wait()
        att_in.copy(p).wait()
        two = lax.rem(p, 2)
        keep = lax.rem(p, lag + 1)
        h2 = h2_buf[two]
        for t in range(0, fc1.shape[1], tile):
            hid, bend = gelu_and_slope(jnp.dot(h2, fc1[:, t : t + tile], preferred_element_type=jnp.float32))
            hid_buf[two, :, t : t + tile] = hid.astype(low)
            slope[keep, :, t : t + tile] = bend.astype(low)
        hid_out.copy(p).start()

        @pl.when(p == 0)
        def _():
            for copy in weights[1:]:
                copy.wait()

        att, hid = att_buf[two], hid_buf[two]
        for j in range(n):
            part = jnp.dot(hid, fc2[:, j * cols : (j + 1) * cols], preferred_element_type=jnp.float32)
            part = (part + jnp.dot(att, dense[:, j * cols : (j + 1) * cols], preferred_element_type=jnp.float32)).astype(low)
            for b in range(per_block):
                own[per_block * p + b, j] = part[b * own.shape[2] : (b + 1) * own.shape[2]]

    def backward(q):
        @pl.when(q >= 2)
        def _():
            for stream in (gp_out, gh_out, ga_out):
                stream.copy(q - 2).wait()

        up_wait(q)
        two = lax.rem(q, 2)
        keep = lax.rem(q, lag + 1)
        up = up_buf[two]
        ga_buf[two] = lax.dot_general(up, dense[...], NT, preferred_element_type=jnp.float32).astype(low)
        ga_out.copy(q).start()
        for t in range(0, fc2.shape[0], tile):
            grad = lax.dot_general(up, fc2[t : t + tile, :], NT, preferred_element_type=jnp.float32)
            gp_buf[two, :, t : t + tile] = (grad * slope[keep, :, t : t + tile].astype(jnp.float32)).astype(low)
        gp_out.copy(q).start()
        grad_pre = gp_buf[two]
        for t in range(0, fc1.shape[0], tile):
            gh_buf[two, :, t : t + tile] = lax.dot_general(grad_pre, fc1[t : t + tile, :], NT, preferred_element_type=jnp.float32).astype(low)
        gh_out.copy(q).start()

    def body(p, _):
        @pl.when(p < blocks)
        def _():
            forward(p)

        line.step(per_block * p)

        @pl.when(within(p - lag, blocks))
        def _():
            backward(p - lag)

        for b in range(1, per_block):
            line.step(per_block * p + b)

        @pl.when(within(p + 1 - lag, blocks))
        def _():
            @pl.when(p + 1 - lag >= 2)
            def _():
                up_put_wait(p - 1 - lag)

            up_start(p + 1 - lag)

        return 0

    lax.fori_loop(0, max(blocks + lag, -(-(chunks + n - 1) // per_block)), body, 0)
    for last in range(max(blocks - 2, 0), blocks):
        for stream in (hid_out, gp_out, gh_out, ga_out):
            stream.copy(jnp.int32(last)).wait()
        up_put_wait(jnp.int32(last))
    line.drain()

    def stored(c, _):
        for j in range(n):
            @pl.when(k == j)
            def _(j=j):
                store(c, j).wait()
        return 0

    lax.fori_loop(0, chunks, stored, 0)


def feed_forward(h2, attended, fc1, fc2, dense, upstream, left, right, own_x, rows=256, chunks=16, tile=512):
    n = lax.axis_size(AX)
    total, width = h2.shape
    hidden, heads_width, cols = fc1.shape[1], attended.shape[1], width // n
    low, dma, vmem = jnp.bfloat16, pltpu.SemaphoreType.DMA, pltpu.VMEM
    piece = total // chunks
    lag = (n + 1) // 2
    tile = min(tile, hidden)
    anywhere = pl.BlockSpec(memory_space=pl.ANY)
    shape = lambda cols: jax.ShapeDtypeStruct((total, cols), low)
    two = lambda cols: vmem((2, rows, cols), low)
    return pl.pallas_call(
        functools.partial(feed_kernel, n, chunks, tile),
        out_shape=[shape(width), shape(hidden), shape(hidden), shape(width), shape(heads_width), shape(cols)],
        in_specs=[anywhere] * 9,
        out_specs=[anywhere] * 6,
        scratch_shapes=[
            vmem((chunks, n, piece, cols), low), vmem((chunks, n + 1, piece, cols), low),
            vmem(fc1.shape, low), vmem(fc2.shape, low), vmem(dense.shape, low), vmem((total, cols), low),
            two(width), two(heads_width), two(width), two(hidden), two(hidden), two(width), two(heads_width), vmem((lag + 1, rows, hidden), low),
            dma((4,)), dma((2, n)), dma((2,)), dma((2,)), dma((2, n)), dma((2,)), dma((2,)), dma((2,)), dma((2,)), dma((chunks,)),
            dma((chunks, n)), dma((chunks, n + 1)), dma((chunks, n)), dma((chunks, n)), dma((chunks, n)),
        ],
        compiler_params=pltpu.CompilerParams(collective_id=1, has_side_effects=True, vmem_limit_bytes=VMEM_CAP),
        name="feed_forward",
    )(h2, attended, fc1, fc2, dense, upstream, left, right, own_x)


def on_device(tokens, segments, positions, ln1_gain, ln1_bias, ln2_gain, ln2_bias, qkv_weight, dense_weight, fc1_weight, fc2_weight, upstream):
    n = lax.axis_size(AX)
    share = tokens.shape[1] // n
    left = lax.ppermute(upstream, AX, [(i, i + 1) for i in range(n - 1)])
    right = lax.ppermute(upstream, AX, [(i + 1, i) for i in range(n - 1)])
    rot = rot_tables(positions)
    h_one, h_two, qkv = project(tokens, ln1_gain, ln1_bias, ln2_gain, ln2_bias, rot, qkv_weight)
    attended, lse = attend(qkv, segments, 1024)
    own_x = lax.dynamic_slice_in_dim(tokens, lax.axis_index(AX) * share, share, 1)
    up, hidden, grad_pre, grad_h_two, grad_att, output = feed_forward(
        h_two, attended, fc1_weight, fc2_weight, dense_weight, upstream, left, right, own_x)
    grad_qkv = attend_back(qkv, grad_att, attended, segments, lse, rot)
    partial_s, norm_part = input_terms(tokens, grad_qkv, grad_h_two, ln1_gain, ln2_gain, qkv_weight)
    groups = [
        dict(x=0, y=0, count=grad_pre.shape[1] // STRIP, turned=True, out=2),
        dict(x=1, y=1, count=hidden.shape[1] // STRIP, turned=False, out=3),
        dict(x=2, y=1, count=attended.shape[1] // STRIP, turned=False, out=1),
        dict(x=3, y=2, count=grad_qkv.shape[1] // STRIP, turned=True, out=0),
    ]
    s, norm_grads, qkv_grad, dense_grad, fc1_grad, fc2_grad = back_sums(
        partial_s, norm_part, [grad_pre, hidden, attended, grad_qkv], [h_two, up, h_one], groups)
    input_grad = finish(tokens, s, up)
    return (
        output, input_grad, qkv_grad, dense_grad, fc1_grad, fc2_grad,
        norm_grads[0], norm_grads[1], norm_grads[2], norm_grads[3],
    )


def solution(mesh):
    in_specs = (
        P("dp", None),
        P("dp"),
        P("dp"),
        P(),
        P(),
        P(),
        P(),
        P(None, "tensor"),
        P("tensor", None),
        P(None, "tensor"),
        P("tensor", None),
        P("dp", "tensor"),
    )
    out_specs = (
        P("dp", "tensor"),
        P("dp", None),
        P("dp", "tensor"),
        P("tensor", "dp"),
        P("dp", "tensor"),
        P("tensor", "dp"),
        P("dp"),
        P("dp"),
        P("dp"),
        P("dp"),
    )
    return jax.shard_map(
        on_device, mesh=mesh, in_specs=in_specs, out_specs=out_specs, check_vma=False
    )
```

```python
import functools
import itertools

import jax
import jax.numpy as jnp
from jax import lax
from jax.experimental import pallas as pl
from jax.experimental.pallas import tpu as pltpu
from jax.sharding import PartitionSpec as P

HEAD_DIM = 256
ROT_DIM = 64
SEQ_LEN = 2048
LANES = 128
VMEM_CAP = 60 * 2**20
NT = (((1,), (1,)), ((), ()))
TN = (((0,), (0,)), ((), ()))


def rot_tables(positions):
    half = ROT_DIM // 2
    steps_up = jnp.arange(half).astype(jnp.float32) * 2.0 / ROT_DIM
    inverse = jnp.power(jnp.float32(10000.0), -steps_up)
    angle = inverse[:, None] * positions.astype(jnp.float32)[None, :]
    return jnp.concatenate([jnp.cos(angle), jnp.sin(angle)], 0)


def rot_tiles(table):
    half = ROT_DIM // 2
    cos, sin = table[:half], table[half:]
    zero = jnp.zeros_like(sin)
    rest = jnp.zeros((LANES - ROT_DIM, table.shape[1]), jnp.float32)
    rows = ((cos, cos, rest + 1.0), (-sin, zero, rest), (zero, sin, rest))
    return tuple(jnp.concatenate(parts, 0).T for parts in rows)


def rotate_tile(u, cos_t, sin_up, sin_down):
    half = ROT_DIM // 2
    return u * cos_t + pltpu.roll(u, LANES - half, 1) * sin_up + pltpu.roll(u, half, 1) * sin_down


def rotate_back_tile(g, cos_t, sin_up, sin_down):
    half = ROT_DIM // 2
    return g * cos_t + pltpu.roll(g * sin_down, LANES - half, 1) + pltpu.roll(g * sin_up, half, 1)


def pre_kernel(x_ref, g1_ref, b1_ref, g2_ref, b2_ref, rot_ref, w_ref, h1_ref, h2_ref, qkv_ref, stats_ref):
    x = x_ref[...].astype(jnp.float32)
    mean = jnp.mean(x, axis=-1, keepdims=True)
    center = x - mean
    inv = lax.rsqrt(jnp.mean(center * center, axis=-1, keepdims=True) + 1e-05)
    stats_ref[:, :1] = mean
    stats_ref[:, 1:] = inv
    normed = center * inv
    h1 = (normed * g1_ref[...] + b1_ref[...]).astype(jnp.bfloat16)
    h1_ref[...] = h1
    h2_ref[...] = (normed * g2_ref[...] + b2_ref[...]).astype(jnp.bfloat16)
    cos_t, su, sd = rot_tiles(rot_ref[...])
    for b in range(w_ref.shape[1] // HEAD_DIM):
        cols = slice(b * HEAD_DIM, (b + 1) * HEAD_DIM)
        y = jnp.dot(h1, w_ref[:, cols], preferred_element_type=jnp.float32)
        if b % 3 < 2:
            qkv_ref[:, b * HEAD_DIM : b * HEAD_DIM + LANES] = rotate_tile(y[:, :LANES], cos_t, su, sd).astype(jnp.bfloat16)
            qkv_ref[:, b * HEAD_DIM + LANES : (b + 1) * HEAD_DIM] = y[:, LANES:].astype(jnp.bfloat16)
        else:
            qkv_ref[:, cols] = y.astype(jnp.bfloat16)


def project(tokens, g1, b1, g2, b2, rot, w, rows=512):
    total, width = tokens.shape
    rows = min(rows, total)
    row_blk = lambda cols: pl.BlockSpec((rows, cols), lambda i: (i, 0))
    vec = pl.BlockSpec((1, width), lambda i: (0, 0))
    cols = w.shape[1]
    return pl.pallas_call(
        pre_kernel,
        grid=(total // rows,),
        in_specs=[row_blk(width), vec, vec, vec, vec, pl.BlockSpec((ROT_DIM, rows), lambda i: (0, i)),
                  pl.BlockSpec((width, cols), lambda i: (0, 0), pipeline_mode=pl.Buffered(1))],
        out_specs=[row_blk(width), row_blk(width), row_blk(cols), row_blk(2)],
        out_shape=[jax.ShapeDtypeStruct((total, width), jnp.bfloat16)] * 2 + [jax.ShapeDtypeStruct((total, cols), jnp.bfloat16), jax.ShapeDtypeStruct((total, 2), jnp.float32)],
        compiler_params=pltpu.CompilerParams(vmem_limit_bytes=VMEM_CAP),
        cost_estimate=pl.CostEstimate(flops=2 * total * width * cols, bytes_accessed=6 * total * width + 2 * cols * (width + total), transcendentals=0),
        name="norm_project",
    )(tokens, g1[None], b1[None], g2[None], b2[None], rot, w)


def attend_kernel(block, heads, qkv_ref, drow_ref, dcol_ref, o_ref, lse_ref, v_turned):
    i = pl.program_id(1)
    scale = HEAD_DIM ** (-0.5)
    part = lambda h, c: slice((3 * h + c) * HEAD_DIM, (3 * h + c + 1) * HEAD_DIM)

    @pl.when(i == 0)
    def _():
        for h in range(heads):
            v_turned[h] = qkv_ref[:, part(h, 2)].T

    here = pl.ds(pl.multiple_of(i * block, block), block)
    queries = [qkv_ref[here, part(h, 0)] for h in range(heads)]
    docs_q = drow_ref[...]
    gap = lax.broadcasted_iota(jnp.int32, (block, block), 1) - lax.broadcasted_iota(jnp.int32, (block, block), 0)

    def body(j, carry):
        rows = pl.ds(pl.multiple_of(j * block, block), block)
        allowed = (docs_q == dcol_ref[rows, :]) & (gap >= (j - i) * block)
        new = []
        for h in range(heads):
            m, l, acc = carry[h]
            s = lax.dot_general(qkv_ref[rows, part(h, 1)], queries[h], NT, preferred_element_type=jnp.float32) * scale
            s = jnp.where(allowed, s, -1e30)
            m_new = jnp.maximum(m, jnp.max(s, axis=0, keepdims=True))
            p = jnp.exp(s - m_new)
            alpha = jnp.exp(m - m_new)
            l = l * alpha + jnp.sum(p, axis=0, keepdims=True)
            acc = acc * alpha + jnp.dot(v_turned[h, :, rows], p.astype(jnp.bfloat16), preferred_element_type=jnp.float32)
            new.append((m_new, l, acc))
        return tuple(new)

    start = (jnp.full((1, block), -1e30, jnp.float32), jnp.zeros((1, block), jnp.float32), jnp.zeros((HEAD_DIM, block), jnp.float32))
    carry = lax.fori_loop(0, i + 1, body, (start,) * heads)
    for h in range(heads):
        m, l, acc = carry[h]
        o_ref[:, h * HEAD_DIM : (h + 1) * HEAD_DIM] = (acc * (1.0 / l)).T.astype(jnp.bfloat16)
        lse_ref[h] = m + jnp.log(l)


def attend(qkv, docs, block=512):
    total, cols = qkv.shape
    heads = cols // (3 * HEAD_DIM)
    seqs = total // SEQ_LEN
    n = SEQ_LEN // block
    return pl.pallas_call(
        functools.partial(attend_kernel, block, heads),
        grid=(seqs, n),
        in_specs=[
            pl.BlockSpec((SEQ_LEN, cols), lambda s, i: (s, 0)),
            pl.BlockSpec((1, block), lambda s, i: (0, s * n + i)),
            pl.BlockSpec((SEQ_LEN, 1), lambda s, i: (s, 0)),
        ],
        out_specs=[pl.BlockSpec((block, heads * HEAD_DIM), lambda s, i: (s * n + i, 0)),
                   pl.BlockSpec((heads, 1, block), lambda s, i: (0, 0, s * n + i))],
        out_shape=[jax.ShapeDtypeStruct((total, heads * HEAD_DIM), jnp.bfloat16), jax.ShapeDtypeStruct((heads, 1, total), jnp.float32)],
        scratch_shapes=[pltpu.VMEM((heads, HEAD_DIM, SEQ_LEN), jnp.bfloat16)],
        compiler_params=pltpu.CompilerParams(vmem_limit_bytes=VMEM_CAP),
        cost_estimate=pl.CostEstimate(flops=2 * total * SEQ_LEN * heads * HEAD_DIM, bytes_accessed=4 * total * cols, transcendentals=total * SEQ_LEN),
        name="attend",
    )(qkv, docs[None, :], docs[:, None])


def finish_kernel(x_ref, stats_ref, s_ref, up_ref, out_ref):
    mean, inv = stats_ref[:, :1], stats_ref[:, 1:]
    s = s_ref[...].astype(jnp.float32)
    center = x_ref[...].astype(jnp.float32) - mean
    bend = jnp.mean(s * center, axis=-1, keepdims=True) * (inv * inv * inv)
    level = jnp.mean(s, axis=-1, keepdims=True) * inv
    out_ref[...] = (up_ref[...].astype(jnp.float32) - level) + (s * inv - center * bend)


def finish(tokens, stats, s, up, rows=512):
    total, width = tokens.shape
    block = pl.BlockSpec((min(rows, total), width), lambda i: (i, 0))
    return pl.pallas_call(
        finish_kernel,
        grid=(total // min(rows, total),),
        in_specs=[block, pl.BlockSpec((min(rows, total), 2), lambda i: (i, 0)), block, block],
        out_specs=block,
        out_shape=jax.ShapeDtypeStruct((total, width), jnp.float32),
        compiler_params=pltpu.CompilerParams(vmem_limit_bytes=VMEM_CAP),
        cost_estimate=pl.CostEstimate(flops=10 * total * width, bytes_accessed=10 * total * width, transcendentals=0),
        name="finish",
    )(tokens, stats, s, up)


AX = "tensor"
DP = "dp"
MESH = pl.DeviceIdType.MESH
STRIP = 256


def greet(peers):
    barrier = pltpu.get_barrier_semaphore()
    count = 0
    for cond, device in peers:
        @pl.when(cond)
        def _(device=device):
            pl.semaphore_signal(barrier, inc=1, device_id=device, device_id_type=MESH)
        count = count + jnp.asarray(cond).astype(jnp.int32)
    pl.semaphore_wait(barrier, count)


def within(c, count):
    return (c >= 0) & (c < count)


def blend(first, second):
    both = [(place / len(one), which, entry) for which, one in enumerate((first, second)) for place, entry in enumerate(one)]
    return [entry for _, _, entry in sorted(both, key=lambda e: e[:2])]


class LineSum:
    def __init__(self, n, chunks, full_ref, own, recv, rs_send, rs_recv, ag_right, ag_left, ag_recv, store_sem):
        self.n, self.chunks, self.full_ref, self.own, self.recv = n, chunks, full_ref, own, recv
        self.rs_send, self.rs_recv, self.ag_send, self.ag_recv, self.store_sem = rs_send, rs_recv, (ag_right, ag_left), ag_recv, store_sem
        self.k = lax.axis_index(AX)
        self.rows, self.cols = own.shape[2], own.shape[3]

    def block(self, c, j):
        return self.full_ref.at[pl.ds(pl.multiple_of(c * self.rows, self.rows), self.rows), pl.ds(j * self.cols, self.cols)]

    def copy(self, src, dst, send, recv, right):
        return pltpu.make_async_remote_copy(src, dst, send, recv, device_id={AX: self.k + 1 if right else self.k - 1}, device_id_type=MESH)

    def scatter_copy(self, c, j, right):
        slot = j if right else jnp.where(self.k - 1 == j, self.n, j)
        return self.copy(self.own.at[c, j], self.recv.at[c, slot], self.rs_send.at[c, j], self.rs_recv.at[c, slot], right)

    def scatter_arrived(self, c, slot):
        dst = self.recv.at[c, slot]
        pltpu.make_async_copy(dst, dst, self.rs_recv.at[c, slot]).wait()

    def gather_copy(self, c, j, right, src=None):
        block = self.block(c, j)
        return self.copy(block if src is None else src, block, self.ag_send[0 if right else 1].at[c, j], self.ag_recv.at[c, j], right)

    def gather_arrived(self, c, j):
        block = self.block(c, j)
        pltpu.make_async_copy(block, block, self.ag_recv.at[c, j]).wait()

    def store(self, c, j):
        return pltpu.make_async_copy(self.own.at[c, j], self.block(c, j), self.store_sem.at[c])

    def pieces(self, i):
        return [functools.partial(self.pass_on, i, p) for p in range(self.n)] + [functools.partial(self.close, i)]

    def pass_on(self, i, p):
        n, k, chunks = self.n, self.k, self.chunks
        for right in (True, False):
            j = p if right else n - 1 - p
            dist = (k - j) if right else (j - k)
            onward = (k < n - 1) if right else (k > 0)
            behind = (k > 0) if right else (k < n - 1)
            c_gather = i - (n - 1) - dist
            c_scatter = i - (k if right else n - 1 - k)

            @pl.when((dist > 0) & within(c_gather, chunks))
            def _(j=j, right=right, c=c_gather, onward=onward):
                self.gather_arrived(c, j)

                @pl.when(onward)
                def _():
                    self.gather_copy(c, j, right).start()

            @pl.when((dist < 0) & within(c_scatter, chunks))
            def _(j=j, right=right, c=c_scatter, behind=behind):
                @pl.when(behind)
                def _():
                    self.scatter_arrived(c, j)
                    self.own[c, j] = self.own[c, j] + self.recv[c, j]

                self.scatter_copy(c, j, right).start()

    def close(self, i):
        n, k, chunks = self.n, self.k, self.chunks
        c = i - (n - 1)
        for j in range(n):
            @pl.when((k == j) & within(c, chunks))
            def _(j=j):
                total = self.own[c, j].astype(jnp.float32)
                if j > 0:
                    self.scatter_arrived(c, j)
                    total = total + self.recv[c, j].astype(jnp.float32)
                if j < n - 1:
                    self.scatter_arrived(c, n)
                    total = total + self.recv[c, n].astype(jnp.float32)
                self.own[c, j] = total.astype(self.own.dtype)
                self.store(c, j).start()
                if j < n - 1:
                    self.gather_copy(c, j, True, self.own.at[c, j]).start()
                if j > 0:
                    self.gather_copy(c, j, False, self.own.at[c, j]).start()

    def drain(self):
        n, k = self.n, self.k

        def one(c, _):
            for j in range(n):
                @pl.when(k < j)
                def _(j=j):
                    self.scatter_copy(c, j, True).wait_send()

                    @pl.when(k > 0)
                    def _():
                        self.gather_copy(c, j, False).wait_send()

                @pl.when(k > j)
                def _(j=j):
                    self.scatter_copy(c, j, False).wait_send()

                    @pl.when(k < n - 1)
                    def _():
                        self.gather_copy(c, j, True).wait_send()

                @pl.when(k == j)
                def _(j=j):
                    self.store(c, j).wait()
                    if j < n - 1:
                        self.gather_copy(c, j, True, self.own.at[c, j]).wait_send()
                    if j > 0:
                        self.gather_copy(c, j, False, self.own.at[c, j]).wait_send()
            return 0

        lax.fori_loop(0, self.chunks, one, 0)


class HalvingSum:
    def __init__(self, dp, groups, xs, ys, outs, xbuf, ybuf, tiles, recvs, stage, stage_turned, x_sem, y_sem, send_sem, recv_sem, out_sem):
        self.dp, self.bits = dp, dp.bit_length() - 1
        self.groups, self.xs, self.ys, self.outs = groups, xs, ys, outs
        self.xbuf, self.ybuf, self.tiles, self.recvs = xbuf, ybuf, tiles, recvs
        self.stage, self.stage_turned = stage, stage_turned
        self.x_sem, self.y_sem, self.send_sem, self.recv_sem, self.out_sem = x_sem, y_sem, send_sem, recv_sem, out_sem
        self.me = lax.axis_index(DP)
        self.slots = tiles.shape[0]
        self.width = tiles.shape[-1]
        self.first = [sum(g["count"] for g in groups[:i]) for i in range(len(groups) + 1)]
        self.total = self.first[-1]
        self.lags = [1] + [1 + 2 * level for level in range(1, self.bits - 1)] + [max(2 * self.bits - 2, 2)]

    def bit(self, b):
        return lax.rem(lax.div(self.me, 2**b), 2)

    def partner(self, b):
        return self.me + (1 - 2 * self.bit(b)) * 2**b

    def order(self, odd):
        rest = list(range(1, self.bits))
        return [0] + (rest[1:] + rest[:1] if odd else rest)

    def pick(self, odd, level, value):
        done = self.order(odd)[:level]
        now = self.order(odd)[level]
        return tuple(0 if b in done else value if b == now else slice(None) for b in range(self.bits))

    def in_group(self, t, g):
        return (t >= self.first[g]) & (t < self.first[g + 1])

    def x_copies(self, t):
        for g, group in enumerate(self.groups):
            at = pl.ds(pl.multiple_of((t - self.first[g]) * STRIP, STRIP), STRIP)
            slot = lax.rem(t, 2)
            yield self.in_group(t, g), pltpu.make_async_copy(self.xs[group["x"]].at[:, at], self.xbuf.at[slot], self.x_sem.at[slot])

    def x_start(self, t):
        for cond, copy in self.x_copies(t):
            @pl.when(cond)
            def _(copy=copy):
                copy.start()

    def x_wait(self, t):
        slot = lax.rem(t, 2)
        pltpu.make_async_copy(self.xbuf.at[slot], self.xbuf.at[slot], self.x_sem.at[slot]).wait()

    def y_copy(self, g):
        y = self.groups[g]["y"]
        return pltpu.make_async_copy(self.ys[y], self.ybuf.at[y % 2], self.y_sem.at[y % 2])

    def send(self, u, odd, level):
        slot = lax.rem(u, self.slots)
        return pltpu.make_async_remote_copy(
            self.tiles.at[(slot, *self.pick(odd, level, 1))], self.recvs[level].at[slot],
            self.send_sem.at[level, slot], self.recv_sem.at[level, slot],
            device_id={DP: self.partner(self.order(odd)[level])}, device_id_type=MESH)

    def out_copies(self, u):
        slot = lax.rem(u, 2)
        for g, group in enumerate(self.groups):
            at = pl.ds(pl.multiple_of((u - self.first[g]) * STRIP, STRIP), STRIP)
            out = self.outs[group["out"]]
            if group["turned"]:
                yield self.in_group(u, g), pltpu.make_async_copy(self.stage_turned.at[slot], out.at[:, at], self.out_sem.at[slot])
            else:
                yield self.in_group(u, g), pltpu.make_async_copy(self.stage.at[slot], out.at[at, :], self.out_sem.at[slot])

    def out_wait(self, u):
        for cond, copy in self.out_copies(u):
            @pl.when(cond)
            def _(copy=copy):
                copy.wait()

    def prologue(self):
        self.x_start(jnp.int32(0))
        self.y_copy(0).start()
        for g in range(1, len(self.groups)):
            if self.groups[g]["y"] == 1:
                self.y_copy(g).start()
                break

    def pieces(self, t, place, period, parts=4):
        odd = place % 2
        share = max(self.dp // parts, 1)
        spans = [range(first, first + share) for first in range(0, self.dp, share)]
        return [functools.partial(self.halve, t, place, period)] + [
            functools.partial(self.multiply, t, place, period, span, span[0] == 0, span[-1] == self.dp - 1) for span in spans]

    def halve(self, t, place, period):
        for level in range(self.bits - 1, -1, -1):
            u = t - self.lags[level]
            u_odd = (place - self.lags[level]) % period % 2

            @pl.when(within(u, self.total))
            def _(u=u, u_odd=u_odd, level=level):
                slot = lax.rem(u, self.slots)
                got = self.recvs[level]
                pltpu.make_async_copy(got.at[slot], got.at[slot], self.recv_sem.at[level, slot]).wait()
                keep = (slot, *self.pick(u_odd, level, 0))
                if level < self.bits - 1:
                    left = [range(2) if isinstance(p, slice) else (p,) for p in keep[1:]]
                    for flat, idx in enumerate(itertools.product(*left)):
                        pos = tuple(int(b) for b in format(flat, "b").zfill(self.bits - 1 - level))
                        self.tiles[(slot, *idx)] = self.tiles[(slot, *idx)] + got[(slot, *pos)]
                    self.send(u, u_odd, level + 1).start()
                else:
                    @pl.when(u >= 2)
                    def _():
                        self.out_wait(u - 2)

                    value = self.tiles[keep].astype(jnp.float32) + got[slot].astype(jnp.float32)
                    for g, group in enumerate(self.groups):
                        @pl.when(self.in_group(u, g))
                        def _(group=group):
                            if group["turned"]:
                                self.stage_turned[lax.rem(u, 2)] = value.T
                            else:
                                self.stage[lax.rem(u, 2)] = value
                    for cond, copy in self.out_copies(u):
                        @pl.when(cond)
                        def _(copy=copy):
                            copy.start()

    def ready(self, t, place, period):
        @pl.when(t >= self.slots)
        def _():
            for level in range(self.bits):
                self.send(t - self.slots, (place - self.slots) % period % 2, level).wait_send()

        seen = []
        for g, group in enumerate(self.groups):
            if group["y"] in seen:
                continue
            seen.append(group["y"])

            @pl.when(t == self.first[g])
            def _(g=g, group=group):
                self.y_copy(g).wait()
                if group["y"] == 1:
                    for later in range(len(self.groups)):
                        if self.groups[later]["y"] == 2:
                            self.y_copy(later).start()
                            break

        @pl.when(t + 1 < self.total)
        def _():
            self.x_start(t + 1)

        self.x_wait(t)

    def multiply(self, t, place, period, span, opens, closes):
        @pl.when(within(t, self.total))
        def _():
            if opens:
                self.ready(t, place, period)
            slot = lax.rem(t, self.slots)
            y_slot = jnp.int32(0)
            for g, group in enumerate(self.groups):
                y_slot = jnp.where(t >= self.first[g], group["y"] % 2, y_slot)
            x = self.xbuf[lax.rem(t, 2)]
            for flat in span:
                idx = tuple((flat >> b) & 1 for b in range(self.bits))
                shard = sum((self.bit(b) + idx[b] * (1 - 2 * self.bit(b))) * 2**b for b in range(self.bits))
                at = pl.ds(pl.multiple_of(shard * self.width, self.width), self.width)
                self.tiles[(slot, *idx)] = lax.dot_general(x, self.ybuf[y_slot, :, at], TN, preferred_element_type=jnp.float32).astype(jnp.bfloat16)
            if closes:
                self.send(t, place % 2, 0).start()

    def drain(self, period):
        for u in range(self.total - self.slots, self.total):
            for level in range(self.bits):
                self.send(jnp.int32(u), u % period % 2, level).wait_send()
        for u in range(self.total - 2, self.total):
            self.out_wait(jnp.int32(u))


class LineScatter:
    def __init__(self, n, own, recv, x_own, out_ref, send_sem, recv_sem, store_sem, hop=1):
        self.hop = hop
        self.n, self.own, self.recv, self.x_own, self.out_ref = n, own, recv, x_own, out_ref
        self.send_sem, self.recv_sem, self.store_sem = send_sem, recv_sem, store_sem
        self.k = lax.axis_index(AX)
        self.chunks, _, self.rows, self.cols = own.shape

    def span(self, c):
        return pl.ds(pl.multiple_of(c * self.rows, self.rows), self.rows)

    def copy(self, c, j, right):
        slot = j if right else jnp.where(self.k - 1 == j, self.n, j)
        return pltpu.make_async_remote_copy(
            self.own.at[c, j], self.recv.at[c, slot], self.send_sem.at[c, j], self.recv_sem.at[c, slot],
            device_id={AX: self.k + 1 if right else self.k - 1}, device_id_type=MESH)

    def arrived(self, c, slot):
        got = self.recv.at[c, slot]
        pltpu.make_async_copy(got, got, self.recv_sem.at[c, slot]).wait()

    def store(self, c, j):
        return pltpu.make_async_copy(self.own.at[c, j], self.out_ref.at[self.span(c), :], self.store_sem.at[c])

    def pieces(self, i):
        return [functools.partial(self.pass_on, i, p) for p in range(self.n)] + [functools.partial(self.close, i)]

    def step(self, i):
        for piece in self.pieces(i):
            piece()

    def pass_on(self, i, p):
        n, k = self.n, self.k
        for right in (True, False):
            j = p if right else n - 1 - p
            ahead = (j > k) if right else (j < k)
            behind = (k > 0) if right else (k < n - 1)
            c = i - self.hop * (k if right else n - 1 - k)

            @pl.when(ahead & within(c, self.chunks))
            def _(j=j, right=right, c=c, behind=behind):
                @pl.when(behind)
                def _():
                    self.arrived(c, j)
                    self.own[c, j] = self.own[c, j] + self.recv[c, j]

                self.copy(c, j, right).start()

    def close(self, i):
        n, k = self.n, self.k
        c = i - self.hop * (n - 1)
        for j in range(n):
            @pl.when((k == j) & within(c, self.chunks))
            def _(j=j):
                total = self.x_own[self.span(c), :].astype(jnp.float32) + self.own[c, j].astype(jnp.float32)
                if j > 0:
                    self.arrived(c, j)
                    total = total + self.recv[c, j].astype(jnp.float32)
                if j < n - 1:
                    self.arrived(c, n)
                    total = total + self.recv[c, n].astype(jnp.float32)
                self.own[c, j] = total.astype(self.own.dtype)
                self.store(c, j).start()

    def drain(self):
        def one(c, _):
            for j in range(self.n):
                @pl.when(self.k < j)
                def _(j=j):
                    self.copy(c, j, True).wait_send()

                @pl.when(self.k > j)
                def _(j=j):
                    self.copy(c, j, False).wait_send()

                @pl.when(self.k == j)
                def _(j=j):
                    self.store(c, j).wait()
            return 0

        lax.fori_loop(0, self.chunks, one, 0)


def scatter_scratch(n, chunks, rows, cols):
    low, dma = jnp.bfloat16, pltpu.SemaphoreType.DMA
    return [pltpu.VMEM((chunks, n, rows, cols), low), pltpu.VMEM((chunks, n + 1, rows, cols), low), pltpu.VMEM((chunks * rows, cols), low),
            dma((chunks, n)), dma((chunks, n + 1)), dma((chunks,))]


class Stream:
    def __init__(self, hbm, slots, sem, inward):
        self.hbm, self.slots, self.sem, self.inward = hbm, slots, sem, inward
        self.rows = slots.shape[1]

    def copy(self, p):
        at = self.hbm.at[pl.ds(pl.multiple_of(p * self.rows, self.rows), self.rows), :]
        slot = lax.rem(p, 2)
        pair = (at, self.slots.at[slot]) if self.inward else (self.slots.at[slot], at)
        return pltpu.make_async_copy(*pair, self.sem.at[slot])


class Terms:
    def __init__(self, n, own, sums, w, gains, streams):
        self.n, self.own, self.sums, self.w, self.gains, self.streams = n, own, sums, w, gains, streams
        self.rows, self.cols = streams[0].rows, own.shape[3]
        self.blocks = own.shape[0] * own.shape[2] // self.rows

    def start(self, i):
        for stream in self.streams:
            stream.copy(i).start()

    def pieces(self, i):
        return [functools.partial(self.tile, i, j) for j in range(self.n)]

    def tile(self, i, j):
        @pl.when(i < self.blocks)
        def _():
            if j == 0:
                @pl.when(i + 1 < self.blocks)
                def _():
                    self.start(i + 1)

                for stream in self.streams:
                    stream.copy(i).wait()
            two = lax.rem(i, 2)
            x, stats, gq, gh2 = (stream.slots for stream in self.streams)
            at = slice(j * self.cols, (j + 1) * self.cols)
            mean, inv = stats[two, :, :1], stats[two, :, 1:]
            one = lax.dot_general(gq[two], self.w[at, :], NT, preferred_element_type=jnp.float32)
            other = gh2[two, :, at].astype(jnp.float32)
            normed = (x[two, :, at].astype(jnp.float32) - mean) * inv
            total = (one * self.gains[:1, at] + other * self.gains[1:, at]).astype(self.own.dtype)
            height = self.own.shape[2]
            for b in range(self.rows // height):
                self.own[i * (self.rows // height) + b, j] = total[b * height : (b + 1) * height]
            for row, value in enumerate((one * normed, one, other * normed, other)):
                self.sums[row : row + 1, at] += jnp.sum(value, axis=0, keepdims=True)


class SmallSum:
    def __init__(self, n, bits, partner, out_ref, acc, dp_recv, line_send, line_recv, sems):
        self.n, self.bits, self.partner = n, bits, partner
        self.out_ref, self.acc, self.dp_recv, self.line_send, self.line_recv = out_ref, acc, dp_recv, line_send, line_recv
        self.dp_send_sem, self.dp_recv_sem, self.line_send_sem, self.line_recv_sem, self.own_sem = sems
        self.k, self.me = lax.axis_index(AX), lax.axis_index(DP)

    def last(self):
        return pltpu.make_async_copy(self.dp_recv.at[0, :, pl.ds(0, self.out_ref.shape[1])], self.out_ref, self.own_sem.at[0])

    def swap(self, b):
        return pltpu.make_async_remote_copy(
            self.acc, self.dp_recv.at[b], self.dp_send_sem.at[b], self.dp_recv_sem.at[b], device_id={DP: self.partner(b)}, device_id_type=MESH)

    def onward(self, way):
        return pltpu.make_async_remote_copy(
            self.line_send.at[way], self.line_recv.at[way], self.line_send_sem.at[way], self.line_recv_sem.at[way],
            device_id={AX: self.k + 1 - 2 * way}, device_id_type=MESH)

    def step(self, i):
        n, k = self.n, self.k
        for b in range(self.bits + 1):
            @pl.when(i == b)
            def _(b=b):
                if b > 0:
                    self.swap(b - 1).wait()
                    self.acc[...] = self.acc[...] + self.dp_recv[b - 1]
                if b < self.bits:
                    self.swap(b).start()
        for way in range(2):
            place = k if way == 0 else n - 1 - k

            @pl.when(i == self.bits + 1 + place)
            def _(way=way, place=place):
                self.line_send[way] = self.acc[...]

                @pl.when(place > 0)
                def _():
                    got = self.line_recv.at[way]
                    pltpu.make_async_copy(got, got, self.line_recv_sem.at[way]).wait()
                    self.line_send[way] = self.acc[...] + self.line_recv[way]

                @pl.when(place < n - 1)
                def _():
                    self.onward(way).start()

        @pl.when(i == self.bits + 1 + n)
        def _():
            self.acc[...] = self.line_send[0] + self.line_send[1] - self.acc[...]
            part = self.out_ref.shape[1]
            self.dp_recv[0, :, :part] = self.acc[:, pl.ds(pl.multiple_of(self.me * part, part), part)]
            self.last().start()

    def drain(self):
        @pl.when(self.k < self.n - 1)
        def _():
            self.onward(0).wait_send()

        @pl.when(self.k > 0)
        def _():
            self.onward(1).wait_send()

        self.last().wait()


def sums_kernel(n, dp, chunks, steps, ticks, groups, n_x, n_y, n_out, *refs):
    refs = list(refs)
    take = lambda count: [refs.pop(0) for _ in range(count)]
    x_ref, stats_ref, gh2_ref, gains, w_ref = take(5)
    xs, ys = take(n_x), take(n_y)
    full_ref, sum_ref = take(2)
    outs = take(n_out)
    own, recv, *line_sems = take(8)
    bits = dp.bit_length() - 1
    xbuf, ybuf, tiles = take(3)
    recvs = take(bits)
    rest = take(7)
    small_bufs, small_sems = take(4), take(5)
    k, me = lax.axis_index(AX), lax.axis_index(DP)
    line = LineSum(n, chunks, full_ref, own, recv, *line_sems)
    halving = HalvingSum(dp, groups, xs, ys, outs, xbuf, ybuf, tiles, recvs, *rest)
    small = SmallSum(n, bits, halving.partner, sum_ref, *small_bufs, small_sems)
    w, w_sem = take(2)
    streams = [Stream(ref, *take(2), True) for ref in (x_ref, stats_ref, xs[-1], gh2_ref)]
    terms = Terms(n, own, small_bufs[0], w, gains, streams)
    small_first = chunks

    w_copy = pltpu.make_async_copy(w_ref, w, w_sem.at[0])
    w_copy.start()
    terms.start(jnp.int32(0))
    halving.prologue()
    greet([(k > 0, {AX: k - 1}), (k < n - 1, {AX: k + 1})] + [(me >= 0, {DP: halving.partner(b)}) for b in range(bits)])

    small_bufs[0][...] = jnp.zeros_like(small_bufs[0])
    w_copy.wait()
    for piece in terms.pieces(jnp.int32(0)):
        piece()

    def small_step(c):
        @pl.when(c >= small_first)
        def _():
            small.step(2 * (c - small_first))
            small.step(2 * (c - small_first) + 1)

    def body(i, _):
        lines, strips = [], []
        for e in range(steps):
            c = steps * i + e
            lines += line.pieces(c)
            lines.append(functools.partial(small_step, c))
        for place in range(ticks):
            strips += halving.pieces(ticks * i + place, place, ticks)
        strips = blend(strips, terms.pieces(i + 1))
        for piece in blend(lines, strips):
            piece()
        return 0

    lax.fori_loop(0, max(-(-max(chunks + 2 * (n - 1), small_first + (bits + n + 3) // 2) // steps), -(-(halving.total + halving.lags[-1]) // ticks)), body, 0)
    line.drain()
    halving.drain(ticks)
    small.drain()


def back_sums(tokens, stats, grad_h2, gains, w_qkv, xs, ys, groups, chunks=16, slots=5, steps=2, ticks=3):
    n, dp = lax.axis_size(AX), lax.axis_size(DP)
    bits = dp.bit_length() - 1
    total, width = tokens.shape
    rows, cols = total // chunks, width // n
    w = width // dp
    block = steps * rows
    two = lambda cols, kind=jnp.bfloat16: [pltpu.VMEM((2, block, cols), kind), pltpu.SemaphoreType.DMA((2,))]
    dma = pltpu.SemaphoreType.DMA
    out_shapes = [None] * len(groups)
    for g in groups:
        size = xs[g["x"]].shape[1]
        out_shapes[g["out"]] = jax.ShapeDtypeStruct((w, size) if g["turned"] else (size, w), jnp.float32)
    anywhere = pl.BlockSpec(memory_space=pl.ANY)
    vmem = pltpu.VMEM
    low = jnp.bfloat16
    return pl.pallas_call(
        functools.partial(sums_kernel, n, dp, chunks, steps, ticks, groups, len(xs), len(ys), len(out_shapes)),
        out_shape=[jax.ShapeDtypeStruct(tokens.shape, low), jax.ShapeDtypeStruct((8, w), jnp.float32)] + out_shapes,
        in_specs=[anywhere] * 3 + [pl.BlockSpec(memory_space=vmem)] + [anywhere] * (1 + len(xs) + len(ys)),
        out_specs=[anywhere] * (2 + len(out_shapes)),
        scratch_shapes=[
            vmem((chunks, n, rows, cols), low), vmem((chunks, n + 1, rows, cols), low),
            dma((chunks, n)), dma((chunks, n + 1)), dma((chunks, n)), dma((chunks, n)), dma((chunks, n)), dma((chunks,)),
            vmem((2, total, STRIP), low), vmem((2, total, width), low), vmem((slots, *(2,) * bits, STRIP, w), low),
            *[vmem((slots, *(2,) * (bits - 1 - level), STRIP, w), low) for level in range(bits)],
            vmem((2, STRIP, w), jnp.float32), vmem((2, w, STRIP), jnp.float32),
            dma((2,)), dma((2,)), dma((bits, slots)), dma((bits, slots)), dma((2,)),
            vmem((8, width), jnp.float32), vmem((bits, 8, width), jnp.float32), vmem((2, 8, width), jnp.float32), vmem((2, 8, width), jnp.float32),
            dma((bits,)), dma((bits,)), dma((2,)), dma((2,)), dma((1,)),
            vmem(w_qkv.shape, low), dma((1,)), *two(width), *two(2, jnp.float32), *two(w_qkv.shape[1]), *two(width),
        ],
        compiler_params=pltpu.CompilerParams(collective_id=0, has_side_effects=True, vmem_limit_bytes=62 * 2**20),
        name="back_sums",
    )(tokens, stats, grad_h2, gains, w_qkv, *xs, *ys)


class LineGather:
    def __init__(self, n, chunks, rows, near_left, near_right, up_ref, right_sem, left_sem, recv_sem, hop):
        self.hop = hop
        self.n, self.chunks, self.rows, self.cols = n, chunks, rows, near_left.shape[1]
        self.near, self.up_ref, self.send_sem, self.recv_sem = (near_left, near_right), up_ref, (right_sem, left_sem), recv_sem
        self.k = lax.axis_index(AX)

    def span(self, c):
        return pl.ds(pl.multiple_of(c * self.rows, self.rows), self.rows)

    def block(self, c, j):
        return self.up_ref.at[self.span(c), pl.ds(j * self.cols, self.cols)]

    def copy(self, c, j, right, near):
        src = self.near[0 if right else 1].at[self.span(c), :] if near else self.block(c, j)
        return pltpu.make_async_remote_copy(
            src, self.block(c, j), self.send_sem[0 if right else 1].at[c, j], self.recv_sem.at[c, j],
            device_id={AX: self.k + 1 if right else self.k - 1}, device_id_type=MESH)

    def arrived(self, c, j):
        block = self.block(c, j)
        pltpu.make_async_copy(block, block, self.recv_sem.at[c, j]).wait()

    def pieces(self, i):
        return [functools.partial(self.pass_on, i, p) for p in range(self.n)]

    def pass_on(self, i, p):
        n, k = self.n, self.k
        for right in (True, False):
            j = p if right else n - 1 - p
            dist = (k - j) if right else (j - k)
            onward = (k < n - 1) if right else (k > 0)
            far = i - self.hop * (dist - 1)

            @pl.when((dist == 1) & onward & within(i, self.chunks))
            def _(j=j, right=right):
                self.copy(i, j, right, True).start()

            @pl.when((dist > 1) & within(far, self.chunks))
            def _(j=j, right=right, c=far, onward=onward):
                self.arrived(c, j)

                @pl.when(onward)
                def _():
                    self.copy(c, j, right, False).start()

    def drain(self):
        def one(c, _):
            for j in range(self.n):
                @pl.when((self.k > j) & (self.k < self.n - 1))
                def _(j=j):
                    self.copy(c, j, True, False).wait_send()

                @pl.when((self.k < j) & (self.k > 0))
                def _(j=j):
                    self.copy(c, j, False, False).wait_send()
            return 0

        lax.fori_loop(0, self.chunks, one, 0)


def gelu_and_slope(x):
    share = 0.5 * (1.0 + lax.erf(x * (0.5**0.5)))
    return x * share, share + x * (jnp.exp(-0.5 * x * x) * (2.0 * jnp.pi) ** -0.5)


def feed_kernel(
    n, chunks, tile, hop,
    h2_ref, att_ref, fc1_ref, fc2_ref, dense_ref, up_own_ref, left_ref, right_ref, x_ref,
    up_ref, hidden_ref, grad_pre_ref, grad_h2_ref, grad_att_ref, out_ref,
    own, recv, x_own, rs_send, rs_recv, out_sem, fc1, fc2, dense, h2_buf, att_buf, up_buf, hid_buf, gp_buf, gh_buf, ga_buf, slope,
    weight_sem, near_sem, h2_sem, att_sem, up_sem, hid_sem, gp_sem, gh_sem, ga_sem, *line_sems,
):
    k = lax.axis_index(AX)
    low = jnp.bfloat16
    rows = h2_buf.shape[1]
    blocks = h2_ref.shape[0] // rows
    per_block = rows // own.shape[2]
    lag = -(-(2 + hop * (n - 2)) // 2)
    cols = own.shape[3]
    rate = 3

    gather = LineGather(n, chunks, own.shape[2], left_ref, right_ref, up_ref, *line_sems, hop)
    scatter = LineScatter(n, own, recv, x_own, out_ref, rs_send, rs_recv, out_sem, hop)

    def gather_step(i):
        for piece in gather.pieces(i):
            piece()

    h2_in, att_in = Stream(h2_ref, h2_buf, h2_sem, True), Stream(att_ref, att_buf, att_sem, True)
    hid_out, gp_out = Stream(hidden_ref, hid_buf, hid_sem, False), Stream(grad_pre_ref, gp_buf, gp_sem, False)
    gh_out, ga_out = Stream(grad_h2_ref, gh_buf, gh_sem, False), Stream(grad_att_ref, ga_buf, ga_sem, False)

    h2_in.copy(jnp.int32(0)).start()
    att_in.copy(jnp.int32(0)).start()
    weights = [pltpu.make_async_copy(a, b, weight_sem.at[w]) for w, (a, b) in enumerate(((fc1_ref, fc1), (dense_ref, dense), (fc2_ref, fc2), (x_ref.at[:, pl.ds(pl.multiple_of(k * own.shape[3], own.shape[3]), own.shape[3])], x_own)))]
    for copy in weights:
        copy.start()

    def up_pieces(q):
        at, two = pl.ds(pl.multiple_of(q * rows, rows), rows), lax.rem(q, 2)
        for j in range(n):
            span = pl.ds(j * cols, cols)
            dst = up_buf.at[two, :, span]
            for cond, src in ((k == j, up_own_ref), (k - 1 == j, left_ref), (k + 1 == j, right_ref)):
                yield cond, True, pltpu.make_async_copy(src.at[at, :], dst, up_sem.at[two, j]), pltpu.make_async_copy(dst, up_ref.at[at, span], near_sem.at[two, j])
            far = (k - j > 1) | (j - k > 1)
            yield far, False, pltpu.make_async_copy(up_ref.at[at, span], dst, up_sem.at[two, j]), None

    def up_start(q):
        for cond, _, load, _ in up_pieces(q):
            @pl.when(cond)
            def _(load=load):
                load.start()

    def up_wait(q):
        for cond, near, load, put in up_pieces(q):
            @pl.when(cond)
            def _(near=near, load=load, put=put):
                load.wait()
                if near:
                    put.start()

    def up_put_wait(q):
        for cond, near, _, put in up_pieces(q):
            if near:
                @pl.when(cond)
                def _(put=put):
                    put.wait()

    greet([(k > 0, {AX: k - 1}), (k < n - 1, {AX: k + 1})])

    def forward(p):
        @pl.when(p + 1 < blocks)
        def _():
            h2_in.copy(p + 1).start()
            att_in.copy(p + 1).start()

        @pl.when(p == 0)
        def _():
            weights[0].wait()

        @pl.when(p >= 2)
        def _():
            hid_out.copy(p - 2).wait()

        h2_in.copy(p).wait()
        att_in.copy(p).wait()
        two = lax.rem(p, 2)
        keep = lax.rem(p, lag + 1)
        h2 = h2_buf[two]
        for t in range(0, fc1.shape[1], tile):
            hid, bend = gelu_and_slope(jnp.dot(h2, fc1[:, t : t + tile], preferred_element_type=jnp.float32))
            hid_buf[two, :, t : t + tile] = hid.astype(low)
            slope[keep, :, t : t + tile] = bend.astype(low)
        hid_out.copy(p).start()

        @pl.when(p == 0)
        def _():
            for copy in weights[1:]:
                copy.wait()

        att, hid = att_buf[two], hid_buf[two]
        for j in range(n):
            part = jnp.dot(hid, fc2[:, j * cols : (j + 1) * cols], preferred_element_type=jnp.float32)
            part = (part + jnp.dot(att, dense[:, j * cols : (j + 1) * cols], preferred_element_type=jnp.float32)).astype(low)
            for b in range(per_block):
                own[per_block * p + b, j] = part[b * own.shape[2] : (b + 1) * own.shape[2]]

    def backward(q):
        @pl.when(q >= 2)
        def _():
            for stream in (gp_out, gh_out, ga_out):
                stream.copy(q - 2).wait()

        up_wait(q)
        two = lax.rem(q, 2)
        keep = lax.rem(q, lag + 1)
        up = up_buf[two]
        ga_buf[two] = lax.dot_general(up, dense[...], NT, preferred_element_type=jnp.float32).astype(low)
        ga_out.copy(q).start()
        for t in range(0, fc2.shape[0], tile):
            grad = lax.dot_general(up, fc2[t : t + tile, :], NT, preferred_element_type=jnp.float32)
            gp_buf[two, :, t : t + tile] = (grad * slope[keep, :, t : t + tile].astype(jnp.float32)).astype(low)
        gp_out.copy(q).start()
        grad_pre = gp_buf[two]
        for t in range(0, fc1.shape[0], tile):
            gh_buf[two, :, t : t + tile] = lax.dot_general(grad_pre, fc1[t : t + tile, :], NT, preferred_element_type=jnp.float32).astype(low)
        gh_out.copy(q).start()

    def body(p, _):
        @pl.when(p < blocks)
        def _():
            forward(p)

        gather_step(per_block * p)
        scatter.step(lax.div(rate * p, 2))

        @pl.when(within(p - lag, blocks))
        def _():
            backward(p - lag)

        for b in range(1, per_block):
            gather_step(per_block * p + b)

        @pl.when(lax.div(rate * (p + 1), 2) - lax.div(rate * p, 2) > 1)
        def _():
            scatter.step(lax.div(rate * p, 2) + 1)

        @pl.when(within(p + 1 - lag, blocks))
        def _():
            @pl.when(p + 1 - lag >= 2)
            def _():
                up_put_wait(p - 1 - lag)

            up_start(p + 1 - lag)

        return 0

    lax.fori_loop(0, max(blocks + lag, -(-(chunks + hop * (n - 2)) // per_block), -(-2 * (scatter.chunks + hop * (n - 1)) // rate)), body, 0)
    for last in range(max(blocks - 2, 0), blocks):
        for stream in (hid_out, gp_out, gh_out, ga_out):
            stream.copy(jnp.int32(last)).wait()
        up_put_wait(jnp.int32(last))
    gather.drain()
    scatter.drain()


def feed_forward(h2, attended, fc1, fc2, dense, upstream, left, right, tokens, rows=256, chunks=16, tile=512, hop=2):
    n = lax.axis_size(AX)
    total, width = h2.shape
    hidden, heads_width, cols = fc1.shape[1], attended.shape[1], width // n
    low, dma, vmem = jnp.bfloat16, pltpu.SemaphoreType.DMA, pltpu.VMEM
    piece = total // chunks
    lag = -(-(2 + hop * (n - 2)) // 2)
    tile = min(tile, hidden)
    anywhere = pl.BlockSpec(memory_space=pl.ANY)
    shape = lambda cols: jax.ShapeDtypeStruct((total, cols), low)
    two = lambda cols: vmem((2, rows, cols), low)
    return pl.pallas_call(
        functools.partial(feed_kernel, n, chunks, tile, hop),
        out_shape=[shape(width), shape(hidden), shape(hidden), shape(width), shape(heads_width), shape(cols)],
        in_specs=[anywhere] * 9,
        out_specs=[anywhere] * 6,
        scratch_shapes=[
            *scatter_scratch(n, chunks, piece, cols),
            vmem(fc1.shape, low), vmem(fc2.shape, low), vmem(dense.shape, low),
            two(width), two(heads_width), two(width), two(hidden), two(hidden), two(width), two(heads_width), vmem((lag + 1, rows, hidden), low),
            dma((4,)), dma((2, n)), dma((2,)), dma((2,)), dma((2, n)), dma((2,)), dma((2,)), dma((2,)), dma((2,)),
            dma((chunks, n)), dma((chunks, n)), dma((chunks, n)),
        ],
        compiler_params=pltpu.CompilerParams(collective_id=1, has_side_effects=True, vmem_limit_bytes=VMEM_CAP),
        name="feed_forward",
    )(h2, attended, fc1, fc2, dense, upstream, left, right, tokens)


def attend_back_kernel(block, n, heads, qkv_ref, g_ref, o_ref, dcol_ref, drow_ref, lse_ref, rot_ref, out_ref, dk, dv):
    i = pl.program_id(1)
    scale = HEAD_DIM ** (-0.5)
    part = lambda h, c: slice((3 * h + c) * HEAD_DIM, (3 * h + c + 1) * HEAD_DIM)
    cols = lambda h: slice(h * HEAD_DIM, (h + 1) * HEAD_DIM)

    @pl.when(i == 0)
    def _():
        dk[...] = jnp.zeros_like(dk)
        dv[...] = jnp.zeros_like(dv)

    here = pl.ds(pl.multiple_of(i * block, block), block)
    docs_q = drow_ref[...]
    ones = jnp.ones((8, HEAD_DIM), jnp.float32)
    queries = [qkv_ref[here, part(h, 0)] for h in range(heads)]
    grads = [g_ref[:, cols(h)] for h in range(heads)]
    deltas = [
        lax.dot_general(ones, grads[h].astype(jnp.float32) * o_ref[:, cols(h)].astype(jnp.float32), NT,
                        precision=lax.Precision.HIGHEST, preferred_element_type=jnp.float32)[:1]
        for h in range(heads)
    ]
    gap = lax.broadcasted_iota(jnp.int32, (block, block), 1) - lax.broadcasted_iota(jnp.int32, (block, block), 0)

    def body(j, carry):
        rows = pl.ds(pl.multiple_of(j * block, block), block)
        allowed = (docs_q == dcol_ref[rows, :]) & (gap >= (j - i) * block)
        new = []
        for h in range(heads):
            q, g = queries[h], grads[h]
            k = qkv_ref[rows, part(h, 1)]
            s = lax.dot_general(k, q, NT, preferred_element_type=jnp.float32) * scale
            p = jnp.exp(jnp.where(allowed, s - lse_ref[h], -1e30))
            dp = lax.dot_general(qkv_ref[rows, part(h, 2)], g, NT, preferred_element_type=jnp.float32)
            ds = (p * (dp - deltas[h]) * scale).astype(jnp.bfloat16)
            dv[rows, cols(h)] += jnp.dot(p.astype(jnp.bfloat16), g, preferred_element_type=jnp.float32)
            dk[rows, cols(h)] += jnp.dot(ds, q, preferred_element_type=jnp.float32)
            new.append(carry[h] + lax.dot_general(ds, k, TN, preferred_element_type=jnp.float32))
        return tuple(new)

    dq = lax.fori_loop(0, i + 1, body, (jnp.zeros((block, HEAD_DIM), jnp.float32),) * heads)

    def put(rows, first, val):
        rot = rot_tiles(rot_ref[:, rows])
        out_ref[rows, first : first + LANES] = rotate_back_tile(val[:, :LANES], *rot).astype(jnp.bfloat16)
        out_ref[rows, first + LANES : first + HEAD_DIM] = val[:, LANES:].astype(jnp.bfloat16)

    for h in range(heads):
        put(here, 3 * h * HEAD_DIM, dq[h])

    @pl.when(i == n - 1)
    def _():
        for h in range(heads):
            for b in range(n):
                rows = slice(b * block, (b + 1) * block)
                put(rows, (3 * h + 1) * HEAD_DIM, dk[rows, cols(h)])
                out_ref[rows, part(h, 2)] = dv[rows, cols(h)].astype(jnp.bfloat16)


def attend_back(qkv, grad_att, attended, docs, lse, rot, block=512):
    total, cols = qkv.shape
    heads = cols // (3 * HEAD_DIM)
    seqs = total // SEQ_LEN
    n = SEQ_LEN // block
    whole = pl.BlockSpec((SEQ_LEN, cols), lambda s, i: (s, 0))
    mine = pl.BlockSpec((block, heads * HEAD_DIM), lambda s, i: (s * n + i, 0))
    table = pl.BlockSpec((ROT_DIM, SEQ_LEN), lambda s, i: (0, s))
    return pl.pallas_call(
        functools.partial(attend_back_kernel, block, n, heads),
        grid=(seqs, n),
        in_specs=[
            whole, mine, mine,
            pl.BlockSpec((SEQ_LEN, 1), lambda s, i: (s, 0)),
            pl.BlockSpec((1, block), lambda s, i: (0, s * n + i)),
            pl.BlockSpec((heads, 1, block), lambda s, i: (0, 0, s * n + i)),
            table,
        ],
        out_specs=whole,
        out_shape=jax.ShapeDtypeStruct((total, cols), jnp.bfloat16),
        scratch_shapes=[pltpu.VMEM((SEQ_LEN, heads * HEAD_DIM), jnp.float32)] * 2,
        compiler_params=pltpu.CompilerParams(vmem_limit_bytes=VMEM_CAP),
        cost_estimate=pl.CostEstimate(flops=5 * total * SEQ_LEN * heads * HEAD_DIM, bytes_accessed=8 * total * cols, transcendentals=total * SEQ_LEN),
        name="attend_back",
    )(qkv, grad_att, attended, docs[:, None], docs[None, :], lse, rot)


def on_device(tokens, segments, positions, ln1_gain, ln1_bias, ln2_gain, ln2_bias, qkv_weight, dense_weight, fc1_weight, fc2_weight, upstream):
    n = lax.axis_size(AX)
    left = lax.ppermute(upstream, AX, [(i, i + 1) for i in range(n - 1)])
    right = lax.ppermute(upstream, AX, [(i + 1, i) for i in range(n - 1)])
    rot = rot_tables(positions)
    h_one, h_two, qkv, stats = project(tokens, ln1_gain, ln1_bias, ln2_gain, ln2_bias, rot, qkv_weight)
    attended, lse = attend(qkv, segments, 1024)
    up, hidden, grad_pre, grad_h_two, grad_att, output = feed_forward(
        h_two, attended, fc1_weight, fc2_weight, dense_weight, upstream, left, right, tokens)
    grad_qkv = attend_back(qkv, grad_att, attended, segments, lse, rot)
    groups = [
        dict(x=0, y=0, count=grad_pre.shape[1] // STRIP, turned=True, out=2),
        dict(x=1, y=1, count=hidden.shape[1] // STRIP, turned=False, out=3),
        dict(x=2, y=1, count=attended.shape[1] // STRIP, turned=False, out=1),
        dict(x=3, y=2, count=grad_qkv.shape[1] // STRIP, turned=True, out=0),
    ]
    s, norm_grads, qkv_grad, dense_grad, fc1_grad, fc2_grad = back_sums(
        tokens, stats, grad_h_two, jnp.stack([ln1_gain, ln2_gain]), qkv_weight, [grad_pre, hidden, attended, grad_qkv], [h_two, up, h_one], groups)
    input_grad = finish(tokens, stats, s, up)
    return (
        output, input_grad, qkv_grad, dense_grad, fc1_grad, fc2_grad,
        norm_grads[0], norm_grads[1], norm_grads[2], norm_grads[3],
    )


def solution(mesh):
    in_specs = (
        P("dp", None),
        P("dp"),
        P("dp"),
        P(),
        P(),
        P(),
        P(),
        P(None, "tensor"),
        P("tensor", None),
        P(None, "tensor"),
        P("tensor", None),
        P("dp", "tensor"),
    )
    out_specs = (
        P("dp", "tensor"),
        P("dp", None),
        P("dp", "tensor"),
        P("tensor", "dp"),
        P("dp", "tensor"),
        P("tensor", "dp"),
        P("dp"),
        P("dp"),
        P("dp"),
        P("dp"),
    )
    return jax.shard_map(
        on_device, mesh=mesh, in_specs=in_specs, out_specs=out_specs, check_vma=False
    )
```

```python
import functools
import itertools

import jax
import jax.numpy as jnp
from jax import lax
from jax.experimental import pallas as pl
from jax.experimental.pallas import tpu as pltpu
from jax.sharding import PartitionSpec as P

HEAD_DIM = 256
ROT_DIM = 64
SEQ_LEN = 2048
LANES = 128
VMEM_CAP = 60 * 2**20
NT = (((1,), (1,)), ((), ()))
TN = (((0,), (0,)), ((), ()))


def rot_tables(positions):
    half = ROT_DIM // 2
    steps_up = jnp.arange(half).astype(jnp.float32) * 2.0 / ROT_DIM
    inverse = jnp.power(jnp.float32(10000.0), -steps_up)
    angle = inverse[:, None] * positions.astype(jnp.float32)[None, :]
    return jnp.concatenate([jnp.cos(angle), jnp.sin(angle)], 0)


def rot_tiles(table):
    half = ROT_DIM // 2
    cos, sin = table[:half], table[half:]
    zero = jnp.zeros_like(sin)
    rest = jnp.zeros((LANES - ROT_DIM, table.shape[1]), jnp.float32)
    rows = ((cos, cos, rest + 1.0), (-sin, zero, rest), (zero, sin, rest))
    return tuple(jnp.concatenate(parts, 0).T for parts in rows)


def rotate_tile(u, cos_t, sin_up, sin_down):
    half = ROT_DIM // 2
    return u * cos_t + pltpu.roll(u, LANES - half, 1) * sin_up + pltpu.roll(u, half, 1) * sin_down


def rotate_back_tile(g, cos_t, sin_up, sin_down):
    half = ROT_DIM // 2
    return g * cos_t + pltpu.roll(g * sin_down, LANES - half, 1) + pltpu.roll(g * sin_up, half, 1)


def pre_kernel(x_ref, g1_ref, b1_ref, g2_ref, b2_ref, rot_ref, w_ref, h1_ref, h2_ref, qkv_ref, stats_ref):
    x = x_ref[...].astype(jnp.float32)
    mean = jnp.mean(x, axis=-1, keepdims=True)
    center = x - mean
    inv = lax.rsqrt(jnp.mean(center * center, axis=-1, keepdims=True) + 1e-05)
    stats_ref[:, :1] = mean
    stats_ref[:, 1:] = inv
    normed = center * inv
    h1 = (normed * g1_ref[...] + b1_ref[...]).astype(jnp.bfloat16)
    h1_ref[...] = h1
    h2_ref[...] = (normed * g2_ref[...] + b2_ref[...]).astype(jnp.bfloat16)
    cos_t, su, sd = rot_tiles(rot_ref[...])
    for b in range(w_ref.shape[1] // HEAD_DIM):
        cols = slice(b * HEAD_DIM, (b + 1) * HEAD_DIM)
        y = jnp.dot(h1, w_ref[:, cols], preferred_element_type=jnp.float32)
        if b % 3 < 2:
            qkv_ref[:, b * HEAD_DIM : b * HEAD_DIM + LANES] = rotate_tile(y[:, :LANES], cos_t, su, sd).astype(jnp.bfloat16)
            qkv_ref[:, b * HEAD_DIM + LANES : (b + 1) * HEAD_DIM] = y[:, LANES:].astype(jnp.bfloat16)
        else:
            qkv_ref[:, cols] = y.astype(jnp.bfloat16)


def project(tokens, g1, b1, g2, b2, rot, w, rows=512):
    total, width = tokens.shape
    rows = min(rows, total)
    row_blk = lambda cols: pl.BlockSpec((rows, cols), lambda i: (i, 0))
    vec = pl.BlockSpec((1, width), lambda i: (0, 0))
    cols = w.shape[1]
    return pl.pallas_call(
        pre_kernel,
        grid=(total // rows,),
        in_specs=[row_blk(width), vec, vec, vec, vec, pl.BlockSpec((ROT_DIM, rows), lambda i: (0, i)),
                  pl.BlockSpec((width, cols), lambda i: (0, 0), pipeline_mode=pl.Buffered(1))],
        out_specs=[row_blk(width), row_blk(width), row_blk(cols), row_blk(2)],
        out_shape=[jax.ShapeDtypeStruct((total, width), jnp.bfloat16)] * 2 + [jax.ShapeDtypeStruct((total, cols), jnp.bfloat16), jax.ShapeDtypeStruct((total, 2), jnp.float32)],
        compiler_params=pltpu.CompilerParams(vmem_limit_bytes=VMEM_CAP),
        cost_estimate=pl.CostEstimate(flops=2 * total * width * cols, bytes_accessed=6 * total * width + 2 * cols * (width + total), transcendentals=0),
        name="norm_project",
    )(tokens, g1[None], b1[None], g2[None], b2[None], rot, w)


def attend_kernel(block, heads, qkv_ref, drow_ref, dcol_ref, o_ref, lse_ref, v_turned):
    i = pl.program_id(1)
    scale = HEAD_DIM ** (-0.5)
    part = lambda h, c: slice((3 * h + c) * HEAD_DIM, (3 * h + c + 1) * HEAD_DIM)

    @pl.when(i == 0)
    def _():
        for h in range(heads):
            v_turned[h] = qkv_ref[:, part(h, 2)].T

    here = pl.ds(pl.multiple_of(i * block, block), block)
    queries = [qkv_ref[here, part(h, 0)] * jnp.bfloat16(scale) for h in range(heads)]
    docs_q = drow_ref[...]
    later = lax.broadcasted_iota(jnp.int32, (block, block), 1) >= lax.broadcasted_iota(jnp.int32, (block, block), 0)

    def body(j, carry, corner=False):
        rows = pl.ds(pl.multiple_of(j * block, block), block)
        allowed = docs_q == dcol_ref[rows, :]
        if corner:
            allowed = allowed & later
        new = []
        for h in range(heads):
            m, l, acc = carry[h]
            s = lax.dot_general(qkv_ref[rows, part(h, 1)], queries[h], NT, preferred_element_type=jnp.float32)
            s = jnp.where(allowed, s, -1e30)
            m_new = jnp.maximum(m, jnp.max(s, axis=0, keepdims=True))
            p = jnp.exp(s - m_new)
            alpha = jnp.exp(m - m_new)
            l = l * alpha + jnp.sum(p, axis=0, keepdims=True)
            acc = acc * alpha + jnp.dot(v_turned[h, :, rows], p.astype(jnp.bfloat16), preferred_element_type=jnp.float32)
            new.append((m_new, l, acc))
        return tuple(new)

    start = (jnp.full((1, block), -1e30, jnp.float32), jnp.zeros((1, block), jnp.float32), jnp.zeros((HEAD_DIM, block), jnp.float32))
    carry = body(i, lax.fori_loop(0, i, body, (start,) * heads), True)
    for h in range(heads):
        m, l, acc = carry[h]
        o_ref[:, h * HEAD_DIM : (h + 1) * HEAD_DIM] = (acc * (1.0 / l)).T.astype(jnp.bfloat16)
        lse_ref[h] = m + jnp.log(l)


def attend(qkv, docs, block=512):
    total, cols = qkv.shape
    heads = cols // (3 * HEAD_DIM)
    seqs = total // SEQ_LEN
    n = SEQ_LEN // block
    return pl.pallas_call(
        functools.partial(attend_kernel, block, heads),
        grid=(seqs, n),
        in_specs=[
            pl.BlockSpec((SEQ_LEN, cols), lambda s, i: (s, 0)),
            pl.BlockSpec((1, block), lambda s, i: (0, s * n + i)),
            pl.BlockSpec((SEQ_LEN, 1), lambda s, i: (s, 0)),
        ],
        out_specs=[pl.BlockSpec((block, heads * HEAD_DIM), lambda s, i: (s * n + i, 0)),
                   pl.BlockSpec((heads, 1, block), lambda s, i: (0, 0, s * n + i))],
        out_shape=[jax.ShapeDtypeStruct((total, heads * HEAD_DIM), jnp.bfloat16), jax.ShapeDtypeStruct((heads, 1, total), jnp.float32)],
        scratch_shapes=[pltpu.VMEM((heads, HEAD_DIM, SEQ_LEN), jnp.bfloat16)],
        compiler_params=pltpu.CompilerParams(vmem_limit_bytes=VMEM_CAP),
        cost_estimate=pl.CostEstimate(flops=2 * total * SEQ_LEN * heads * HEAD_DIM, bytes_accessed=4 * total * cols, transcendentals=total * SEQ_LEN),
        name="attend",
    )(qkv, docs[None, :], docs[:, None])


def finish_kernel(x_ref, stats_ref, s_ref, up_ref, out_ref):
    mean, inv = stats_ref[:, :1], stats_ref[:, 1:]
    s = s_ref[...].astype(jnp.float32)
    center = x_ref[...].astype(jnp.float32) - mean
    bend = jnp.mean(s * center, axis=-1, keepdims=True) * (inv * inv * inv)
    level = jnp.mean(s, axis=-1, keepdims=True) * inv
    out_ref[...] = (up_ref[...].astype(jnp.float32) - level) + (s * inv - center * bend)


def finish(tokens, stats, s, up, rows=512):
    total, width = tokens.shape
    block = pl.BlockSpec((min(rows, total), width), lambda i: (i, 0))
    return pl.pallas_call(
        finish_kernel,
        grid=(total // min(rows, total),),
        in_specs=[block, pl.BlockSpec((min(rows, total), 2), lambda i: (i, 0)), block, block],
        out_specs=block,
        out_shape=jax.ShapeDtypeStruct((total, width), jnp.float32),
        compiler_params=pltpu.CompilerParams(vmem_limit_bytes=VMEM_CAP),
        cost_estimate=pl.CostEstimate(flops=10 * total * width, bytes_accessed=10 * total * width, transcendentals=0),
        name="finish",
    )(tokens, stats, s, up)


AX = "tensor"
DP = "dp"
MESH = pl.DeviceIdType.MESH
STRIP = 256


def greet(peers):
    barrier = pltpu.get_barrier_semaphore()
    count = 0
    for cond, device in peers:
        @pl.when(cond)
        def _(device=device):
            pl.semaphore_signal(barrier, inc=1, device_id=device, device_id_type=MESH)
        count = count + jnp.asarray(cond).astype(jnp.int32)
    pl.semaphore_wait(barrier, count)


def within(c, count):
    return (c >= 0) & (c < count)


def blend(first, second):
    both = [(place / len(one), which, entry) for which, one in enumerate((first, second)) for place, entry in enumerate(one)]
    return [entry for _, _, entry in sorted(both, key=lambda e: e[:2])]


class LineSum:
    def __init__(self, n, chunks, full_ref, own, recv, rs_send, rs_recv, ag_right, ag_left, ag_recv, store_sem):
        self.n, self.chunks, self.full_ref, self.own, self.recv = n, chunks, full_ref, own, recv
        self.rs_send, self.rs_recv, self.ag_send, self.ag_recv, self.store_sem = rs_send, rs_recv, (ag_right, ag_left), ag_recv, store_sem
        self.k = lax.axis_index(AX)
        self.rows, self.cols = own.shape[2], own.shape[3]

    def block(self, c, j):
        return self.full_ref.at[pl.ds(pl.multiple_of(c * self.rows, self.rows), self.rows), pl.ds(j * self.cols, self.cols)]

    def copy(self, src, dst, send, recv, right):
        return pltpu.make_async_remote_copy(src, dst, send, recv, device_id={AX: self.k + 1 if right else self.k - 1}, device_id_type=MESH)

    def scatter_copy(self, c, j, right):
        slot = j if right else jnp.where(self.k - 1 == j, self.n, j)
        return self.copy(self.own.at[c, j], self.recv.at[c, slot], self.rs_send.at[c, j], self.rs_recv.at[c, slot], right)

    def scatter_arrived(self, c, slot):
        dst = self.recv.at[c, slot]
        pltpu.make_async_copy(dst, dst, self.rs_recv.at[c, slot]).wait()

    def gather_copy(self, c, j, right, src=None):
        block = self.block(c, j)
        return self.copy(block if src is None else src, block, self.ag_send[0 if right else 1].at[c, j], self.ag_recv.at[c, j], right)

    def gather_arrived(self, c, j):
        block = self.block(c, j)
        pltpu.make_async_copy(block, block, self.ag_recv.at[c, j]).wait()

    def store(self, c, j):
        return pltpu.make_async_copy(self.own.at[c, j], self.block(c, j), self.store_sem.at[c])

    def pieces(self, i):
        return [functools.partial(self.pass_on, i, p) for p in range(self.n)] + [functools.partial(self.close, i)]

    def pass_on(self, i, p):
        n, k, chunks = self.n, self.k, self.chunks
        for right in (True, False):
            j = p if right else n - 1 - p
            dist = (k - j) if right else (j - k)
            onward = (k < n - 1) if right else (k > 0)
            behind = (k > 0) if right else (k < n - 1)
            c_gather = i - (n - 1) - dist
            c_scatter = i - (k if right else n - 1 - k)

            @pl.when((dist > 0) & within(c_gather, chunks))
            def _(j=j, right=right, c=c_gather, onward=onward):
                self.gather_arrived(c, j)

                @pl.when(onward)
                def _():
                    self.gather_copy(c, j, right).start()

            @pl.when((dist < 0) & within(c_scatter, chunks))
            def _(j=j, right=right, c=c_scatter, behind=behind):
                @pl.when(behind)
                def _():
                    self.scatter_arrived(c, j)
                    self.own[c, j] = self.own[c, j] + self.recv[c, j]

                self.scatter_copy(c, j, right).start()

    def close(self, i):
        n, k, chunks = self.n, self.k, self.chunks
        c = i - (n - 1)
        for j in range(n):
            @pl.when((k == j) & within(c, chunks))
            def _(j=j):
                total = self.own[c, j].astype(jnp.float32)
                if j > 0:
                    self.scatter_arrived(c, j)
                    total = total + self.recv[c, j].astype(jnp.float32)
                if j < n - 1:
                    self.scatter_arrived(c, n)
                    total = total + self.recv[c, n].astype(jnp.float32)
                self.own[c, j] = total.astype(self.own.dtype)
                self.store(c, j).start()
                if j < n - 1:
                    self.gather_copy(c, j, True, self.own.at[c, j]).start()
                if j > 0:
                    self.gather_copy(c, j, False, self.own.at[c, j]).start()

    def drain(self):
        n, k = self.n, self.k

        def one(c, _):
            for j in range(n):
                @pl.when(k < j)
                def _(j=j):
                    self.scatter_copy(c, j, True).wait_send()

                    @pl.when(k > 0)
                    def _():
                        self.gather_copy(c, j, False).wait_send()

                @pl.when(k > j)
                def _(j=j):
                    self.scatter_copy(c, j, False).wait_send()

                    @pl.when(k < n - 1)
                    def _():
                        self.gather_copy(c, j, True).wait_send()

                @pl.when(k == j)
                def _(j=j):
                    self.store(c, j).wait()
                    if j < n - 1:
                        self.gather_copy(c, j, True, self.own.at[c, j]).wait_send()
                    if j > 0:
                        self.gather_copy(c, j, False, self.own.at[c, j]).wait_send()
            return 0

        lax.fori_loop(0, self.chunks, one, 0)


class HalvingSum:
    def __init__(self, dp, groups, xs, ys, outs, xbuf, ybuf, tiles, recvs, stage, stage_turned, x_sem, y_sem, send_sem, recv_sem, out_sem):
        self.dp, self.bits = dp, dp.bit_length() - 1
        self.groups, self.xs, self.ys, self.outs = groups, xs, ys, outs
        self.xbuf, self.ybuf, self.tiles, self.recvs = xbuf, ybuf, tiles, recvs
        self.stage, self.stage_turned = stage, stage_turned
        self.x_sem, self.y_sem, self.send_sem, self.recv_sem, self.out_sem = x_sem, y_sem, send_sem, recv_sem, out_sem
        self.me = lax.axis_index(DP)
        self.slots = tiles.shape[0]
        self.width = tiles.shape[-1]
        self.first = [sum(g["count"] for g in groups[:i]) for i in range(len(groups) + 1)]
        self.total = self.first[-1]
        self.lags = [1] + [1 + 2 * level for level in range(1, self.bits - 1)] + [max(2 * self.bits - 2, 2)]

    def bit(self, b):
        return lax.rem(lax.div(self.me, 2**b), 2)

    def partner(self, b):
        return self.me + (1 - 2 * self.bit(b)) * 2**b

    def order(self, odd):
        rest = list(range(1, self.bits))
        return [0] + (rest[1:] + rest[:1] if odd else rest)

    def pick(self, odd, level, value):
        done = self.order(odd)[:level]
        now = self.order(odd)[level]
        return tuple(0 if b in done else value if b == now else slice(None) for b in range(self.bits))

    def in_group(self, t, g):
        return (t >= self.first[g]) & (t < self.first[g + 1])

    def x_copies(self, t):
        for g, group in enumerate(self.groups):
            at = pl.ds(pl.multiple_of((t - self.first[g]) * STRIP, STRIP), STRIP)
            slot = lax.rem(t, 2)
            yield self.in_group(t, g), pltpu.make_async_copy(self.xs[group["x"]].at[:, at], self.xbuf.at[slot], self.x_sem.at[slot])

    def x_start(self, t):
        for cond, copy in self.x_copies(t):
            @pl.when(cond)
            def _(copy=copy):
                copy.start()

    def x_wait(self, t):
        slot = lax.rem(t, 2)
        pltpu.make_async_copy(self.xbuf.at[slot], self.xbuf.at[slot], self.x_sem.at[slot]).wait()

    def y_copy(self, g):
        y = self.groups[g]["y"]
        return pltpu.make_async_copy(self.ys[y], self.ybuf.at[y % 2], self.y_sem.at[y % 2])

    def send(self, u, odd, level):
        slot = lax.rem(u, self.slots)
        return pltpu.make_async_remote_copy(
            self.tiles.at[(slot, *self.pick(odd, level, 1))], self.recvs[level].at[slot],
            self.send_sem.at[level, slot], self.recv_sem.at[level, slot],
            device_id={DP: self.partner(self.order(odd)[level])}, device_id_type=MESH)

    def out_copies(self, u):
        slot = lax.rem(u, 2)
        for g, group in enumerate(self.groups):
            at = pl.ds(pl.multiple_of((u - self.first[g]) * STRIP, STRIP), STRIP)
            out = self.outs[group["out"]]
            if group["turned"]:
                yield self.in_group(u, g), pltpu.make_async_copy(self.stage_turned.at[slot], out.at[:, at], self.out_sem.at[slot])
            else:
                yield self.in_group(u, g), pltpu.make_async_copy(self.stage.at[slot], out.at[at, :], self.out_sem.at[slot])

    def out_wait(self, u):
        for cond, copy in self.out_copies(u):
            @pl.when(cond)
            def _(copy=copy):
                copy.wait()

    def prologue(self):
        self.x_start(jnp.int32(0))
        self.y_copy(0).start()
        for g in range(1, len(self.groups)):
            if self.groups[g]["y"] == 1:
                self.y_copy(g).start()
                break

    def pieces(self, t, place, period, parts=4):
        odd = place % 2
        share = max(self.dp // parts, 1)
        spans = [range(first, first + share) for first in range(0, self.dp, share)]
        return [functools.partial(self.halve, t, place, period)] + [
            functools.partial(self.multiply, t, place, period, span, span[0] == 0, span[-1] == self.dp - 1) for span in spans]

    def halve(self, t, place, period):
        for level in range(self.bits - 1, -1, -1):
            u = t - self.lags[level]
            u_odd = (place - self.lags[level]) % period % 2

            @pl.when(within(u, self.total))
            def _(u=u, u_odd=u_odd, level=level):
                slot = lax.rem(u, self.slots)
                got = self.recvs[level]
                pltpu.make_async_copy(got.at[slot], got.at[slot], self.recv_sem.at[level, slot]).wait()
                keep = (slot, *self.pick(u_odd, level, 0))
                if level < self.bits - 1:
                    left = [range(2) if isinstance(p, slice) else (p,) for p in keep[1:]]
                    for flat, idx in enumerate(itertools.product(*left)):
                        pos = tuple(int(b) for b in format(flat, "b").zfill(self.bits - 1 - level))
                        self.tiles[(slot, *idx)] = self.tiles[(slot, *idx)] + got[(slot, *pos)]
                    self.send(u, u_odd, level + 1).start()
                else:
                    @pl.when(u >= 2)
                    def _():
                        self.out_wait(u - 2)

                    value = self.tiles[keep].astype(jnp.float32) + got[slot].astype(jnp.float32)
                    for g, group in enumerate(self.groups):
                        @pl.when(self.in_group(u, g))
                        def _(group=group):
                            if group["turned"]:
                                self.stage_turned[lax.rem(u, 2)] = value.T
                            else:
                                self.stage[lax.rem(u, 2)] = value
                    for cond, copy in self.out_copies(u):
                        @pl.when(cond)
                        def _(copy=copy):
                            copy.start()

    def ready(self, t, place, period):
        @pl.when(t >= self.slots)
        def _():
            for level in range(self.bits):
                self.send(t - self.slots, (place - self.slots) % period % 2, level).wait_send()

        seen = []
        for g, group in enumerate(self.groups):
            if group["y"] in seen:
                continue
            seen.append(group["y"])

            @pl.when(t == self.first[g])
            def _(g=g, group=group):
                self.y_copy(g).wait()
                if group["y"] == 1:
                    for later in range(len(self.groups)):
                        if self.groups[later]["y"] == 2:
                            self.y_copy(later).start()
                            break

        @pl.when(t + 1 < self.total)
        def _():
            self.x_start(t + 1)

        self.x_wait(t)

    def multiply(self, t, place, period, span, opens, closes):
        @pl.when(within(t, self.total))
        def _():
            if opens:
                self.ready(t, place, period)
            slot = lax.rem(t, self.slots)
            y_slot = jnp.int32(0)
            for g, group in enumerate(self.groups):
                y_slot = jnp.where(t >= self.first[g], group["y"] % 2, y_slot)
            x = self.xbuf[lax.rem(t, 2)]
            for flat in span:
                idx = tuple((flat >> b) & 1 for b in range(self.bits))
                shard = sum((self.bit(b) + idx[b] * (1 - 2 * self.bit(b))) * 2**b for b in range(self.bits))
                at = pl.ds(pl.multiple_of(shard * self.width, self.width), self.width)
                self.tiles[(slot, *idx)] = lax.dot_general(x, self.ybuf[y_slot, :, at], TN, preferred_element_type=jnp.float32).astype(jnp.bfloat16)
            if closes:
                self.send(t, place % 2, 0).start()

    def drain(self, period):
        for u in range(self.total - self.slots, self.total):
            for level in range(self.bits):
                self.send(jnp.int32(u), u % period % 2, level).wait_send()
        for u in range(self.total - 2, self.total):
            self.out_wait(jnp.int32(u))


class LineScatter:
    def __init__(self, n, own, recv, x_own, out_ref, send_sem, recv_sem, store_sem, hop=1):
        self.hop = hop
        self.n, self.own, self.recv, self.x_own, self.out_ref = n, own, recv, x_own, out_ref
        self.send_sem, self.recv_sem, self.store_sem = send_sem, recv_sem, store_sem
        self.k = lax.axis_index(AX)
        self.chunks, _, self.rows, self.cols = own.shape

    def span(self, c):
        return pl.ds(pl.multiple_of(c * self.rows, self.rows), self.rows)

    def copy(self, c, j, right):
        slot = j if right else jnp.where(self.k - 1 == j, self.n, j)
        return pltpu.make_async_remote_copy(
            self.own.at[c, j], self.recv.at[c, slot], self.send_sem.at[c, j], self.recv_sem.at[c, slot],
            device_id={AX: self.k + 1 if right else self.k - 1}, device_id_type=MESH)

    def arrived(self, c, slot):
        got = self.recv.at[c, slot]
        pltpu.make_async_copy(got, got, self.recv_sem.at[c, slot]).wait()

    def store(self, c, j):
        return pltpu.make_async_copy(self.own.at[c, j], self.out_ref.at[self.span(c), :], self.store_sem.at[c])

    def pieces(self, i):
        return [functools.partial(self.pass_on, i, p) for p in range(self.n)] + [functools.partial(self.close, i)]

    def step(self, i):
        for piece in self.pieces(i):
            piece()

    def pass_on(self, i, p):
        n, k = self.n, self.k
        for right in (True, False):
            j = p if right else n - 1 - p
            ahead = (j > k) if right else (j < k)
            behind = (k > 0) if right else (k < n - 1)
            c = i - self.hop * (k if right else n - 1 - k)

            @pl.when(ahead & within(c, self.chunks))
            def _(j=j, right=right, c=c, behind=behind):
                @pl.when(behind)
                def _():
                    self.arrived(c, j)
                    self.own[c, j] = self.own[c, j] + self.recv[c, j]

                self.copy(c, j, right).start()

    def close(self, i):
        n, k = self.n, self.k
        c = i - self.hop * (n - 1)
        for j in range(n):
            @pl.when((k == j) & within(c, self.chunks))
            def _(j=j):
                total = self.x_own[self.span(c), :].astype(jnp.float32) + self.own[c, j].astype(jnp.float32)
                if j > 0:
                    self.arrived(c, j)
                    total = total + self.recv[c, j].astype(jnp.float32)
                if j < n - 1:
                    self.arrived(c, n)
                    total = total + self.recv[c, n].astype(jnp.float32)
                self.own[c, j] = total.astype(self.own.dtype)
                self.store(c, j).start()

    def drain(self):
        def one(c, _):
            for j in range(self.n):
                @pl.when(self.k < j)
                def _(j=j):
                    self.copy(c, j, True).wait_send()

                @pl.when(self.k > j)
                def _(j=j):
                    self.copy(c, j, False).wait_send()

                @pl.when(self.k == j)
                def _(j=j):
                    self.store(c, j).wait()
            return 0

        lax.fori_loop(0, self.chunks, one, 0)


def scatter_scratch(n, chunks, rows, cols):
    low, dma = jnp.bfloat16, pltpu.SemaphoreType.DMA
    return [pltpu.VMEM((chunks, n, rows, cols), low), pltpu.VMEM((chunks, n + 1, rows, cols), low), pltpu.VMEM((chunks * rows, cols), low),
            dma((chunks, n)), dma((chunks, n + 1)), dma((chunks,))]


class Stream:
    def __init__(self, hbm, slots, sem, inward):
        self.hbm, self.slots, self.sem, self.inward = hbm, slots, sem, inward
        self.rows = slots.shape[1]

    def copy(self, p):
        at = self.hbm.at[pl.ds(pl.multiple_of(p * self.rows, self.rows), self.rows), :]
        slot = lax.rem(p, 2)
        pair = (at, self.slots.at[slot]) if self.inward else (self.slots.at[slot], at)
        return pltpu.make_async_copy(*pair, self.sem.at[slot])


class Terms:
    def __init__(self, n, own, sums, w, gains, streams):
        self.n, self.own, self.sums, self.w, self.gains, self.streams = n, own, sums, w, gains, streams
        self.rows, self.cols = streams[0].rows, own.shape[3]
        self.blocks = own.shape[0] * own.shape[2] // self.rows

    def start(self, i):
        for stream in self.streams:
            stream.copy(i).start()

    def pieces(self, i):
        return [functools.partial(self.tile, i, j) for j in range(self.n)]

    def tile(self, i, j):
        @pl.when(i < self.blocks)
        def _():
            if j == 0:
                @pl.when(i + 1 < self.blocks)
                def _():
                    self.start(i + 1)

                for stream in self.streams:
                    stream.copy(i).wait()
            two = lax.rem(i, 2)
            x, stats, gq, gh2 = (stream.slots for stream in self.streams)
            at = slice(j * self.cols, (j + 1) * self.cols)
            mean, inv = stats[two, :, :1], stats[two, :, 1:]
            one = lax.dot_general(gq[two], self.w[at, :], NT, preferred_element_type=jnp.float32)
            other = gh2[two, :, at].astype(jnp.float32)
            normed = (x[two, :, at].astype(jnp.float32) - mean) * inv
            total = (one * self.gains[:1, at] + other * self.gains[1:, at]).astype(self.own.dtype)
            height = self.own.shape[2]
            for b in range(self.rows // height):
                self.own[i * (self.rows // height) + b, j] = total[b * height : (b + 1) * height]
            for row, value in enumerate((one * normed, one, other * normed, other)):
                self.sums[row : row + 1, at] += jnp.sum(value, axis=0, keepdims=True)


class SmallSum:
    def __init__(self, n, bits, partner, out_ref, acc, dp_recv, line_send, line_recv, sems):
        self.n, self.bits, self.partner = n, bits, partner
        self.out_ref, self.acc, self.dp_recv, self.line_send, self.line_recv = out_ref, acc, dp_recv, line_send, line_recv
        self.dp_send_sem, self.dp_recv_sem, self.line_send_sem, self.line_recv_sem, self.own_sem = sems
        self.k, self.me = lax.axis_index(AX), lax.axis_index(DP)

    def last(self):
        return pltpu.make_async_copy(self.dp_recv.at[0, :, pl.ds(0, self.out_ref.shape[1])], self.out_ref, self.own_sem.at[0])

    def swap(self, b):
        return pltpu.make_async_remote_copy(
            self.acc, self.dp_recv.at[b], self.dp_send_sem.at[b], self.dp_recv_sem.at[b], device_id={DP: self.partner(b)}, device_id_type=MESH)

    def onward(self, way):
        return pltpu.make_async_remote_copy(
            self.line_send.at[way], self.line_recv.at[way], self.line_send_sem.at[way], self.line_recv_sem.at[way],
            device_id={AX: self.k + 1 - 2 * way}, device_id_type=MESH)

    def step(self, i):
        n, k = self.n, self.k
        for b in range(self.bits + 1):
            @pl.when(i == b)
            def _(b=b):
                if b > 0:
                    self.swap(b - 1).wait()
                    self.acc[...] = self.acc[...] + self.dp_recv[b - 1]
                if b < self.bits:
                    self.swap(b).start()
        for way in range(2):
            place = k if way == 0 else n - 1 - k

            @pl.when(i == self.bits + 1 + place)
            def _(way=way, place=place):
                self.line_send[way] = self.acc[...]

                @pl.when(place > 0)
                def _():
                    got = self.line_recv.at[way]
                    pltpu.make_async_copy(got, got, self.line_recv_sem.at[way]).wait()
                    self.line_send[way] = self.acc[...] + self.line_recv[way]

                @pl.when(place < n - 1)
                def _():
                    self.onward(way).start()

        @pl.when(i == self.bits + 1 + n)
        def _():
            self.acc[...] = self.line_send[0] + self.line_send[1] - self.acc[...]
            part = self.out_ref.shape[1]
            self.dp_recv[0, :, :part] = self.acc[:, pl.ds(pl.multiple_of(self.me * part, part), part)]
            self.last().start()

    def drain(self):
        @pl.when(self.k < self.n - 1)
        def _():
            self.onward(0).wait_send()

        @pl.when(self.k > 0)
        def _():
            self.onward(1).wait_send()

        self.last().wait()


def sums_kernel(n, dp, chunks, steps, ticks, groups, n_x, n_y, n_out, *refs):
    refs = list(refs)
    take = lambda count: [refs.pop(0) for _ in range(count)]
    x_ref, stats_ref, gh2_ref, gains, w_ref = take(5)
    xs, ys = take(n_x), take(n_y)
    full_ref, sum_ref = take(2)
    outs = take(n_out)
    own, recv, *line_sems = take(8)
    bits = dp.bit_length() - 1
    xbuf, ybuf, tiles = take(3)
    recvs = take(bits)
    rest = take(7)
    small_bufs, small_sems = take(4), take(5)
    k, me = lax.axis_index(AX), lax.axis_index(DP)
    line = LineSum(n, chunks, full_ref, own, recv, *line_sems)
    halving = HalvingSum(dp, groups, xs, ys, outs, xbuf, ybuf, tiles, recvs, *rest)
    small = SmallSum(n, bits, halving.partner, sum_ref, *small_bufs, small_sems)
    w, w_sem = take(2)
    streams = [Stream(ref, *take(2), True) for ref in (x_ref, stats_ref, xs[-1], gh2_ref)]
    terms = Terms(n, own, small_bufs[0], w, gains, streams)
    small_first = chunks

    w_copy = pltpu.make_async_copy(w_ref, w, w_sem.at[0])
    w_copy.start()
    terms.start(jnp.int32(0))
    halving.prologue()
    greet([(k > 0, {AX: k - 1}), (k < n - 1, {AX: k + 1})] + [(me >= 0, {DP: halving.partner(b)}) for b in range(bits)])

    small_bufs[0][...] = jnp.zeros_like(small_bufs[0])
    w_copy.wait()
    for piece in terms.pieces(jnp.int32(0)):
        piece()

    def small_step(c):
        @pl.when(c >= small_first)
        def _():
            small.step(2 * (c - small_first))
            small.step(2 * (c - small_first) + 1)

    def body(i, _):
        lines, strips = [], []
        for e in range(steps):
            c = steps * i + e
            lines += line.pieces(c)
            lines.append(functools.partial(small_step, c))
        for place in range(ticks):
            strips += halving.pieces(ticks * i + place, place, ticks)
        strips = blend(strips, terms.pieces(i + 1))
        for piece in blend(lines, strips):
            piece()
        return 0

    lax.fori_loop(0, max(-(-max(chunks + 2 * (n - 1), small_first + (bits + n + 3) // 2) // steps), -(-(halving.total + halving.lags[-1]) // ticks)), body, 0)
    line.drain()
    halving.drain(ticks)
    small.drain()


def back_sums(tokens, stats, grad_h2, gains, w_qkv, xs, ys, groups, chunks=16, slots=5, steps=2, ticks=3):
    n, dp = lax.axis_size(AX), lax.axis_size(DP)
    bits = dp.bit_length() - 1
    total, width = tokens.shape
    rows, cols = total // chunks, width // n
    w = width // dp
    block = steps * rows
    two = lambda cols, kind=jnp.bfloat16: [pltpu.VMEM((2, block, cols), kind), pltpu.SemaphoreType.DMA((2,))]
    dma = pltpu.SemaphoreType.DMA
    out_shapes = [None] * len(groups)
    for g in groups:
        size = xs[g["x"]].shape[1]
        out_shapes[g["out"]] = jax.ShapeDtypeStruct((w, size) if g["turned"] else (size, w), jnp.float32)
    anywhere = pl.BlockSpec(memory_space=pl.ANY)
    vmem = pltpu.VMEM
    low = jnp.bfloat16
    return pl.pallas_call(
        functools.partial(sums_kernel, n, dp, chunks, steps, ticks, groups, len(xs), len(ys), len(out_shapes)),
        out_shape=[jax.ShapeDtypeStruct(tokens.shape, low), jax.ShapeDtypeStruct((8, w), jnp.float32)] + out_shapes,
        in_specs=[anywhere] * 3 + [pl.BlockSpec(memory_space=vmem)] + [anywhere] * (1 + len(xs) + len(ys)),
        out_specs=[anywhere] * (2 + len(out_shapes)),
        scratch_shapes=[
            vmem((chunks, n, rows, cols), low), vmem((chunks, n + 1, rows, cols), low),
            dma((chunks, n)), dma((chunks, n + 1)), dma((chunks, n)), dma((chunks, n)), dma((chunks, n)), dma((chunks,)),
            vmem((2, total, STRIP), low), vmem((2, total, width), low), vmem((slots, *(2,) * bits, STRIP, w), low),
            *[vmem((slots, *(2,) * (bits - 1 - level), STRIP, w), low) for level in range(bits)],
            vmem((2, STRIP, w), jnp.float32), vmem((2, w, STRIP), jnp.float32),
            dma((2,)), dma((2,)), dma((bits, slots)), dma((bits, slots)), dma((2,)),
            vmem((8, width), jnp.float32), vmem((bits, 8, width), jnp.float32), vmem((2, 8, width), jnp.float32), vmem((2, 8, width), jnp.float32),
            dma((bits,)), dma((bits,)), dma((2,)), dma((2,)), dma((1,)),
            vmem(w_qkv.shape, low), dma((1,)), *two(width), *two(2, jnp.float32), *two(w_qkv.shape[1]), *two(width),
        ],
        compiler_params=pltpu.CompilerParams(collective_id=0, has_side_effects=True, vmem_limit_bytes=62 * 2**20),
        name="back_sums",
    )(tokens, stats, grad_h2, gains, w_qkv, *xs, *ys)


class LineGather:
    def __init__(self, n, chunks, rows, near_left, near_right, up_ref, right_sem, left_sem, recv_sem, hop):
        self.hop = hop
        self.n, self.chunks, self.rows, self.cols = n, chunks, rows, near_left.shape[1]
        self.near, self.up_ref, self.send_sem, self.recv_sem = (near_left, near_right), up_ref, (right_sem, left_sem), recv_sem
        self.k = lax.axis_index(AX)

    def span(self, c):
        return pl.ds(pl.multiple_of(c * self.rows, self.rows), self.rows)

    def block(self, c, j):
        return self.up_ref.at[self.span(c), pl.ds(j * self.cols, self.cols)]

    def copy(self, c, j, right, near):
        src = self.near[0 if right else 1].at[self.span(c), :] if near else self.block(c, j)
        return pltpu.make_async_remote_copy(
            src, self.block(c, j), self.send_sem[0 if right else 1].at[c, j], self.recv_sem.at[c, j],
            device_id={AX: self.k + 1 if right else self.k - 1}, device_id_type=MESH)

    def arrived(self, c, j):
        block = self.block(c, j)
        pltpu.make_async_copy(block, block, self.recv_sem.at[c, j]).wait()

    def pieces(self, i):
        return [functools.partial(self.pass_on, i, p) for p in range(self.n)]

    def pass_on(self, i, p):
        n, k = self.n, self.k
        for right in (True, False):
            j = p if right else n - 1 - p
            dist = (k - j) if right else (j - k)
            onward = (k < n - 1) if right else (k > 0)
            far = i - self.hop * (dist - 1)

            @pl.when((dist == 1) & onward & within(i, self.chunks))
            def _(j=j, right=right):
                self.copy(i, j, right, True).start()

            @pl.when((dist > 1) & within(far, self.chunks))
            def _(j=j, right=right, c=far, onward=onward):
                self.arrived(c, j)

                @pl.when(onward)
                def _():
                    self.copy(c, j, right, False).start()

    def drain(self):
        def one(c, _):
            for j in range(self.n):
                @pl.when((self.k > j) & (self.k < self.n - 1))
                def _(j=j):
                    self.copy(c, j, True, False).wait_send()

                @pl.when((self.k < j) & (self.k > 0))
                def _(j=j):
                    self.copy(c, j, False, False).wait_send()
            return 0

        lax.fori_loop(0, self.chunks, one, 0)


def gelu_and_slope(x):
    share = 0.5 * (1.0 + lax.erf(x * (0.5**0.5)))
    return x * share, share + x * (jnp.exp(-0.5 * x * x) * (2.0 * jnp.pi) ** -0.5)


def feed_kernel(
    n, chunks, tile, hop,
    h2_ref, att_ref, fc1_ref, fc2_ref, dense_ref, up_own_ref, left_ref, right_ref, x_ref,
    up_ref, hidden_ref, grad_pre_ref, grad_h2_ref, grad_att_ref, out_ref,
    own, recv, x_own, rs_send, rs_recv, out_sem, fc1, fc2, dense, h2_buf, att_buf, up_buf, hid_buf, gp_buf, gh_buf, ga_buf, slope,
    weight_sem, near_sem, h2_sem, att_sem, up_sem, hid_sem, gp_sem, gh_sem, ga_sem, *line_sems,
):
    k = lax.axis_index(AX)
    low = jnp.bfloat16
    rows = h2_buf.shape[1]
    blocks = h2_ref.shape[0] // rows
    per_block = rows // own.shape[2]
    lag = -(-(2 + hop * (n - 2)) // 2)
    cols = own.shape[3]
    rate = 3

    gather = LineGather(n, chunks, own.shape[2], left_ref, right_ref, up_ref, *line_sems, hop)
    scatter = LineScatter(n, own, recv, x_own, out_ref, rs_send, rs_recv, out_sem, hop)

    def gather_step(i):
        for piece in gather.pieces(i):
            piece()

    h2_in, att_in = Stream(h2_ref, h2_buf, h2_sem, True), Stream(att_ref, att_buf, att_sem, True)
    hid_out, gp_out = Stream(hidden_ref, hid_buf, hid_sem, False), Stream(grad_pre_ref, gp_buf, gp_sem, False)
    gh_out, ga_out = Stream(grad_h2_ref, gh_buf, gh_sem, False), Stream(grad_att_ref, ga_buf, ga_sem, False)

    h2_in.copy(jnp.int32(0)).start()
    att_in.copy(jnp.int32(0)).start()
    weights = [pltpu.make_async_copy(a, b, weight_sem.at[w]) for w, (a, b) in enumerate(((fc1_ref, fc1), (dense_ref, dense), (fc2_ref, fc2), (x_ref.at[:, pl.ds(pl.multiple_of(k * own.shape[3], own.shape[3]), own.shape[3])], x_own)))]
    for copy in weights:
        copy.start()

    def up_pieces(q):
        at, two = pl.ds(pl.multiple_of(q * rows, rows), rows), lax.rem(q, 2)
        for j in range(n):
            span = pl.ds(j * cols, cols)
            dst = up_buf.at[two, :, span]
            for cond, src in ((k == j, up_own_ref), (k - 1 == j, left_ref), (k + 1 == j, right_ref)):
                yield cond, True, pltpu.make_async_copy(src.at[at, :], dst, up_sem.at[two, j]), pltpu.make_async_copy(dst, up_ref.at[at, span], near_sem.at[two, j])
            far = (k - j > 1) | (j - k > 1)
            yield far, False, pltpu.make_async_copy(up_ref.at[at, span], dst, up_sem.at[two, j]), None

    def up_start(q):
        for cond, _, load, _ in up_pieces(q):
            @pl.when(cond)
            def _(load=load):
                load.start()

    def up_wait(q):
        for cond, near, load, put in up_pieces(q):
            @pl.when(cond)
            def _(near=near, load=load, put=put):
                load.wait()
                if near:
                    put.start()

    def up_put_wait(q):
        for cond, near, _, put in up_pieces(q):
            if near:
                @pl.when(cond)
                def _(put=put):
                    put.wait()

    greet([(k > 0, {AX: k - 1}), (k < n - 1, {AX: k + 1})])

    def forward(p):
        @pl.when(p + 1 < blocks)
        def _():
            h2_in.copy(p + 1).start()
            att_in.copy(p + 1).start()

        @pl.when(p == 0)
        def _():
            weights[0].wait()

        @pl.when(p >= 2)
        def _():
            hid_out.copy(p - 2).wait()

        h2_in.copy(p).wait()
        att_in.copy(p).wait()
        two = lax.rem(p, 2)
        keep = lax.rem(p, lag + 1)
        h2 = h2_buf[two]
        for t in range(0, fc1.shape[1], tile):
            hid, bend = gelu_and_slope(jnp.dot(h2, fc1[:, t : t + tile], preferred_element_type=jnp.float32))
            hid_buf[two, :, t : t + tile] = hid.astype(low)
            slope[keep, :, t : t + tile] = bend.astype(low)
        hid_out.copy(p).start()

        @pl.when(p == 0)
        def _():
            for copy in weights[1:]:
                copy.wait()

        att, hid = att_buf[two], hid_buf[two]
        for j in range(n):
            part = jnp.dot(hid, fc2[:, j * cols : (j + 1) * cols], preferred_element_type=jnp.float32)
            part = (part + jnp.dot(att, dense[:, j * cols : (j + 1) * cols], preferred_element_type=jnp.float32)).astype(low)
            for b in range(per_block):
                own[per_block * p + b, j] = part[b * own.shape[2] : (b + 1) * own.shape[2]]

    def backward(q):
        @pl.when(q >= 2)
        def _():
            for stream in (gp_out, gh_out, ga_out):
                stream.copy(q - 2).wait()

        up_wait(q)
        two = lax.rem(q, 2)
        keep = lax.rem(q, lag + 1)
        up = up_buf[two]
        ga_buf[two] = lax.dot_general(up, dense[...], NT, preferred_element_type=jnp.float32).astype(low)
        ga_out.copy(q).start()
        for t in range(0, fc2.shape[0], tile):
            grad = lax.dot_general(up, fc2[t : t + tile, :], NT, preferred_element_type=jnp.float32)
            gp_buf[two, :, t : t + tile] = (grad * slope[keep, :, t : t + tile].astype(jnp.float32)).astype(low)
        gp_out.copy(q).start()
        grad_pre = gp_buf[two]
        for t in range(0, fc1.shape[0], tile):
            gh_buf[two, :, t : t + tile] = lax.dot_general(grad_pre, fc1[t : t + tile, :], NT, preferred_element_type=jnp.float32).astype(low)
        gh_out.copy(q).start()

    def body(p, _):
        @pl.when(p < blocks)
        def _():
            forward(p)

        gather_step(per_block * p)
        scatter.step(lax.div(rate * p, 2))

        @pl.when(within(p - lag, blocks))
        def _():
            backward(p - lag)

        for b in range(1, per_block):
            gather_step(per_block * p + b)

        @pl.when(lax.div(rate * (p + 1), 2) - lax.div(rate * p, 2) > 1)
        def _():
            scatter.step(lax.div(rate * p, 2) + 1)

        @pl.when(within(p + 1 - lag, blocks))
        def _():
            @pl.when(p + 1 - lag >= 2)
            def _():
                up_put_wait(p - 1 - lag)

            up_start(p + 1 - lag)

        return 0

    lax.fori_loop(0, max(blocks + lag, -(-(chunks + hop * (n - 2)) // per_block), -(-2 * (scatter.chunks + hop * (n - 1)) // rate)), body, 0)
    for last in range(max(blocks - 2, 0), blocks):
        for stream in (hid_out, gp_out, gh_out, ga_out):
            stream.copy(jnp.int32(last)).wait()
        up_put_wait(jnp.int32(last))
    gather.drain()
    scatter.drain()


def feed_forward(h2, attended, fc1, fc2, dense, upstream, left, right, tokens, rows=256, chunks=16, tile=512, hop=2):
    n = lax.axis_size(AX)
    total, width = h2.shape
    hidden, heads_width, cols = fc1.shape[1], attended.shape[1], width // n
    low, dma, vmem = jnp.bfloat16, pltpu.SemaphoreType.DMA, pltpu.VMEM
    piece = total // chunks
    lag = -(-(2 + hop * (n - 2)) // 2)
    tile = min(tile, hidden)
    anywhere = pl.BlockSpec(memory_space=pl.ANY)
    shape = lambda cols: jax.ShapeDtypeStruct((total, cols), low)
    two = lambda cols: vmem((2, rows, cols), low)
    return pl.pallas_call(
        functools.partial(feed_kernel, n, chunks, tile, hop),
        out_shape=[shape(width), shape(hidden), shape(hidden), shape(width), shape(heads_width), shape(cols)],
        in_specs=[anywhere] * 9,
        out_specs=[anywhere] * 6,
        scratch_shapes=[
            *scatter_scratch(n, chunks, piece, cols),
            vmem(fc1.shape, low), vmem(fc2.shape, low), vmem(dense.shape, low),
            two(width), two(heads_width), two(width), two(hidden), two(hidden), two(width), two(heads_width), vmem((lag + 1, rows, hidden), low),
            dma((4,)), dma((2, n)), dma((2,)), dma((2,)), dma((2, n)), dma((2,)), dma((2,)), dma((2,)), dma((2,)),
            dma((chunks, n)), dma((chunks, n)), dma((chunks, n)),
        ],
        compiler_params=pltpu.CompilerParams(collective_id=1, has_side_effects=True, vmem_limit_bytes=VMEM_CAP),
        name="feed_forward",
    )(h2, attended, fc1, fc2, dense, upstream, left, right, tokens)


def attend_back_kernel(block, n, heads, qkv_ref, g_ref, o_ref, dcol_ref, drow_ref, lse_ref, rot_ref, out_ref, dk, dv):
    i = pl.program_id(1)
    scale = HEAD_DIM ** (-0.5)
    part = lambda h, c: slice((3 * h + c) * HEAD_DIM, (3 * h + c + 1) * HEAD_DIM)
    cols = lambda h: slice(h * HEAD_DIM, (h + 1) * HEAD_DIM)

    @pl.when(i == 0)
    def _():
        dk[...] = jnp.zeros_like(dk)
        dv[...] = jnp.zeros_like(dv)

    here = pl.ds(pl.multiple_of(i * block, block), block)
    docs_q = drow_ref[...]
    ones = jnp.ones((8, HEAD_DIM), jnp.float32)
    queries = [qkv_ref[here, part(h, 0)] * jnp.bfloat16(scale) for h in range(heads)]
    grads = [g_ref[:, cols(h)] for h in range(heads)]
    deltas = [
        lax.dot_general(ones, grads[h].astype(jnp.float32) * o_ref[:, cols(h)].astype(jnp.float32), NT,
                        precision=lax.Precision.HIGHEST, preferred_element_type=jnp.float32)[:1]
        for h in range(heads)
    ]
    later = lax.broadcasted_iota(jnp.int32, (block, block), 1) >= lax.broadcasted_iota(jnp.int32, (block, block), 0)

    def body(j, carry, corner=False):
        rows = pl.ds(pl.multiple_of(j * block, block), block)
        allowed = docs_q == dcol_ref[rows, :]
        if corner:
            allowed = allowed & later
        new = []
        for h in range(heads):
            q, g = queries[h], grads[h]
            k = qkv_ref[rows, part(h, 1)]
            s = lax.dot_general(k, q, NT, preferred_element_type=jnp.float32)
            p = jnp.exp(jnp.where(allowed, s - lse_ref[h], -1e30))
            dp = lax.dot_general(qkv_ref[rows, part(h, 2)], g, NT, preferred_element_type=jnp.float32)
            ds = (p * (dp - deltas[h])).astype(jnp.bfloat16)
            dv[rows, cols(h)] += jnp.dot(p.astype(jnp.bfloat16), g, preferred_element_type=jnp.float32)
            dk[rows, cols(h)] += jnp.dot(ds, q, preferred_element_type=jnp.float32)
            new.append(carry[h] + lax.dot_general(ds, k, TN, preferred_element_type=jnp.float32))
        return tuple(new)

    dq = body(i, lax.fori_loop(0, i, body, (jnp.zeros((block, HEAD_DIM), jnp.float32),) * heads), True)

    def put(rows, first, val):
        rot = rot_tiles(rot_ref[:, rows])
        out_ref[rows, first : first + LANES] = rotate_back_tile(val[:, :LANES], *rot).astype(jnp.bfloat16)
        out_ref[rows, first + LANES : first + HEAD_DIM] = val[:, LANES:].astype(jnp.bfloat16)

    for h in range(heads):
        put(here, 3 * h * HEAD_DIM, dq[h] * scale)

    @pl.when(i == n - 1)
    def _():
        for h in range(heads):
            for b in range(n):
                rows = slice(b * block, (b + 1) * block)
                put(rows, (3 * h + 1) * HEAD_DIM, dk[rows, cols(h)])
                out_ref[rows, part(h, 2)] = dv[rows, cols(h)].astype(jnp.bfloat16)


def attend_back(qkv, grad_att, attended, docs, lse, rot, block=512):
    total, cols = qkv.shape
    heads = cols // (3 * HEAD_DIM)
    seqs = total // SEQ_LEN
    n = SEQ_LEN // block
    whole = pl.BlockSpec((SEQ_LEN, cols), lambda s, i: (s, 0))
    mine = pl.BlockSpec((block, heads * HEAD_DIM), lambda s, i: (s * n + i, 0))
    table = pl.BlockSpec((ROT_DIM, SEQ_LEN), lambda s, i: (0, s))
    return pl.pallas_call(
        functools.partial(attend_back_kernel, block, n, heads),
        grid=(seqs, n),
        in_specs=[
            whole, mine, mine,
            pl.BlockSpec((SEQ_LEN, 1), lambda s, i: (s, 0)),
            pl.BlockSpec((1, block), lambda s, i: (0, s * n + i)),
            pl.BlockSpec((heads, 1, block), lambda s, i: (0, 0, s * n + i)),
            table,
        ],
        out_specs=whole,
        out_shape=jax.ShapeDtypeStruct((total, cols), jnp.bfloat16),
        scratch_shapes=[pltpu.VMEM((SEQ_LEN, heads * HEAD_DIM), jnp.float32)] * 2,
        compiler_params=pltpu.CompilerParams(vmem_limit_bytes=VMEM_CAP),
        cost_estimate=pl.CostEstimate(flops=5 * total * SEQ_LEN * heads * HEAD_DIM, bytes_accessed=8 * total * cols, transcendentals=total * SEQ_LEN),
        name="attend_back",
    )(qkv, grad_att, attended, docs[:, None], docs[None, :], lse, rot)


def on_device(tokens, segments, positions, ln1_gain, ln1_bias, ln2_gain, ln2_bias, qkv_weight, dense_weight, fc1_weight, fc2_weight, upstream):
    n = lax.axis_size(AX)
    left = lax.ppermute(upstream, AX, [(i, i + 1) for i in range(n - 1)])
    right = lax.ppermute(upstream, AX, [(i + 1, i) for i in range(n - 1)])
    rot = rot_tables(positions)
    h_one, h_two, qkv, stats = project(tokens, ln1_gain, ln1_bias, ln2_gain, ln2_bias, rot, qkv_weight)
    attended, lse = attend(qkv, segments, 1024)
    up, hidden, grad_pre, grad_h_two, grad_att, output = feed_forward(
        h_two, attended, fc1_weight, fc2_weight, dense_weight, upstream, left, right, tokens)
    grad_qkv = attend_back(qkv, grad_att, attended, segments, lse, rot)
    groups = [
        dict(x=0, y=0, count=grad_pre.shape[1] // STRIP, turned=True, out=2),
        dict(x=1, y=1, count=hidden.shape[1] // STRIP, turned=False, out=3),
        dict(x=2, y=1, count=attended.shape[1] // STRIP, turned=False, out=1),
        dict(x=3, y=2, count=grad_qkv.shape[1] // STRIP, turned=True, out=0),
    ]
    s, norm_grads, qkv_grad, dense_grad, fc1_grad, fc2_grad = back_sums(
        tokens, stats, grad_h_two, jnp.stack([ln1_gain, ln2_gain]), qkv_weight, [grad_pre, hidden, attended, grad_qkv], [h_two, up, h_one], groups)
    input_grad = finish(tokens, stats, s, up)
    return (
        output, input_grad, qkv_grad, dense_grad, fc1_grad, fc2_grad,
        norm_grads[0], norm_grads[1], norm_grads[2], norm_grads[3],
    )


def solution(mesh):
    in_specs = (
        P("dp", None),
        P("dp"),
        P("dp"),
        P(),
        P(),
        P(),
        P(),
        P(None, "tensor"),
        P("tensor", None),
        P(None, "tensor"),
        P("tensor", None),
        P("dp", "tensor"),
    )
    out_specs = (
        P("dp", "tensor"),
        P("dp", None),
        P("dp", "tensor"),
        P("tensor", "dp"),
        P("dp", "tensor"),
        P("tensor", "dp"),
        P("dp"),
        P("dp"),
        P("dp"),
        P("dp"),
    )
    return jax.shard_map(
        on_device, mesh=mesh, in_specs=in_specs, out_specs=out_specs, check_vma=False
    )
```

```python
import functools
import itertools

import jax
import jax.numpy as jnp
from jax import lax
from jax.experimental import pallas as pl
from jax.experimental.pallas import tpu as pltpu
from jax.sharding import PartitionSpec as P

HEAD_DIM = 256
ROT_DIM = 64
SEQ_LEN = 2048
LANES = 128
VMEM_CAP = 60 * 2**20
NT = (((1,), (1,)), ((), ()))
TN = (((0,), (0,)), ((), ()))


def rot_tables(positions):
    half = ROT_DIM // 2
    steps_up = jnp.arange(half).astype(jnp.float32) * 2.0 / ROT_DIM
    inverse = jnp.power(jnp.float32(10000.0), -steps_up)
    angle = inverse[:, None] * positions.astype(jnp.float32)[None, :]
    return jnp.concatenate([jnp.cos(angle), jnp.sin(angle)], 0)


def rot_tiles(table):
    half = ROT_DIM // 2
    cos, sin = table[:half], table[half:]
    zero = jnp.zeros_like(sin)
    rest = jnp.zeros((LANES - ROT_DIM, table.shape[1]), jnp.float32)
    rows = ((cos, cos, rest + 1.0), (-sin, zero, rest), (zero, sin, rest))
    return tuple(jnp.concatenate(parts, 0).T for parts in rows)


def rotate_tile(u, cos_t, sin_up, sin_down):
    half = ROT_DIM // 2
    return u * cos_t + pltpu.roll(u, LANES - half, 1) * sin_up + pltpu.roll(u, half, 1) * sin_down


def rotate_back_tile(g, cos_t, sin_up, sin_down):
    half = ROT_DIM // 2
    return g * cos_t + pltpu.roll(g * sin_down, LANES - half, 1) + pltpu.roll(g * sin_up, half, 1)


def pre_kernel(x_ref, g1_ref, b1_ref, g2_ref, b2_ref, rot_ref, w_ref, h1_ref, h2_ref, qkv_ref, stats_ref):
    x = x_ref[...].astype(jnp.float32)
    mean = jnp.mean(x, axis=-1, keepdims=True)
    center = x - mean
    inv = lax.rsqrt(jnp.mean(center * center, axis=-1, keepdims=True) + 1e-05)
    stats_ref[:, :1] = mean
    stats_ref[:, 1:] = inv
    normed = center * inv
    h1 = (normed * g1_ref[...] + b1_ref[...]).astype(jnp.bfloat16)
    h1_ref[...] = h1
    h2_ref[...] = (normed * g2_ref[...] + b2_ref[...]).astype(jnp.bfloat16)
    cos_t, su, sd = rot_tiles(rot_ref[...])
    for b in range(w_ref.shape[1] // HEAD_DIM):
        cols = slice(b * HEAD_DIM, (b + 1) * HEAD_DIM)
        y = jnp.dot(h1, w_ref[:, cols], preferred_element_type=jnp.float32)
        if b % 3 < 2:
            qkv_ref[:, b * HEAD_DIM : b * HEAD_DIM + LANES] = rotate_tile(y[:, :LANES], cos_t, su, sd).astype(jnp.bfloat16)
            qkv_ref[:, b * HEAD_DIM + LANES : (b + 1) * HEAD_DIM] = y[:, LANES:].astype(jnp.bfloat16)
        else:
            qkv_ref[:, cols] = y.astype(jnp.bfloat16)


def project(tokens, g1, b1, g2, b2, rot, w, rows=512):
    total, width = tokens.shape
    rows = min(rows, total)
    row_blk = lambda cols: pl.BlockSpec((rows, cols), lambda i: (i, 0))
    vec = pl.BlockSpec((1, width), lambda i: (0, 0))
    cols = w.shape[1]
    return pl.pallas_call(
        pre_kernel,
        grid=(total // rows,),
        in_specs=[row_blk(width), vec, vec, vec, vec, pl.BlockSpec((ROT_DIM, rows), lambda i: (0, i)),
                  pl.BlockSpec((width, cols), lambda i: (0, 0), pipeline_mode=pl.Buffered(1))],
        out_specs=[row_blk(width), row_blk(width), row_blk(cols), row_blk(2)],
        out_shape=[jax.ShapeDtypeStruct((total, width), jnp.bfloat16)] * 2 + [jax.ShapeDtypeStruct((total, cols), jnp.bfloat16), jax.ShapeDtypeStruct((total, 2), jnp.float32)],
        compiler_params=pltpu.CompilerParams(vmem_limit_bytes=VMEM_CAP),
        cost_estimate=pl.CostEstimate(flops=2 * total * width * cols, bytes_accessed=6 * total * width + 2 * cols * (width + total), transcendentals=0),
        name="norm_project",
    )(tokens, g1[None], b1[None], g2[None], b2[None], rot, w)


def attend_kernel(block, heads, qkv_ref, drow_ref, dcol_ref, o_ref, lse_ref, v_turned):
    i = pl.program_id(1)
    scale = HEAD_DIM ** (-0.5)
    part = lambda h, c: slice((3 * h + c) * HEAD_DIM, (3 * h + c + 1) * HEAD_DIM)

    @pl.when(i == 0)
    def _():
        for h in range(heads):
            v_turned[h] = qkv_ref[:, part(h, 2)].T

    here = pl.ds(pl.multiple_of(i * block, block), block)
    queries = [qkv_ref[here, part(h, 0)] * jnp.bfloat16(scale) for h in range(heads)]
    docs_q = drow_ref[...]
    later = lax.broadcasted_iota(jnp.int32, (block, block), 1) >= lax.broadcasted_iota(jnp.int32, (block, block), 0)

    def body(j, carry, corner=False):
        rows = pl.ds(pl.multiple_of(j * block, block), block)
        allowed = docs_q == dcol_ref[rows, :]
        if corner:
            allowed = allowed & later
        new = []
        for h in range(heads):
            m, l, acc = carry[h]
            s = lax.dot_general(qkv_ref[rows, part(h, 1)], queries[h], NT, preferred_element_type=jnp.float32)
            s = jnp.where(allowed, s, -1e30)
            m_new = jnp.maximum(m, jnp.max(s, axis=0, keepdims=True))
            p = jnp.exp(s - m_new)
            alpha = jnp.exp(m - m_new)
            l = l * alpha + jnp.sum(p, axis=0, keepdims=True)
            acc = acc * alpha + jnp.dot(v_turned[h, :, rows], p.astype(jnp.bfloat16), preferred_element_type=jnp.float32)
            new.append((m_new, l, acc))
        return tuple(new)

    start = (jnp.full((1, block), -1e30, jnp.float32), jnp.zeros((1, block), jnp.float32), jnp.zeros((HEAD_DIM, block), jnp.float32))
    carry = body(i, lax.fori_loop(0, i, body, (start,) * heads), True)
    for h in range(heads):
        m, l, acc = carry[h]
        o_ref[:, h * HEAD_DIM : (h + 1) * HEAD_DIM] = (acc * (1.0 / l)).T.astype(jnp.bfloat16)
        lse_ref[h] = m + jnp.log(l)


def attend(qkv, docs, block=512):
    total, cols = qkv.shape
    heads = cols // (3 * HEAD_DIM)
    seqs = total // SEQ_LEN
    n = SEQ_LEN // block
    return pl.pallas_call(
        functools.partial(attend_kernel, block, heads),
        grid=(seqs, n),
        in_specs=[
            pl.BlockSpec((SEQ_LEN, cols), lambda s, i: (s, 0)),
            pl.BlockSpec((1, block), lambda s, i: (0, s * n + i)),
            pl.BlockSpec((SEQ_LEN, 1), lambda s, i: (s, 0)),
        ],
        out_specs=[pl.BlockSpec((block, heads * HEAD_DIM), lambda s, i: (s * n + i, 0)),
                   pl.BlockSpec((heads, 1, block), lambda s, i: (0, 0, s * n + i))],
        out_shape=[jax.ShapeDtypeStruct((total, heads * HEAD_DIM), jnp.bfloat16), jax.ShapeDtypeStruct((heads, 1, total), jnp.float32)],
        scratch_shapes=[pltpu.VMEM((heads, HEAD_DIM, SEQ_LEN), jnp.bfloat16)],
        compiler_params=pltpu.CompilerParams(vmem_limit_bytes=VMEM_CAP),
        cost_estimate=pl.CostEstimate(flops=2 * total * SEQ_LEN * heads * HEAD_DIM, bytes_accessed=4 * total * cols, transcendentals=total * SEQ_LEN),
        name="attend",
    )(qkv, docs[None, :], docs[:, None])


def finish_kernel(x_ref, stats_ref, s_ref, up_ref, out_ref):
    mean, inv = stats_ref[:, :1], stats_ref[:, 1:]
    s = s_ref[...].astype(jnp.float32)
    center = x_ref[...].astype(jnp.float32) - mean
    bend = jnp.mean(s * center, axis=-1, keepdims=True) * (inv * inv * inv)
    level = jnp.mean(s, axis=-1, keepdims=True) * inv
    out_ref[...] = (up_ref[...].astype(jnp.float32) - level) + (s * inv - center * bend)


def finish(tokens, stats, s, up, rows=512):
    total, width = tokens.shape
    block = pl.BlockSpec((min(rows, total), width), lambda i: (i, 0))
    return pl.pallas_call(
        finish_kernel,
        grid=(total // min(rows, total),),
        in_specs=[block, pl.BlockSpec((min(rows, total), 2), lambda i: (i, 0)), block, block],
        out_specs=block,
        out_shape=jax.ShapeDtypeStruct((total, width), jnp.float32),
        compiler_params=pltpu.CompilerParams(vmem_limit_bytes=VMEM_CAP),
        cost_estimate=pl.CostEstimate(flops=10 * total * width, bytes_accessed=10 * total * width, transcendentals=0),
        name="finish",
    )(tokens, stats, s, up)


AX = "tensor"
DP = "dp"
MESH = pl.DeviceIdType.MESH
STRIP = 256


def greet(peers):
    barrier = pltpu.get_barrier_semaphore()
    count = 0
    for cond, device in peers:
        @pl.when(cond)
        def _(device=device):
            pl.semaphore_signal(barrier, inc=1, device_id=device, device_id_type=MESH)
        count = count + jnp.asarray(cond).astype(jnp.int32)
    pl.semaphore_wait(barrier, count)


def within(c, count):
    return (c >= 0) & (c < count)


def blend(first, second):
    both = [(place / len(one), which, entry) for which, one in enumerate((first, second)) for place, entry in enumerate(one)]
    return [entry for _, _, entry in sorted(both, key=lambda e: e[:2])]


class LineSum:
    def __init__(self, n, chunks, full_ref, own, recv, rs_send, rs_recv, ag_right, ag_left, ag_recv, store_sem):
        self.n, self.chunks, self.full_ref, self.own, self.recv = n, chunks, full_ref, own, recv
        self.rs_send, self.rs_recv, self.ag_send, self.ag_recv, self.store_sem = rs_send, rs_recv, (ag_right, ag_left), ag_recv, store_sem
        self.k = lax.axis_index(AX)
        self.rows, self.cols = own.shape[2], own.shape[3]

    def block(self, c, j):
        return self.full_ref.at[pl.ds(pl.multiple_of(c * self.rows, self.rows), self.rows), pl.ds(j * self.cols, self.cols)]

    def copy(self, src, dst, send, recv, right):
        return pltpu.make_async_remote_copy(src, dst, send, recv, device_id={AX: self.k + 1 if right else self.k - 1}, device_id_type=MESH)

    def scatter_copy(self, c, j, right):
        slot = j if right else jnp.where(self.k - 1 == j, self.n, j)
        return self.copy(self.own.at[c, j], self.recv.at[c, slot], self.rs_send.at[c, j], self.rs_recv.at[c, slot], right)

    def scatter_arrived(self, c, slot):
        dst = self.recv.at[c, slot]
        pltpu.make_async_copy(dst, dst, self.rs_recv.at[c, slot]).wait()

    def gather_copy(self, c, j, right, src=None):
        block = self.block(c, j)
        return self.copy(block if src is None else src, block, self.ag_send[0 if right else 1].at[c, j], self.ag_recv.at[c, j], right)

    def gather_arrived(self, c, j):
        block = self.block(c, j)
        pltpu.make_async_copy(block, block, self.ag_recv.at[c, j]).wait()

    def store(self, c, j):
        return pltpu.make_async_copy(self.own.at[c, j], self.block(c, j), self.store_sem.at[c])

    def pieces(self, i):
        return [functools.partial(self.pass_on, i, p) for p in range(self.n)] + [functools.partial(self.close, i)]

    def pass_on(self, i, p):
        n, k, chunks = self.n, self.k, self.chunks
        for right in (True, False):
            j = p if right else n - 1 - p
            dist = (k - j) if right else (j - k)
            onward = (k < n - 1) if right else (k > 0)
            behind = (k > 0) if right else (k < n - 1)
            c_gather = i - (n - 1) - dist
            c_scatter = i - (k if right else n - 1 - k)

            @pl.when((dist > 0) & within(c_gather, chunks))
            def _(j=j, right=right, c=c_gather, onward=onward):
                self.gather_arrived(c, j)

                @pl.when(onward)
                def _():
                    self.gather_copy(c, j, right).start()

            @pl.when((dist < 0) & within(c_scatter, chunks))
            def _(j=j, right=right, c=c_scatter, behind=behind):
                @pl.when(behind)
                def _():
                    self.scatter_arrived(c, j)
                    self.own[c, j] = self.own[c, j] + self.recv[c, j]

                self.scatter_copy(c, j, right).start()

    def close(self, i):
        n, k, chunks = self.n, self.k, self.chunks
        c = i - (n - 1)
        for j in range(n):
            @pl.when((k == j) & within(c, chunks))
            def _(j=j):
                total = self.own[c, j].astype(jnp.float32)
                if j > 0:
                    self.scatter_arrived(c, j)
                    total = total + self.recv[c, j].astype(jnp.float32)
                if j < n - 1:
                    self.scatter_arrived(c, n)
                    total = total + self.recv[c, n].astype(jnp.float32)
                self.own[c, j] = total.astype(self.own.dtype)
                self.store(c, j).start()
                if j < n - 1:
                    self.gather_copy(c, j, True, self.own.at[c, j]).start()
                if j > 0:
                    self.gather_copy(c, j, False, self.own.at[c, j]).start()

    def drain(self):
        n, k = self.n, self.k

        def one(c, _):
            for j in range(n):
                @pl.when(k < j)
                def _(j=j):
                    self.scatter_copy(c, j, True).wait_send()

                    @pl.when(k > 0)
                    def _():
                        self.gather_copy(c, j, False).wait_send()

                @pl.when(k > j)
                def _(j=j):
                    self.scatter_copy(c, j, False).wait_send()

                    @pl.when(k < n - 1)
                    def _():
                        self.gather_copy(c, j, True).wait_send()

                @pl.when(k == j)
                def _(j=j):
                    self.store(c, j).wait()
                    if j < n - 1:
                        self.gather_copy(c, j, True, self.own.at[c, j]).wait_send()
                    if j > 0:
                        self.gather_copy(c, j, False, self.own.at[c, j]).wait_send()
            return 0

        lax.fori_loop(0, self.chunks, one, 0)


class HalvingSum:
    def __init__(self, dp, groups, xs, ys, outs, xbuf, ybuf, tiles, recvs, stage, stage_turned, x_sem, y_sem, send_sem, recv_sem, out_sem):
        self.dp, self.bits = dp, dp.bit_length() - 1
        self.groups, self.xs, self.ys, self.outs = groups, xs, ys, outs
        self.xbuf, self.ybuf, self.tiles, self.recvs = xbuf, ybuf, tiles, recvs
        self.stage, self.stage_turned = stage, stage_turned
        self.x_sem, self.y_sem, self.send_sem, self.recv_sem, self.out_sem = x_sem, y_sem, send_sem, recv_sem, out_sem
        self.me = lax.axis_index(DP)
        self.slots = tiles.shape[0]
        self.width = tiles.shape[-1]
        self.first = [sum(g["count"] for g in groups[:i]) for i in range(len(groups) + 1)]
        self.total = self.first[-1]
        self.lags = [1] + [1 + 2 * level for level in range(1, self.bits - 1)] + [max(2 * self.bits - 2, 2)]

    def bit(self, b):
        return lax.rem(lax.div(self.me, 2**b), 2)

    def partner(self, b):
        return self.me + (1 - 2 * self.bit(b)) * 2**b

    def order(self, odd):
        rest = list(range(1, self.bits))
        return [0] + (rest[1:] + rest[:1] if odd else rest)

    def pick(self, odd, level, value):
        done = self.order(odd)[:level]
        now = self.order(odd)[level]
        return tuple(0 if b in done else value if b == now else slice(None) for b in range(self.bits))

    def in_group(self, t, g):
        return (t >= self.first[g]) & (t < self.first[g + 1])

    def x_copies(self, t):
        for g, group in enumerate(self.groups):
            at = pl.ds(pl.multiple_of((t - self.first[g]) * STRIP, STRIP), STRIP)
            slot = lax.rem(t, 2)
            yield self.in_group(t, g), pltpu.make_async_copy(self.xs[group["x"]].at[:, at], self.xbuf.at[slot], self.x_sem.at[slot])

    def x_start(self, t):
        for cond, copy in self.x_copies(t):
            @pl.when(cond)
            def _(copy=copy):
                copy.start()

    def x_wait(self, t):
        slot = lax.rem(t, 2)
        pltpu.make_async_copy(self.xbuf.at[slot], self.xbuf.at[slot], self.x_sem.at[slot]).wait()

    def y_copy(self, g):
        y = self.groups[g]["y"]
        return pltpu.make_async_copy(self.ys[y], self.ybuf.at[y % 2], self.y_sem.at[y % 2])

    def send(self, u, odd, level):
        slot = lax.rem(u, self.slots)
        return pltpu.make_async_remote_copy(
            self.tiles.at[(slot, *self.pick(odd, level, 1))], self.recvs[level].at[slot],
            self.send_sem.at[level, slot], self.recv_sem.at[level, slot],
            device_id={DP: self.partner(self.order(odd)[level])}, device_id_type=MESH)

    def out_copies(self, u):
        slot = lax.rem(u, 2)
        for g, group in enumerate(self.groups):
            at = pl.ds(pl.multiple_of((u - self.first[g]) * STRIP, STRIP), STRIP)
            out = self.outs[group["out"]]
            if group["turned"]:
                yield self.in_group(u, g), pltpu.make_async_copy(self.stage_turned.at[slot], out.at[:, at], self.out_sem.at[slot])
            else:
                yield self.in_group(u, g), pltpu.make_async_copy(self.stage.at[slot], out.at[at, :], self.out_sem.at[slot])

    def out_wait(self, u):
        for cond, copy in self.out_copies(u):
            @pl.when(cond)
            def _(copy=copy):
                copy.wait()

    def prologue(self):
        self.x_start(jnp.int32(0))
        self.y_copy(0).start()
        for g in range(1, len(self.groups)):
            if self.groups[g]["y"] == 1:
                self.y_copy(g).start()
                break

    def pieces(self, t, place, period, parts=4):
        odd = place % 2
        share = max(self.dp // parts, 1)
        spans = [range(first, first + share) for first in range(0, self.dp, share)]
        return [functools.partial(self.halve, t, place, period)] + [
            functools.partial(self.multiply, t, place, period, span, span[0] == 0, span[-1] == self.dp - 1) for span in spans]

    def halve(self, t, place, period):
        for level in range(self.bits - 1, -1, -1):
            u = t - self.lags[level]
            u_odd = (place - self.lags[level]) % period % 2

            @pl.when(within(u, self.total))
            def _(u=u, u_odd=u_odd, level=level):
                slot = lax.rem(u, self.slots)
                got = self.recvs[level]
                pltpu.make_async_copy(got.at[slot], got.at[slot], self.recv_sem.at[level, slot]).wait()
                keep = (slot, *self.pick(u_odd, level, 0))
                if level < self.bits - 1:
                    left = [range(2) if isinstance(p, slice) else (p,) for p in keep[1:]]
                    for flat, idx in enumerate(itertools.product(*left)):
                        pos = tuple(int(b) for b in format(flat, "b").zfill(self.bits - 1 - level))
                        self.tiles[(slot, *idx)] = self.tiles[(slot, *idx)] + got[(slot, *pos)]
                    self.send(u, u_odd, level + 1).start()
                else:
                    @pl.when(u >= 2)
                    def _():
                        self.out_wait(u - 2)

                    value = self.tiles[keep].astype(jnp.float32) + got[slot].astype(jnp.float32)
                    for g, group in enumerate(self.groups):
                        @pl.when(self.in_group(u, g))
                        def _(group=group):
                            if group["turned"]:
                                self.stage_turned[lax.rem(u, 2)] = value.T
                            else:
                                self.stage[lax.rem(u, 2)] = value
                    for cond, copy in self.out_copies(u):
                        @pl.when(cond)
                        def _(copy=copy):
                            copy.start()

    def ready(self, t, place, period):
        @pl.when(t >= self.slots)
        def _():
            for level in range(self.bits):
                self.send(t - self.slots, (place - self.slots) % period % 2, level).wait_send()

        seen = []
        for g, group in enumerate(self.groups):
            if group["y"] in seen:
                continue
            seen.append(group["y"])

            @pl.when(t == self.first[g])
            def _(g=g, group=group):
                self.y_copy(g).wait()
                if group["y"] == 1:
                    for later in range(len(self.groups)):
                        if self.groups[later]["y"] == 2:
                            self.y_copy(later).start()
                            break

        @pl.when(t + 1 < self.total)
        def _():
            self.x_start(t + 1)

        self.x_wait(t)

    def multiply(self, t, place, period, span, opens, closes):
        @pl.when(within(t, self.total))
        def _():
            if opens:
                self.ready(t, place, period)
            slot = lax.rem(t, self.slots)
            y_slot = jnp.int32(0)
            for g, group in enumerate(self.groups):
                y_slot = jnp.where(t >= self.first[g], group["y"] % 2, y_slot)
            x = self.xbuf[lax.rem(t, 2)]
            for flat in span:
                idx = tuple((flat >> b) & 1 for b in range(self.bits))
                shard = sum((self.bit(b) + idx[b] * (1 - 2 * self.bit(b))) * 2**b for b in range(self.bits))
                at = pl.ds(pl.multiple_of(shard * self.width, self.width), self.width)
                self.tiles[(slot, *idx)] = lax.dot_general(x, self.ybuf[y_slot, :, at], TN, preferred_element_type=jnp.float32).astype(jnp.bfloat16)
            if closes:
                self.send(t, place % 2, 0).start()

    def drain(self, period):
        for u in range(self.total - self.slots, self.total):
            for level in range(self.bits):
                self.send(jnp.int32(u), u % period % 2, level).wait_send()
        for u in range(self.total - 2, self.total):
            self.out_wait(jnp.int32(u))


class LineScatter:
    def __init__(self, n, own, recv, x_own, out_ref, send_sem, recv_sem, store_sem, hop=1):
        self.hop = hop
        self.n, self.own, self.recv, self.x_own, self.out_ref = n, own, recv, x_own, out_ref
        self.send_sem, self.recv_sem, self.store_sem = send_sem, recv_sem, store_sem
        self.k = lax.axis_index(AX)
        self.chunks, _, self.rows, self.cols = own.shape

    def span(self, c):
        return pl.ds(pl.multiple_of(c * self.rows, self.rows), self.rows)

    def copy(self, c, j, right):
        slot = j if right else jnp.where(self.k - 1 == j, self.n, j)
        return pltpu.make_async_remote_copy(
            self.own.at[c, j], self.recv.at[c, slot], self.send_sem.at[c, j], self.recv_sem.at[c, slot],
            device_id={AX: self.k + 1 if right else self.k - 1}, device_id_type=MESH)

    def arrived(self, c, slot):
        got = self.recv.at[c, slot]
        pltpu.make_async_copy(got, got, self.recv_sem.at[c, slot]).wait()

    def store(self, c, j):
        return pltpu.make_async_copy(self.own.at[c, j], self.out_ref.at[self.span(c), :], self.store_sem.at[c])

    def pieces(self, i):
        return [functools.partial(self.pass_on, i, p) for p in range(self.n)] + [functools.partial(self.close, i)]

    def step(self, i):
        for piece in self.pieces(i):
            piece()

    def pass_on(self, i, p):
        n, k = self.n, self.k
        for right in (True, False):
            j = p if right else n - 1 - p
            ahead = (j > k) if right else (j < k)
            behind = (k > 0) if right else (k < n - 1)
            c = i - self.hop * (k if right else n - 1 - k)

            @pl.when(ahead & within(c, self.chunks))
            def _(j=j, right=right, c=c, behind=behind):
                @pl.when(behind)
                def _():
                    self.arrived(c, j)
                    self.own[c, j] = self.own[c, j] + self.recv[c, j]

                self.copy(c, j, right).start()

    def close(self, i):
        n, k = self.n, self.k
        c = i - self.hop * (n - 1)
        for j in range(n):
            @pl.when((k == j) & within(c, self.chunks))
            def _(j=j):
                total = self.x_own[self.span(c), :].astype(jnp.float32) + self.own[c, j].astype(jnp.float32)
                if j > 0:
                    self.arrived(c, j)
                    total = total + self.recv[c, j].astype(jnp.float32)
                if j < n - 1:
                    self.arrived(c, n)
                    total = total + self.recv[c, n].astype(jnp.float32)
                self.own[c, j] = total.astype(self.own.dtype)
                self.store(c, j).start()

    def drain(self):
        def one(c, _):
            for j in range(self.n):
                @pl.when(self.k < j)
                def _(j=j):
                    self.copy(c, j, True).wait_send()

                @pl.when(self.k > j)
                def _(j=j):
                    self.copy(c, j, False).wait_send()

                @pl.when(self.k == j)
                def _(j=j):
                    self.store(c, j).wait()
            return 0

        lax.fori_loop(0, self.chunks, one, 0)


def scatter_scratch(n, chunks, rows, cols):
    low, dma = jnp.bfloat16, pltpu.SemaphoreType.DMA
    return [pltpu.VMEM((chunks, n, rows, cols), low), pltpu.VMEM((chunks, n + 1, rows, cols), low), pltpu.VMEM((chunks * rows, cols), low),
            dma((chunks, n)), dma((chunks, n + 1)), dma((chunks,))]


class Stream:
    def __init__(self, hbm, slots, sem, inward):
        self.hbm, self.slots, self.sem, self.inward = hbm, slots, sem, inward
        self.rows = slots.shape[1]

    def copy(self, p):
        at = self.hbm.at[pl.ds(pl.multiple_of(p * self.rows, self.rows), self.rows), :]
        slot = lax.rem(p, 2)
        pair = (at, self.slots.at[slot]) if self.inward else (self.slots.at[slot], at)
        return pltpu.make_async_copy(*pair, self.sem.at[slot])


class Terms:
    def __init__(self, n, own, sums, w, gains, streams):
        self.n, self.own, self.sums, self.w, self.gains, self.streams = n, own, sums, w, gains, streams
        self.rows, self.cols = streams[0].rows, own.shape[3]
        self.blocks = own.shape[0] * own.shape[2] // self.rows

    def start(self, i):
        for stream in self.streams:
            stream.copy(i).start()

    def pieces(self, i):
        return [functools.partial(self.tile, i, j) for j in range(self.n)]

    def tile(self, i, j):
        @pl.when(i < self.blocks)
        def _():
            if j == 0:
                @pl.when(i + 1 < self.blocks)
                def _():
                    self.start(i + 1)

                for stream in self.streams:
                    stream.copy(i).wait()
            two = lax.rem(i, 2)
            x, stats, gq, gh2 = (stream.slots for stream in self.streams)
            at = slice(j * self.cols, (j + 1) * self.cols)
            mean, inv = stats[two, :, :1], stats[two, :, 1:]
            one = lax.dot_general(gq[two], self.w[at, :], NT, preferred_element_type=jnp.float32)
            other = gh2[two, :, at].astype(jnp.float32)
            normed = (x[two, :, at].astype(jnp.float32) - mean) * inv
            total = (one * self.gains[:1, at] + other * self.gains[1:, at]).astype(self.own.dtype)
            height = self.own.shape[2]
            for b in range(self.rows // height):
                self.own[i * (self.rows // height) + b, j] = total[b * height : (b + 1) * height]
            for row, value in enumerate((one * normed, one, other * normed, other)):
                self.sums[row : row + 1, at] += jnp.sum(value, axis=0, keepdims=True)


class SmallSum:
    def __init__(self, n, bits, partner, out_ref, acc, dp_recv, line_send, line_recv, sems):
        self.n, self.bits, self.partner = n, bits, partner
        self.out_ref, self.acc, self.dp_recv, self.line_send, self.line_recv = out_ref, acc, dp_recv, line_send, line_recv
        self.dp_send_sem, self.dp_recv_sem, self.line_send_sem, self.line_recv_sem, self.own_sem = sems
        self.k, self.me = lax.axis_index(AX), lax.axis_index(DP)

    def last(self):
        return pltpu.make_async_copy(self.dp_recv.at[0, :, pl.ds(0, self.out_ref.shape[1])], self.out_ref, self.own_sem.at[0])

    def swap(self, b):
        return pltpu.make_async_remote_copy(
            self.acc, self.dp_recv.at[b], self.dp_send_sem.at[b], self.dp_recv_sem.at[b], device_id={DP: self.partner(b)}, device_id_type=MESH)

    def onward(self, way):
        return pltpu.make_async_remote_copy(
            self.line_send.at[way], self.line_recv.at[way], self.line_send_sem.at[way], self.line_recv_sem.at[way],
            device_id={AX: self.k + 1 - 2 * way}, device_id_type=MESH)

    def step(self, i):
        n, k = self.n, self.k
        for b in range(self.bits + 1):
            @pl.when(i == b)
            def _(b=b):
                if b > 0:
                    self.swap(b - 1).wait()
                    self.acc[...] = self.acc[...] + self.dp_recv[b - 1]
                if b < self.bits:
                    self.swap(b).start()
        for way in range(2):
            place = k if way == 0 else n - 1 - k

            @pl.when(i == self.bits + 1 + place)
            def _(way=way, place=place):
                self.line_send[way] = self.acc[...]

                @pl.when(place > 0)
                def _():
                    got = self.line_recv.at[way]
                    pltpu.make_async_copy(got, got, self.line_recv_sem.at[way]).wait()
                    self.line_send[way] = self.acc[...] + self.line_recv[way]

                @pl.when(place < n - 1)
                def _():
                    self.onward(way).start()

        @pl.when(i == self.bits + 1 + n)
        def _():
            self.acc[...] = self.line_send[0] + self.line_send[1] - self.acc[...]
            part = self.out_ref.shape[1]
            self.dp_recv[0, :, :part] = self.acc[:, pl.ds(pl.multiple_of(self.me * part, part), part)]
            self.last().start()

    def drain(self):
        @pl.when(self.k < self.n - 1)
        def _():
            self.onward(0).wait_send()

        @pl.when(self.k > 0)
        def _():
            self.onward(1).wait_send()

        self.last().wait()


def sums_kernel(n, dp, chunks, steps, ticks, groups, n_x, n_y, n_out, *refs):
    refs = list(refs)
    take = lambda count: [refs.pop(0) for _ in range(count)]
    x_ref, stats_ref, gh2_ref, gains, w_ref = take(5)
    xs, ys = take(n_x), take(n_y)
    full_ref, sum_ref = take(2)
    outs = take(n_out)
    own, recv, *line_sems = take(8)
    bits = dp.bit_length() - 1
    xbuf, ybuf, tiles = take(3)
    recvs = take(bits)
    rest = take(7)
    small_bufs, small_sems = take(4), take(5)
    k, me = lax.axis_index(AX), lax.axis_index(DP)
    line = LineSum(n, chunks, full_ref, own, recv, *line_sems)
    halving = HalvingSum(dp, groups, xs, ys, outs, xbuf, ybuf, tiles, recvs, *rest)
    small = SmallSum(n, bits, halving.partner, sum_ref, *small_bufs, small_sems)
    w, w_sem = take(2)
    streams = [Stream(ref, *take(2), True) for ref in (x_ref, stats_ref, xs[-1], gh2_ref)]
    terms = Terms(n, own, small_bufs[0], w, gains, streams)
    small_first = chunks

    w_copy = pltpu.make_async_copy(w_ref, w, w_sem.at[0])
    w_copy.start()
    terms.start(jnp.int32(0))
    halving.prologue()
    greet([(k > 0, {AX: k - 1}), (k < n - 1, {AX: k + 1})] + [(me >= 0, {DP: halving.partner(b)}) for b in range(bits)])

    small_bufs[0][...] = jnp.zeros_like(small_bufs[0])
    w_copy.wait()
    for piece in terms.pieces(jnp.int32(0)):
        piece()

    def small_step(c):
        @pl.when(c >= small_first)
        def _():
            small.step(2 * (c - small_first))
            small.step(2 * (c - small_first) + 1)

    def body(i, _):
        lines, strips = [], []
        for e in range(steps):
            c = steps * i + e
            lines += line.pieces(c)
            lines.append(functools.partial(small_step, c))
        for place in range(ticks):
            strips += halving.pieces(ticks * i + place, place, ticks)
        strips = blend(strips, terms.pieces(i + 1))
        for piece in blend(lines, strips):
            piece()
        return 0

    lax.fori_loop(0, max(-(-max(chunks + 2 * (n - 1), small_first + (bits + n + 3) // 2) // steps), -(-(halving.total + halving.lags[-1]) // ticks)), body, 0)
    line.drain()
    halving.drain(ticks)
    small.drain()


def back_sums(tokens, stats, grad_h2, gains, w_qkv, xs, ys, groups, chunks=16, slots=5, steps=2, ticks=3):
    n, dp = lax.axis_size(AX), lax.axis_size(DP)
    bits = dp.bit_length() - 1
    total, width = tokens.shape
    rows, cols = total // chunks, width // n
    w = width // dp
    block = steps * rows
    two = lambda cols, kind=jnp.bfloat16: [pltpu.VMEM((2, block, cols), kind), pltpu.SemaphoreType.DMA((2,))]
    dma = pltpu.SemaphoreType.DMA
    out_shapes = [None] * len(groups)
    for g in groups:
        size = xs[g["x"]].shape[1]
        out_shapes[g["out"]] = jax.ShapeDtypeStruct((w, size) if g["turned"] else (size, w), jnp.float32)
    anywhere = pl.BlockSpec(memory_space=pl.ANY)
    vmem = pltpu.VMEM
    low = jnp.bfloat16
    return pl.pallas_call(
        functools.partial(sums_kernel, n, dp, chunks, steps, ticks, groups, len(xs), len(ys), len(out_shapes)),
        out_shape=[jax.ShapeDtypeStruct(tokens.shape, low), jax.ShapeDtypeStruct((8, w), jnp.float32)] + out_shapes,
        in_specs=[anywhere] * 3 + [pl.BlockSpec(memory_space=vmem)] + [anywhere] * (1 + len(xs) + len(ys)),
        out_specs=[anywhere] * (2 + len(out_shapes)),
        scratch_shapes=[
            vmem((chunks, n, rows, cols), low), vmem((chunks, n + 1, rows, cols), low),
            dma((chunks, n)), dma((chunks, n + 1)), dma((chunks, n)), dma((chunks, n)), dma((chunks, n)), dma((chunks,)),
            vmem((2, total, STRIP), low), vmem((2, total, width), low), vmem((slots, *(2,) * bits, STRIP, w), low),
            *[vmem((slots, *(2,) * (bits - 1 - level), STRIP, w), low) for level in range(bits)],
            vmem((2, STRIP, w), jnp.float32), vmem((2, w, STRIP), jnp.float32),
            dma((2,)), dma((2,)), dma((bits, slots)), dma((bits, slots)), dma((2,)),
            vmem((8, width), jnp.float32), vmem((bits, 8, width), jnp.float32), vmem((2, 8, width), jnp.float32), vmem((2, 8, width), jnp.float32),
            dma((bits,)), dma((bits,)), dma((2,)), dma((2,)), dma((1,)),
            vmem(w_qkv.shape, low), dma((1,)), *two(width), *two(2, jnp.float32), *two(w_qkv.shape[1]), *two(width),
        ],
        compiler_params=pltpu.CompilerParams(collective_id=0, has_side_effects=True, vmem_limit_bytes=62 * 2**20),
        name="back_sums",
    )(tokens, stats, grad_h2, gains, w_qkv, *xs, *ys)


class LineGather:
    def __init__(self, n, chunks, rows, near_left, near_right, up_ref, right_sem, left_sem, recv_sem, hop):
        self.hop = hop
        self.n, self.chunks, self.rows, self.cols = n, chunks, rows, near_left.shape[1]
        self.near, self.up_ref, self.send_sem, self.recv_sem = (near_left, near_right), up_ref, (right_sem, left_sem), recv_sem
        self.k = lax.axis_index(AX)

    def span(self, c):
        return pl.ds(pl.multiple_of(c * self.rows, self.rows), self.rows)

    def block(self, c, j):
        return self.up_ref.at[self.span(c), pl.ds(j * self.cols, self.cols)]

    def copy(self, c, j, right, near):
        src = self.near[0 if right else 1].at[self.span(c), :] if near else self.block(c, j)
        return pltpu.make_async_remote_copy(
            src, self.block(c, j), self.send_sem[0 if right else 1].at[c, j], self.recv_sem.at[c, j],
            device_id={AX: self.k + 1 if right else self.k - 1}, device_id_type=MESH)

    def arrived(self, c, j):
        block = self.block(c, j)
        pltpu.make_async_copy(block, block, self.recv_sem.at[c, j]).wait()

    def pieces(self, i):
        return [functools.partial(self.pass_on, i, p) for p in range(self.n)]

    def pass_on(self, i, p):
        n, k = self.n, self.k
        for right in (True, False):
            j = p if right else n - 1 - p
            dist = (k - j) if right else (j - k)
            onward = (k < n - 1) if right else (k > 0)
            far = i - self.hop * (dist - 1)

            @pl.when((dist == 1) & onward & within(i, self.chunks))
            def _(j=j, right=right):
                self.copy(i, j, right, True).start()

            @pl.when((dist > 1) & within(far, self.chunks))
            def _(j=j, right=right, c=far, onward=onward):
                self.arrived(c, j)

                @pl.when(onward)
                def _():
                    self.copy(c, j, right, False).start()

    def drain(self):
        def one(c, _):
            for j in range(self.n):
                @pl.when((self.k > j) & (self.k < self.n - 1))
                def _(j=j):
                    self.copy(c, j, True, False).wait_send()

                @pl.when((self.k < j) & (self.k > 0))
                def _(j=j):
                    self.copy(c, j, False, False).wait_send()
            return 0

        lax.fori_loop(0, self.chunks, one, 0)


def gelu_and_slope(x):
    share = 0.5 * (1.0 + lax.erf(x * (0.5**0.5)))
    return x * share, share + x * (jnp.exp(-0.5 * x * x) * (2.0 * jnp.pi) ** -0.5)


def feed_kernel(
    n, chunks, tile, hop,
    h2_ref, att_ref, fc1_ref, fc2_ref, dense_ref, up_own_ref, left_ref, right_ref, x_ref,
    up_ref, hidden_ref, grad_pre_ref, grad_h2_ref, grad_att_ref, out_ref,
    own, recv, x_own, rs_send, rs_recv, out_sem, fc1, fc2, dense, h2_buf, att_buf, up_buf, hid_buf, gp_buf, gh_buf, ga_buf, slope,
    first_sem, weight_sem, near_sem, h2_sem, att_sem, up_sem, hid_sem, gp_sem, gh_sem, ga_sem, *line_sems,
):
    k = lax.axis_index(AX)
    low = jnp.bfloat16
    rows = h2_buf.shape[1]
    blocks = h2_ref.shape[0] // rows
    per_block = rows // own.shape[2]
    lag = -(-(2 + hop * (n - 2)) // 2)
    cols = own.shape[3]
    rate = 3

    gather = LineGather(n, chunks, own.shape[2], left_ref, right_ref, up_ref, *line_sems, hop)
    scatter = LineScatter(n, own, recv, x_own, out_ref, rs_send, rs_recv, out_sem, hop)

    def gather_step(i):
        for piece in gather.pieces(i):
            piece()

    h2_in, att_in = Stream(h2_ref, h2_buf, h2_sem, True), Stream(att_ref, att_buf, att_sem, True)
    hid_out, gp_out = Stream(hidden_ref, hid_buf, hid_sem, False), Stream(grad_pre_ref, gp_buf, gp_sem, False)
    gh_out, ga_out = Stream(grad_h2_ref, gh_buf, gh_sem, False), Stream(grad_att_ref, ga_buf, ga_sem, False)

    h2_in.copy(jnp.int32(0)).start()
    att_in.copy(jnp.int32(0)).start()
    strips = [pl.ds(t, tile) for t in range(0, fc1.shape[1], tile)]
    first = [pltpu.make_async_copy(fc1_ref.at[:, at], fc1.at[:, at], first_sem.at[w]) for w, at in enumerate(strips)]
    weights = first + [pltpu.make_async_copy(a, b, weight_sem.at[w]) for w, (a, b) in enumerate(((dense_ref, dense), (fc2_ref, fc2), (x_ref.at[:, pl.ds(pl.multiple_of(k * own.shape[3], own.shape[3]), own.shape[3])], x_own)))]
    for copy in weights:
        copy.start()

    def up_pieces(q):
        at, two = pl.ds(pl.multiple_of(q * rows, rows), rows), lax.rem(q, 2)
        for j in range(n):
            span = pl.ds(j * cols, cols)
            dst = up_buf.at[two, :, span]
            for cond, src in ((k == j, up_own_ref), (k - 1 == j, left_ref), (k + 1 == j, right_ref)):
                yield cond, True, pltpu.make_async_copy(src.at[at, :], dst, up_sem.at[two, j]), pltpu.make_async_copy(dst, up_ref.at[at, span], near_sem.at[two, j])
            far = (k - j > 1) | (j - k > 1)
            yield far, False, pltpu.make_async_copy(up_ref.at[at, span], dst, up_sem.at[two, j]), None

    def up_start(q):
        for cond, _, load, _ in up_pieces(q):
            @pl.when(cond)
            def _(load=load):
                load.start()

    def up_wait(q):
        for cond, near, load, put in up_pieces(q):
            @pl.when(cond)
            def _(near=near, load=load, put=put):
                load.wait()
                if near:
                    put.start()

    def up_put_wait(q):
        for cond, near, _, put in up_pieces(q):
            if near:
                @pl.when(cond)
                def _(put=put):
                    put.wait()

    greet([(k > 0, {AX: k - 1}), (k < n - 1, {AX: k + 1})])

    def forward(p):
        @pl.when(p + 1 < blocks)
        def _():
            h2_in.copy(p + 1).start()
            att_in.copy(p + 1).start()

        @pl.when(p >= 2)
        def _():
            hid_out.copy(p - 2).wait()

        h2_in.copy(p).wait()
        att_in.copy(p).wait()
        two = lax.rem(p, 2)
        keep = lax.rem(p, lag + 1)
        h2 = h2_buf[two]
        for t in range(0, fc1.shape[1], tile):
            @pl.when(p == 0)
            def _(t=t):
                first[t // tile].wait()

            hid, bend = gelu_and_slope(jnp.dot(h2, fc1[:, t : t + tile], preferred_element_type=jnp.float32))
            hid_buf[two, :, t : t + tile] = hid.astype(low)
            slope[keep, :, t : t + tile] = bend.astype(low)
        hid_out.copy(p).start()

        @pl.when(p == 0)
        def _():
            for copy in weights[len(first):]:
                copy.wait()

        att, hid = att_buf[two], hid_buf[two]
        for j in range(n):
            part = jnp.dot(hid, fc2[:, j * cols : (j + 1) * cols], preferred_element_type=jnp.float32)
            part = (part + jnp.dot(att, dense[:, j * cols : (j + 1) * cols], preferred_element_type=jnp.float32)).astype(low)
            for b in range(per_block):
                own[per_block * p + b, j] = part[b * own.shape[2] : (b + 1) * own.shape[2]]

    def backward(q):
        @pl.when(q >= 2)
        def _():
            for stream in (gp_out, gh_out, ga_out):
                stream.copy(q - 2).wait()

        up_wait(q)
        two = lax.rem(q, 2)
        keep = lax.rem(q, lag + 1)
        up = up_buf[two]
        ga_buf[two] = lax.dot_general(up, dense[...], NT, preferred_element_type=jnp.float32).astype(low)
        ga_out.copy(q).start()
        for t in range(0, fc2.shape[0], tile):
            grad = lax.dot_general(up, fc2[t : t + tile, :], NT, preferred_element_type=jnp.float32)
            gp_buf[two, :, t : t + tile] = (grad * slope[keep, :, t : t + tile].astype(jnp.float32)).astype(low)
        gp_out.copy(q).start()
        grad_pre = gp_buf[two]
        for t in range(0, fc1.shape[0], tile):
            gh_buf[two, :, t : t + tile] = lax.dot_general(grad_pre, fc1[t : t + tile, :], NT, preferred_element_type=jnp.float32).astype(low)
        gh_out.copy(q).start()

    def body(p, _):
        @pl.when(p < blocks)
        def _():
            forward(p)

        gather_step(per_block * p)
        scatter.step(lax.div(rate * p, 2))

        @pl.when(within(p - lag, blocks))
        def _():
            backward(p - lag)

        for b in range(1, per_block):
            gather_step(per_block * p + b)

        @pl.when(lax.div(rate * (p + 1), 2) - lax.div(rate * p, 2) > 1)
        def _():
            scatter.step(lax.div(rate * p, 2) + 1)

        @pl.when(within(p + 1 - lag, blocks))
        def _():
            @pl.when(p + 1 - lag >= 2)
            def _():
                up_put_wait(p - 1 - lag)

            up_start(p + 1 - lag)

        return 0

    lax.fori_loop(0, max(blocks + lag, -(-(chunks + hop * (n - 2)) // per_block), -(-2 * (scatter.chunks + hop * (n - 1)) // rate)), body, 0)
    for last in range(max(blocks - 2, 0), blocks):
        for stream in (hid_out, gp_out, gh_out, ga_out):
            stream.copy(jnp.int32(last)).wait()
        up_put_wait(jnp.int32(last))
    gather.drain()
    scatter.drain()


def feed_forward(h2, attended, fc1, fc2, dense, upstream, left, right, tokens, rows=256, chunks=16, tile=512, hop=2):
    n = lax.axis_size(AX)
    total, width = h2.shape
    hidden, heads_width, cols = fc1.shape[1], attended.shape[1], width // n
    low, dma, vmem = jnp.bfloat16, pltpu.SemaphoreType.DMA, pltpu.VMEM
    piece = total // chunks
    lag = -(-(2 + hop * (n - 2)) // 2)
    tile = min(tile, hidden)
    anywhere = pl.BlockSpec(memory_space=pl.ANY)
    shape = lambda cols: jax.ShapeDtypeStruct((total, cols), low)
    two = lambda cols: vmem((2, rows, cols), low)
    return pl.pallas_call(
        functools.partial(feed_kernel, n, chunks, tile, hop),
        out_shape=[shape(width), shape(hidden), shape(hidden), shape(width), shape(heads_width), shape(cols)],
        in_specs=[anywhere] * 9,
        out_specs=[anywhere] * 6,
        scratch_shapes=[
            *scatter_scratch(n, chunks, piece, cols),
            vmem(fc1.shape, low), vmem(fc2.shape, low), vmem(dense.shape, low),
            two(width), two(heads_width), two(width), two(hidden), two(hidden), two(width), two(heads_width), vmem((lag + 1, rows, hidden), low),
            dma((hidden // tile,)), dma((3,)), dma((2, n)), dma((2,)), dma((2,)), dma((2, n)), dma((2,)), dma((2,)), dma((2,)), dma((2,)),
            dma((chunks, n)), dma((chunks, n)), dma((chunks, n)),
        ],
        compiler_params=pltpu.CompilerParams(collective_id=1, has_side_effects=True, vmem_limit_bytes=VMEM_CAP),
        name="feed_forward",
    )(h2, attended, fc1, fc2, dense, upstream, left, right, tokens)


def attend_back_kernel(block, n, heads, qkv_ref, g_ref, o_ref, dcol_ref, drow_ref, lse_ref, rot_ref, out_ref, dk, dv):
    i = pl.program_id(1)
    scale = HEAD_DIM ** (-0.5)
    part = lambda h, c: slice((3 * h + c) * HEAD_DIM, (3 * h + c + 1) * HEAD_DIM)
    cols = lambda h: slice(h * HEAD_DIM, (h + 1) * HEAD_DIM)

    @pl.when(i == 0)
    def _():
        dk[...] = jnp.zeros_like(dk)
        dv[...] = jnp.zeros_like(dv)

    here = pl.ds(pl.multiple_of(i * block, block), block)
    docs_q = drow_ref[...]
    ones = jnp.ones((8, HEAD_DIM), jnp.float32)
    queries = [qkv_ref[here, part(h, 0)] * jnp.bfloat16(scale) for h in range(heads)]
    grads = [g_ref[:, cols(h)] for h in range(heads)]
    deltas = [
        lax.dot_general(ones, grads[h].astype(jnp.float32) * o_ref[:, cols(h)].astype(jnp.float32), NT,
                        precision=lax.Precision.HIGHEST, preferred_element_type=jnp.float32)[:1]
        for h in range(heads)
    ]
    later = lax.broadcasted_iota(jnp.int32, (block, block), 1) >= lax.broadcasted_iota(jnp.int32, (block, block), 0)

    def body(j, carry, corner=False):
        rows = pl.ds(pl.multiple_of(j * block, block), block)
        allowed = docs_q == dcol_ref[rows, :]
        if corner:
            allowed = allowed & later
        new = []
        for h in range(heads):
            q, g = queries[h], grads[h]
            k = qkv_ref[rows, part(h, 1)]
            s = lax.dot_general(k, q, NT, preferred_element_type=jnp.float32)
            p = jnp.exp(jnp.where(allowed, s - lse_ref[h], -1e30))
            dp = lax.dot_general(qkv_ref[rows, part(h, 2)], g, NT, preferred_element_type=jnp.float32)
            ds = (p * (dp - deltas[h])).astype(jnp.bfloat16)
            dv[rows, cols(h)] += jnp.dot(p.astype(jnp.bfloat16), g, preferred_element_type=jnp.float32)
            dk[rows, cols(h)] += jnp.dot(ds, q, preferred_element_type=jnp.float32)
            new.append(carry[h] + lax.dot_general(ds, k, TN, preferred_element_type=jnp.float32))
        return tuple(new)

    dq = body(i, lax.fori_loop(0, i, body, (jnp.zeros((block, HEAD_DIM), jnp.float32),) * heads), True)

    def put(rows, first, val):
        rot = rot_tiles(rot_ref[:, rows])
        out_ref[rows, first : first + LANES] = rotate_back_tile(val[:, :LANES], *rot).astype(jnp.bfloat16)
        out_ref[rows, first + LANES : first + HEAD_DIM] = val[:, LANES:].astype(jnp.bfloat16)

    for h in range(heads):
        put(here, 3 * h * HEAD_DIM, dq[h] * scale)

    @pl.when(i == n - 1)
    def _():
        for h in range(heads):
            for b in range(n):
                rows = slice(b * block, (b + 1) * block)
                put(rows, (3 * h + 1) * HEAD_DIM, dk[rows, cols(h)])
                out_ref[rows, part(h, 2)] = dv[rows, cols(h)].astype(jnp.bfloat16)


def attend_back(qkv, grad_att, attended, docs, lse, rot, block=512):
    total, cols = qkv.shape
    heads = cols // (3 * HEAD_DIM)
    seqs = total // SEQ_LEN
    n = SEQ_LEN // block
    whole = pl.BlockSpec((SEQ_LEN, cols), lambda s, i: (s, 0))
    mine = pl.BlockSpec((block, heads * HEAD_DIM), lambda s, i: (s * n + i, 0))
    table = pl.BlockSpec((ROT_DIM, SEQ_LEN), lambda s, i: (0, s))
    return pl.pallas_call(
        functools.partial(attend_back_kernel, block, n, heads),
        grid=(seqs, n),
        in_specs=[
            whole, mine, mine,
            pl.BlockSpec((SEQ_LEN, 1), lambda s, i: (s, 0)),
            pl.BlockSpec((1, block), lambda s, i: (0, s * n + i)),
            pl.BlockSpec((heads, 1, block), lambda s, i: (0, 0, s * n + i)),
            table,
        ],
        out_specs=whole,
        out_shape=jax.ShapeDtypeStruct((total, cols), jnp.bfloat16),
        scratch_shapes=[pltpu.VMEM((SEQ_LEN, heads * HEAD_DIM), jnp.float32)] * 2,
        compiler_params=pltpu.CompilerParams(vmem_limit_bytes=VMEM_CAP),
        cost_estimate=pl.CostEstimate(flops=5 * total * SEQ_LEN * heads * HEAD_DIM, bytes_accessed=8 * total * cols, transcendentals=total * SEQ_LEN),
        name="attend_back",
    )(qkv, grad_att, attended, docs[:, None], docs[None, :], lse, rot)


def on_device(tokens, segments, positions, ln1_gain, ln1_bias, ln2_gain, ln2_bias, qkv_weight, dense_weight, fc1_weight, fc2_weight, upstream):
    n = lax.axis_size(AX)
    left = lax.ppermute(upstream, AX, [(i, i + 1) for i in range(n - 1)])
    right = lax.ppermute(upstream, AX, [(i + 1, i) for i in range(n - 1)])
    rot = rot_tables(positions)
    h_one, h_two, qkv, stats = project(tokens, ln1_gain, ln1_bias, ln2_gain, ln2_bias, rot, qkv_weight)
    attended, lse = attend(qkv, segments, 1024)
    up, hidden, grad_pre, grad_h_two, grad_att, output = feed_forward(
        h_two, attended, fc1_weight, fc2_weight, dense_weight, upstream, left, right, tokens)
    grad_qkv = attend_back(qkv, grad_att, attended, segments, lse, rot)
    groups = [
        dict(x=0, y=0, count=grad_pre.shape[1] // STRIP, turned=True, out=2),
        dict(x=1, y=1, count=hidden.shape[1] // STRIP, turned=False, out=3),
        dict(x=2, y=1, count=attended.shape[1] // STRIP, turned=False, out=1),
        dict(x=3, y=2, count=grad_qkv.shape[1] // STRIP, turned=True, out=0),
    ]
    s, norm_grads, qkv_grad, dense_grad, fc1_grad, fc2_grad = back_sums(
        tokens, stats, grad_h_two, jnp.stack([ln1_gain, ln2_gain]), qkv_weight, [grad_pre, hidden, attended, grad_qkv], [h_two, up, h_one], groups)
    input_grad = finish(tokens, stats, s, up)
    return (
        output, input_grad, qkv_grad, dense_grad, fc1_grad, fc2_grad,
        norm_grads[0], norm_grads[1], norm_grads[2], norm_grads[3],
    )


def solution(mesh):
    in_specs = (
        P("dp", None),
        P("dp"),
        P("dp"),
        P(),
        P(),
        P(),
        P(),
        P(None, "tensor"),
        P("tensor", None),
        P(None, "tensor"),
        P("tensor", None),
        P("dp", "tensor"),
    )
    out_specs = (
        P("dp", "tensor"),
        P("dp", None),
        P("dp", "tensor"),
        P("tensor", "dp"),
        P("dp", "tensor"),
        P("tensor", "dp"),
        P("dp"),
        P("dp"),
        P("dp"),
        P("dp"),
    )
    return jax.shard_map(
        on_device, mesh=mesh, in_specs=in_specs, out_specs=out_specs, check_vma=False
    )
```
